32 devices in a mesh: wide: 8 (over y, x, core), narrow: 4 (over z).
Axes of the slice: x: 2, y: 2, z: 4, core: 2. Of those that a mesh axis runs over, the one named last changes fastest.
Arguments:
- node_feats: bfloat16 [8192, 1024], P('wide'), may hold values from -6 to 6
- neigh_weight: bfloat16 [1024, 1024], P(None, 'narrow'), may hold values from -0.1875 to 0.1875
- neigh_bias: bfloat16 [1024], P('narrow'), may hold values from -3 to 3
- combine_weight: bfloat16 [2048, 1024], P(None, 'narrow')
- combine_bias: bfloat16 [1024], P('narrow'), may hold values from -3 to 3
- cotangent: bfloat16 [8192, 1024], P('wide', 'narrow'), may hold values from -6 to 6
- neighbour_slot: int32 [8192, 50], P('wide'), may hold values from 0 to 3071, as said below
- neighbour_mask: int32 [8192, 50], P('wide'), may hold values from 0 to 1, as said below
- visit_count: int32 [8192, 50], P('wide'), may hold values from 1 to 128, as said below
- send_rows: int32 [64, 256], P('wide'), may hold values from 0 to 1023, as said below
Outputs:
- embedding: bfloat16 [8192, 1024], P('wide', 'narrow')
- grad_features: float32 [8192, 1024], P('wide', 'narrow')
- grad_neigh_weight: float32 [1024, 1024], P(None, 'narrow')
- grad_neigh_bias: float32 [1024], P('narrow')
- grad_combine_weight: float32 [2048, 1024], P(None, 'narrow')
- grad_combine_bias: float32 [1024], P('narrow')
The draws below stay inside these ranges and needn't reach their ends.
Inputs may be any that keep to these rules, and one draw needn't show every extreme that they name: `neighbour_slot`: an entry below 1024 is a row of the node's own device; an entry e of 1024 or more names slot (e - 1024) % 256 of the rows that owner (e - 1024) // 256 sends, never the node's own device. `neighbour_mask`: each row holds 5 to 50 ones followed by zeros. `visit_count`: powers of two. `send_rows`: row o * (devices along wide) + r lists, by index among owner o's 1024 nodes, the rows that requester r receives from o; the 256 entries of a row are distinct.
All inputs are finite; a program needn't handle non-finite values.
Results may differ from the reference program's by a relative error of at most 0.0095.
Values may be sent and summed in bfloat16 or wider, within the bound.
A program may use at most 128 MiB of HBM per device.

```python
import jax
import jax.numpy as jnp
from jax import lax

D = 1024
K = 50
MIN_NBR = 5
NODE_DEV = 1024
CAP = 256
NODES = 8192


def draw_combine_weight(key, part):
    base = jnp.clip(jax.random.normal(key, (2 * D, D), jnp.float32), -6.0, 6.0)
    row_pos = jnp.arange(2 * D, dtype=jnp.int32)
    row_scale = jnp.where(row_pos < D, 0.7, 2.0).astype(jnp.float32) / jnp.sqrt(jnp.float32(D))
    frac = jnp.arange(D, dtype=jnp.float32) / jnp.float32(max(D - 1, 1))
    col_scale = jnp.power(10.0, frac)
    return (base * row_scale[:, None] * col_scale[None, :]).astype(jnp.bfloat16)


def draw_neighbour_slot(key, part):
    owners = NODES // NODE_DEV
    keys = jax.random.split(key, 4)
    own_index = (jnp.arange(NODES, dtype=jnp.int32) // NODE_DEV)[:, None]
    local_pick = jax.random.randint(keys[0], (NODES, K), 0, NODE_DEV, dtype=jnp.int32)
    offset = jax.random.randint(keys[1], (NODES, K), 1, owners, dtype=jnp.int32)
    owner_index = (own_index + offset) % owners
    slot_column = jax.random.randint(keys[2], (NODES, K), 0, CAP, dtype=jnp.int32)
    remote_pick = NODE_DEV + owner_index * CAP + slot_column
    chooser = jax.random.randint(keys[3], (NODES, K), 0, 2, dtype=jnp.int32)
    return jnp.where(chooser == 1, remote_pick, local_pick).astype(jnp.int32)


def draw_neighbour_mask(key, part):
    present = jax.random.randint(key, (NODES, 1), MIN_NBR, K + 1, dtype=jnp.int32)
    positions = jnp.arange(K, dtype=jnp.int32)[None, :]
    return (positions < present).astype(jnp.int32)


def draw_visit_count(key, part):
    powers = jax.random.randint(key, (NODES, K), 0, 8, dtype=jnp.int32)
    return jnp.left_shift(jnp.ones_like(powers), powers).astype(jnp.int32)


def draw_send_rows(key, part):
    owners = NODES // NODE_DEV
    keys = jax.random.split(key, owners * owners)

    def one_list(single_key):
        return jax.random.permutation(single_key, NODE_DEV)[:CAP].astype(jnp.int32)
    return jax.vmap(one_list)(keys).astype(jnp.int32)


def block_levels(stream_key, extent, pieces, low, high):
    def one(dim, parts):
        draws = jax.random.uniform(jax.random.fold_in(jax.random.fold_in(stream_key, 6), dim), (parts,), jnp.float32, low / len(pieces), high / len(pieces))
        return jnp.repeat(jnp.exp(draws), extent[dim] // parts).reshape((-1,) + (1,) * (len(extent) - dim - 1))

    gain = one(*pieces[0])
    for cut in pieces[1:]:
        gain = gain * one(*cut)
    return gain


def scatter_about(rng, shape, deviation, limit, cuts=(), kind=jnp.bfloat16):
    drawn = jax.random.normal(rng, shape, jnp.float32) * deviation
    if len(cuts) > 0:
        drawn = block_levels(rng, shape, cuts, -0.22, 0.18) * drawn
    return jnp.clip(drawn, min=-limit, max=limit).astype(kind)


def setup_inputs(seed: int = 0) -> dict:
    arg_keys = jax.random.split(jax.random.key(seed), 11)
    return {
        "node_feats": scatter_about(arg_keys[0], (NODES, D), 1.0, 6.0, ((0, 8),)),
        "neigh_weight": scatter_about(arg_keys[1], (D, D), D ** -0.5, 0.1875, ((1, 4),)),
        "neigh_bias": scatter_about(arg_keys[2], (D,), 0.5, 3.0, ((0, 4),)),
        "combine_weight": draw_combine_weight(jax.random.fold_in(arg_keys[10], 71), 0),
        "combine_bias": scatter_about(arg_keys[4], (D,), 0.5, 3.0, ((0, 4),)),
        "cotangent": scatter_about(arg_keys[5], (NODES, D), 1.0, 6.0, ((0, 8), (1, 4))),
        "neighbour_slot": draw_neighbour_slot(jax.random.fold_in(arg_keys[10], 71), 0),
        "neighbour_mask": draw_neighbour_mask(jax.random.fold_in(arg_keys[10], 71), 0),
        "visit_count": draw_visit_count(jax.random.fold_in(arg_keys[10], 71), 0),
        "send_rows": draw_send_rows(jax.random.fold_in(arg_keys[10], 71), 0),
    }


EPSILON = 1e-06

@jax.custom_vjp
def low(v):
    return lax.optimization_barrier(v.astype(jnp.bfloat16)).astype(jnp.float32)

@jax.custom_vjp
def low_back(v):
    return v

def low_keep(v):
    return (low(v), None)

def low_pass(kept, grad):
    return (grad,)

def back_keep(v):
    return (v, None)

def back_low(kept, grad):
    return (low(grad),)
low.defvjp(low_keep, low_pass)
low_back.defvjp(back_keep, back_low)

def neighbour_ids(neighbour_slot, send_rows):
    owners = NODES // NODE_DEV
    capacity = send_rows.shape[1]
    own_index = (jnp.arange(NODES, dtype=jnp.int32) // NODE_DEV)[:, None]
    is_local = neighbour_slot < NODE_DEV
    remote_slot = jnp.where(is_local, 0, neighbour_slot - NODE_DEV).astype(jnp.int32)
    owner_index = (remote_slot // capacity).astype(jnp.int32)
    slot_column = (remote_slot % capacity).astype(jnp.int32)
    remote_row = send_rows[owner_index * owners + own_index, slot_column]
    local_id = own_index * NODE_DEV + neighbour_slot
    remote_id = owner_index * NODE_DEV + remote_row
    return jnp.where(is_local, local_id, remote_id).astype(jnp.int32)

def reference(node_feats, neigh_weight, neigh_bias, combine_weight, combine_bias, cotangent, neighbour_slot, neighbour_mask, visit_count, send_rows):
    global_ids = neighbour_ids(neighbour_slot, send_rows)
    masked = (visit_count * neighbour_mask).astype(jnp.float32)
    importance = masked / lax.optimization_barrier(jnp.sum(masked, axis=1, keepdims=True))
    half_rows = NODE_DEV // 2
    num_blocks = NODES // half_rows
    id_blocks = global_ids.reshape(num_blocks, half_rows, K)
    weight_blocks = importance.reshape(num_blocks, half_rows, K)
    highest = lax.Precision.HIGHEST

    def forward(features, neigh_w, neigh_b, combine_w, combine_b):
        hidden = jnp.dot(features, neigh_w, precision=highest, preferred_element_type=jnp.float32) + neigh_b
        message = low_back(jax.nn.relu(hidden))

        def pool_block(inputs):
            block_ids, block_weights = inputs
            return lax.optimization_barrier(jnp.sum(block_weights[:, :, None] * message[block_ids], axis=1))
        pooled = lax.map(jax.checkpoint(pool_block), (id_blocks, weight_blocks)).reshape(NODES, -1)
        pooled = low_back(pooled)
        joined = jnp.concatenate([features, pooled], axis=1)
        pre_act = jnp.dot(joined, combine_w, precision=highest, preferred_element_type=jnp.float32) + combine_b
        pre_act = low_back(pre_act)
        activated = jax.nn.relu(pre_act)
        inv_norm = lax.rsqrt(lax.optimization_barrier(jnp.mean(activated * activated, axis=1, keepdims=True)) + EPSILON)
        return activated * inv_norm
    embedding, pullback = jax.vjp(forward, node_feats.astype(jnp.float32), neigh_weight.astype(jnp.float32), neigh_bias.astype(jnp.float32), combine_weight.astype(jnp.float32), combine_bias.astype(jnp.float32))
    grad_features, grad_neigh, grad_nbias, grad_combine, grad_cbias = pullback(cotangent.astype(jnp.float32))
    return (embedding.astype(jnp.bfloat16), grad_features, grad_neigh, grad_nbias, grad_combine, grad_cbias)
```

```python
import jax
import jax.numpy as jnp
from jax import lax
from jax.sharding import PartitionSpec as P

EPSILON = 1e-06
F32 = jnp.float32
BF16 = jnp.bfloat16


def mm(left, right, dims=((1,), (0,))):
    return lax.dot_general(left, right, (dims, ((), ())), preferred_element_type=F32)


def split(value):
    high = lax.reduce_precision(value, 8, 7)
    return high.astype(BF16), (value - high).astype(BF16)


def mm2(left, right):
    high, low = split(right)
    return mm(left, high) + mm(left, low)


def counts_matrix(slots, weights, table_rows):
    positions = jnp.arange(table_rows, dtype=jnp.int32)
    hits = slots[:, :, None] == positions[None, None, :]
    return jnp.sum(jnp.where(hits, weights[:, :, None], 0.0), axis=1)


def shards(
    node_feats,
    neigh_weight,
    neigh_bias,
    combine_weight,
    combine_bias,
    cotangent,
    neighbour_slot,
    neighbour_mask,
    visit_count,
    send_rows,
):
    width = node_feats.shape[1]
    local_rows = node_feats.shape[0]
    owners = lax.axis_size("wide")
    capacity = send_rows.shape[1]
    masked = (visit_count * neighbour_mask).astype(F32)
    inv_sum = 1.0 / jnp.sum(masked, axis=1, keepdims=True)
    counts = counts_matrix(neighbour_slot, masked, local_rows + owners * capacity)
    counts_hi, counts_lo = split(counts)
    selector = (
        send_rows.reshape(-1)[:, None] == jnp.arange(local_rows, dtype=jnp.int32)[None, :]
    ).astype(BF16)
    neigh_full = lax.all_gather(neigh_weight, "narrow", axis=1, tiled=True)
    bias_full = lax.all_gather(neigh_bias, "narrow", axis=0, tiled=True)
    hidden = mm(node_feats, neigh_full) + bias_full.astype(F32)
    message = jnp.maximum(hidden, 0.0)
    msg_hi, msg_lo = split(message)
    self_rows = combine_weight[:width]
    pool_weight = combine_weight[width:]
    z = mm(msg_hi, pool_weight) + mm(msg_lo, pool_weight)
    outgoing = mm2(selector, z).reshape(owners, capacity, -1)
    incoming = lax.all_to_all(outgoing, "wide", split_axis=0, concat_axis=0, tiled=True)
    table = jnp.concatenate([z, incoming.reshape(owners * capacity, -1)], axis=0)
    t_hi, t_lo = split(table)
    pool = mm(counts_hi, t_hi) + mm(counts_hi, t_lo) + mm(counts_lo, t_hi)
    pre_act = mm(node_feats, self_rows) + pool * inv_sum + combine_bias.astype(F32)
    activated = jnp.maximum(pre_act, 0.0)
    upstream = cotangent.astype(F32)
    squares = lax.psum(jnp.sum(activated * activated, axis=1), "narrow")
    inner_dot = lax.psum(jnp.sum(activated * upstream, axis=1), "narrow")
    inv_norm = lax.rsqrt(squares / width + EPSILON)
    embedding = (activated * inv_norm[:, None]).astype(BF16)
    cubed = inv_norm * inv_norm * inv_norm
    grad_act = upstream * inv_norm[:, None] - activated * (inner_dot * cubed / width)[:, None]
    grad_pre = jnp.where(pre_act > 0, grad_act, 0.0)
    scaled = (grad_pre * inv_sum).astype(BF16)
    grad_pre = grad_pre.astype(BF16)
    grad_cbias = jnp.sum(grad_pre.astype(F32), axis=0)
    grad_table = mm(counts_hi, scaled, ((0,), (0,)))
    returned = lax.all_to_all(
        grad_table[local_rows:].astype(BF16).reshape(owners, capacity, -1),
        "wide",
        split_axis=0,
        concat_axis=0,
        tiled=True,
    )
    y = (
        grad_table[:local_rows]
        + mm(selector, returned.reshape(owners * capacity, -1), ((0,), (0,)))
    ).astype(BF16)
    grad_combine = jnp.concatenate(
        [mm(node_feats, grad_pre, ((0,), (0,))), mm(msg_hi, y, ((0,), (0,)))], axis=0
    )
    to_rows = lambda v: lax.all_to_all(v, "narrow", split_axis=0, concat_axis=1, tiled=True)
    to_cols = lambda v: lax.all_to_all(v, "narrow", split_axis=1, concat_axis=0, tiled=True)
    combine_full = lax.all_gather(combine_weight, "narrow", axis=1, tiled=True)
    grad_pre_rows = to_rows(grad_pre)
    y_rows = to_rows(y)
    rows = local_rows // lax.axis_size("narrow")
    hidden_rows = lax.dynamic_slice_in_dim(hidden, lax.axis_index("narrow") * rows, rows, 0)
    grad_message = mm(y_rows, combine_full[width:], ((1,), (1,)))
    grad_hidden_rows = jnp.where(hidden_rows > 0, grad_message, 0.0).astype(BF16)
    grad_hidden = to_cols(grad_hidden_rows)
    grad_features_rows = mm(grad_pre_rows, combine_full[:width], ((1,), (1,))) + mm(
        grad_hidden_rows, neigh_full, ((1,), (1,))
    )
    grad_features = to_cols(grad_features_rows.astype(BF16)).astype(F32)
    grad_neigh = mm(node_feats, grad_hidden, ((0,), (0,)))
    grad_nbias = jnp.sum(grad_hidden.astype(F32), axis=0)
    grad_neigh, grad_nbias, grad_combine, grad_cbias = lax.psum(
        (grad_neigh, grad_nbias, grad_combine, grad_cbias), "wide"
    )
    return (embedding, grad_features, grad_neigh, grad_nbias, grad_combine, grad_cbias)


def solution(mesh):
    placed = (
        P("wide", None),
        P(None, "narrow"),
        P("narrow"),
        P(None, "narrow"),
        P("narrow"),
        P("wide", "narrow"),
        P("wide", None),
        P("wide", None),
        P("wide", None),
        P("wide", None),
    )
    return jax.shard_map(
        shards,
        mesh=mesh,
        in_specs=placed,
        out_specs=(
            P("wide", "narrow"),
            P("wide", "narrow"),
            P(None, "narrow"),
            P("narrow"),
            P(None, "narrow"),
            P("narrow"),
        ),
        check_vma=False,
    )
```

```python
import functools

import jax
import jax.numpy as jnp
from jax import lax
from jax.experimental import pallas as pl
from jax.experimental.pallas import tpu as pltpu
from jax.sharding import PartitionSpec as P

EPSILON = 1e-06
F32 = jnp.float32
BF16 = jnp.bfloat16
I32 = jnp.int32
MESH = pl.DeviceIdType.MESH


def mm(left, right):
    return jnp.dot(left, right, preferred_element_type=F32)


def mm_nt(left, right):
    return lax.dot_general(left, right, (((1,), (1,)), ((), ())), preferred_element_type=F32)


def at(index, size):
    return pl.ds(pl.multiple_of(index * size, size), size)


class Sizes:
    def __init__(self, feats, neigh, send, slot, wide, narrow):
        self.rows, self.width = feats.shape
        self.cols = neigh.shape[1]
        self.cap = send.shape[1]
        self.slots = slot.shape[1]
        self.wide, self.narrow = wide, narrow
        self.chunk = min(256, self.rows)
        self.part = self.rows // narrow
        self.local = self.rows // self.cap
        self.blocks = self.local + wide
        self.red_rows = max(16, self.cols // wide)
        self.red_down = self.cols // self.red_rows
        self.red_across = wide // self.red_down
        self.red_lanes = self.width // self.red_across


NAMES_IN = ["feats_in", "nw_in", "nb_in", "comb_in", "cb_in", "cot_in", "slot_in", "mask_in", "visit_in", "send_in"]
NAMES_OUT = ["emb_out", "gf_out", "gn_out", "gc_out", "gnb_out", "gcb_out"]


def scratch(z):
    R, D, C, W, N, U, CAP = z.rows, z.width, z.cols, z.wide, z.narrow, z.part, z.cap
    v = lambda *shape: pltpu.VMEM(shape[:-1], shape[-1])
    bufs = dict(
        feats=v(R, D, BF16),
        nwfull=v(N, D, C, BF16),
        nbfull=v(N, 8, C, F32),
        wfull=v(N, 2 * D, C, BF16),
        cb=v(8, C, F32),
        cot=v(R, C, BF16),
        slot=v(R, z.slots, I32),
        mask=v(R, z.slots, I32),
        visit=v(R, z.slots, I32),
        send=v(CAP, W, I32),
        code=v(R, 128, I32),
        wts=v(R, 128, F32),
        counts=v(z.blocks, R, CAP, BF16),
        sel=v(W, CAP, R, BF16),
        msg=v(R, D, BF16),
        zacc=v(R, C, F32),
        zhi=v(R, C, BF16),
        zlo=v(R, C, BF16),
        zsend=v(W, 2, CAP, C, BF16),
        ztab=v(W, 2, CAP, C, BF16),
        acc=v(R, C, F32),
        self_t=v(C, R, F32),
        cot_t=v(C, R, F32),
        invs=v(16, R, F32),
        stat=v(8, R, F32),
        stats=v(N, 8, R, F32),
        emb=v(R, C, BF16),
        gp=v(C, R, BF16),
        gps=v(C, R, BF16),
        gprows=v(N, C, U, BF16),
        gsend=v(W, C, CAP, BF16),
        gret=v(W, C, CAP, BF16),
        yacc=v(C, R, F32),
        y=v(C, R, BF16),
        yrows=v(N, C, U, BF16),
        msg_t=v(D, U, BF16),
        gh=v(D, U, BF16),
        ghc=v(N, C, U, BF16),
        gf=v(D, U, F32),
        gfb=v(D, U, BF16),
        gfc=v(N, C, U, BF16),
        gc=v(2, C, D, BF16),
        gc_in=v(W, 2, z.red_rows, z.red_lanes, BF16),
        gc_sum=v(2, C, D, BF16),
        gn=v(1, C, D, BF16),
        gn_in=v(W, 1, z.red_rows, z.red_lanes, BF16),
        gn_sum=v(1, C, D, BF16),
        gcb=v(8, C, F32),
        gcb_in=v(W, 8, C, F32),
        gnb=v(8, C, F32),
        gnb_in=v(W, 8, C, F32),
    )
    sems = {}
    for name, count in dict(
        nw=N, nwf=N, nb=N, wt=N, wtf=N, st=N, gp_n=N, y_n=N, gh_n=N, gf_n=N,
        z_w=W, gr_w=W, rsc=W, agc=W, rsn=W, agn=W, bc=W, bn=W,
    ).items():
        sems[name + "_s"] = pltpu.SemaphoreType.DMA((count,))
        sems[name + "_r"] = pltpu.SemaphoreType.DMA((count,))
    sems["load"] = pltpu.SemaphoreType.DMA((10,))
    sems["store"] = pltpu.SemaphoreType.DMA((6,))
    return bufs, sems


class Refs:
    pass


def kernel(z, names, *refs):
    g = Refs()
    for name, ref in zip(names, refs):
        setattr(g, name, ref)
    R, D, C, W, N, U, CAP = z.rows, z.width, z.cols, z.wide, z.narrow, z.part, z.cap
    CH = z.chunk
    half = D // 2
    me_w, me_n = lax.axis_index("wide"), lax.axis_index("narrow")
    core = lax.rem(me_w, 2)
    sibling = me_w + 1 - 2 * core

    def loop(count, body, start=0):
        def step(i, carry):
            body(i)
            return carry

        lax.fori_loop(start, count, step, 0)

    def ahead_n(d):
        return lax.rem(me_n + d, N)

    def behind_n(d):
        return lax.rem(me_n - d + N, N)

    def ahead_w(d):
        return lax.rem(me_w + d, W)

    def behind_w(d):
        return lax.rem(me_w - d + W, W)

    def remote(name, d, src, dst, axis, peer):
        return pltpu.make_async_remote_copy(
            src_ref=src,
            dst_ref=dst,
            send_sem=getattr(g, name + "_s").at[d],
            recv_sem=getattr(g, name + "_r").at[d],
            device_id={axis: peer},
            device_id_type=MESH,
        )

    def nw_copy(d):
        return remote("nw", d, g.nw_in.at[at(core, half)], g.nwfull.at[me_n, at(core, half)], "narrow", ahead_n(d))

    def nw_arrive(d):
        s = behind_n(d)
        return remote("nw", d, g.nwfull.at[s, at(core, half)], g.nwfull.at[s, at(core, half)], "narrow", s)

    def nw_forward(d):
        s = behind_n(d)
        return remote("nwf", d, g.nwfull.at[s, at(core, half)], g.nwfull.at[s, at(core, half)], "wide", sibling)

    def nb_copy(d):
        return remote("nb", d, g.nbfull.at[me_n], g.nbfull.at[me_n], "narrow", ahead_n(d))

    def wt_copy(d):
        return remote("wt", d, g.comb_in.at[at(core, D)], g.wfull.at[me_n, at(core, D)], "narrow", ahead_n(d))

    def wt_arrive(d):
        s = behind_n(d)
        return remote("wt", d, g.wfull.at[s, at(core, D)], g.wfull.at[s, at(core, D)], "narrow", s)

    def wt_forward(d):
        s = behind_n(d)
        return remote("wtf", d, g.wfull.at[s, at(core, D)], g.wfull.at[s, at(core, D)], "wide", sibling)

    def z_copy(d):
        peer = ahead_w(d)
        return remote("z_w", d, g.zsend.at[peer], g.ztab.at[me_w], "wide", peer)

    def stat_copy(d):
        return remote("st", d, g.stat, g.stats.at[me_n], "narrow", ahead_n(d))

    def gp_copy(d):
        s = ahead_n(d)
        return remote("gp_n", d, g.gp.at[:, at(s, U)], g.gprows.at[me_n], "narrow", s)

    def ret_copy(d):
        peer = ahead_w(d)
        return remote("gr_w", d, g.gsend.at[peer], g.gret.at[me_w], "wide", peer)

    def y_copy(d):
        s = ahead_n(d)
        return remote("y_n", d, g.y.at[:, at(s, U)], g.yrows.at[me_n], "narrow", s)

    def gh_copy(d):
        s = ahead_n(d)
        return remote("gh_n", d, g.gh.at[at(s, C)], g.ghc.at[me_n], "narrow", s)

    def gf_copy(d):
        s = ahead_n(d)
        return remote("gf_n", d, g.gfb.at[at(s, C)], g.gfc.at[me_n], "narrow", s)

    def red_block(w):
        down, across = lax.rem(w, z.red_down), w // z.red_down
        return (slice(None), at(down, z.red_rows), at(across, z.red_lanes))

    def rs_copy(name, src, dst, d):
        peer = ahead_w(d)
        return remote(name, d, src.at[red_block(peer)], dst.at[me_w], "wide", peer)

    def ag_copy(name, ref, d):
        mine = red_block(me_w)
        return remote(name, d, ref.at[mine], ref.at[mine], "wide", ahead_w(d))

    def bias_copy(name, src, dst, d):
        return remote(name, d, src, dst.at[me_w], "wide", ahead_w(d))

    loads = [
        (g.feats_in, g.feats),
        (g.nw_in, g.nwfull.at[me_n]),
        (g.comb_in, g.wfull.at[me_n]),
        (g.slot_in, g.slot),
        (g.mask_in, g.mask),
        (g.visit_in, g.visit),
        (g.send_in, g.send),
        (g.cot_in, g.cot),
        (g.nb_in, g.nbfull.at[me_n]),
        (g.cb_in, g.cb),
    ]

    def load(i):
        return pltpu.make_async_copy(loads[i][0], loads[i][1], g.load.at[i])

    barrier = pltpu.get_barrier_semaphore()
    loop(W, lambda d: pl.semaphore_signal(barrier, inc=1, device_id={"wide": ahead_w(d)}, device_id_type=MESH), 1)
    loop(N, lambda d: pl.semaphore_signal(barrier, inc=1, device_id={"narrow": ahead_n(d)}, device_id_type=MESH), 1)
    order = (8, 3, 4, 5, 0, 1, 2, 6, 7, 9)
    for i in order:
        load(i).start()
    pl.semaphore_wait(barrier, W - 1 + N - 1)
    loop(N, lambda d: nw_copy(d).start(), 1)
    load(8).wait()
    loop(N, lambda d: nb_copy(d).start(), 1)

    for i in (3, 4, 5):
        load(i).wait()
    K = z.slots
    shift = CAP.bit_length() - 1

    def fill(i):
        rows = at(i, CH)
        g.code[rows, :] = jnp.zeros((CH, 128), I32)
        g.wts[rows, :] = jnp.zeros((CH, 128), F32)
        g.code[rows, 0:K] = g.slot[rows, :]
        g.code[rows, 64 : 64 + K] = g.slot[rows, :]
        weight = (g.mask[rows, :] * g.visit[rows, :]).astype(F32)
        g.wts[rows, 0:K] = weight
        g.wts[rows, 64 : 64 + K] = weight

    loop(R // CH, fill)

    lane = lax.broadcasted_iota(I32, (8, 128), 1)
    sub = lax.broadcasted_iota(I32, (8, 128), 0)
    half_lane = jnp.where(lane >= 64, 1, 0)
    place = [sub == 2 * j + half_lane for j in range(4)]
    place_b = [jnp.where(m, 1.0, 0.0) for m in place]
    place_b = [jnp.concatenate([m, m], axis=0).astype(BF16) for m in place_b]
    low_row = lax.broadcasted_iota(I32, (CAP, 128), 0).astype(F32).astype(BF16)

    def count_group(i):
        start = pl.multiple_of(i * 16, 16)
        outs = []
        for p in range(2):
            rows = pl.ds(pl.multiple_of(start + 8 * p, 8), 8)
            code, weight = g.code[rows, :], g.wts[rows, :]
            high, low = code >> shift, (code & (CAP - 1)).astype(F32)
            left = []
            for h in range(0, z.blocks, 2):
                pair = [jnp.where(high == h + q, weight, 0.0) for q in range(2)]
                pair = jnp.concatenate(pair, axis=0).astype(BF16)
                left.append(jnp.concatenate([pair * place_b[j] for j in range(4)], axis=1))
            left = jnp.concatenate(left, axis=0)
            right = []
            for j in range(4):
                row = jnp.sum(jnp.where(place[j], low, 0.0), axis=0, keepdims=True)
                row = jnp.broadcast_to(row.astype(BF16), (CAP, 128))
                right.append(jnp.where(low_row == row, jnp.ones((), BF16), jnp.zeros((), BF16)))
            outs.append(mm_nt(left, jnp.concatenate(right, axis=1)))
        for h in range(z.blocks):
            block = [out[h * 8 : h * 8 + 8] for out in outs]
            g.counts[h, pl.ds(start, 16), :] = jnp.concatenate(block, axis=0).astype(BF16)

    UNROLL = 4
    groups = R // 16 // UNROLL

    def count_groups(first, last):
        def body(i):
            for q in range(UNROLL):
                count_group(i * UNROLL + q)

        loop(last, body, first)

    def hidden(s):
        def body(i):
            rows = at(i, CH)
            value = mm(g.feats[rows, :], g.nwfull[s]) + g.nbfull[s, 0:1, :]
            value = jnp.maximum(value, 0.0)
            top = value.astype(BF16)
            rest = (value - top.astype(F32)).astype(BF16)
            g.msg[rows, at(s, C)] = top
            weight = g.wfull[me_n, pl.ds(pl.multiple_of(D + s * C, C), C), :]
            g.zacc[rows, :] += mm(top, weight) + mm(rest, weight)

        loop(R // CH, body)

    def zero(i):
        g.zacc[at(i, CH), :] = jnp.zeros((CH, C), F32)

    loop(R // CH, zero)
    for i in (0, 1, 2):
        load(i).wait()
    hidden(me_n)

    load(6).wait()

    def select(d):
        r = ahead_w(d)
        which = lax.broadcasted_iota(I32, (CAP, W), 1)
        col = jnp.sum(jnp.where(which == r, g.send[...], 0), axis=1, keepdims=True)
        place_u = lax.broadcasted_iota(I32, (CAP, R), 1)
        g.sel[r] = jnp.where(place_u == col, 1.0, 0.0).astype(BF16)

    loop(W, select, 1)

    per = groups // N if groups >= N else 0
    for d in range(1, N):
        count_groups((d - 1) * per, d * per)
        nw_arrive(d).wait_recv()
        nw_forward(d).start()
    loop(N, lambda d: wt_copy(d).start(), 1)
    count_groups((N - 1) * per, groups)

    def take(d):
        s = behind_n(d)
        nw_forward(d).wait_recv()
        nb_copy(d).wait_recv()
        hidden(s)

    loop(N, take, 1)

    def split_z(i):
        rows = at(i, CH)
        value = g.zacc[rows, :]
        top = value.astype(BF16)
        g.zhi[rows, :] = top
        g.zlo[rows, :] = (value - top.astype(F32)).astype(BF16)

    loop(R // CH, split_z)

    def send_z(d):
        peer = ahead_w(d)
        g.zsend[peer, 0] = mm(g.sel[peer], g.zhi[...]).astype(BF16)
        g.zsend[peer, 1] = mm(g.sel[peer], g.zlo[...]).astype(BF16)
        z_copy(d).start()

    loop(W, send_z, 1)

    load(7).wait()
    load(9).wait()

    def own_part(i):
        rows = at(i, CH)
        value = mm(g.feats[rows, :], g.wfull[me_n, 0:D, :]) + g.cb[0:1, :]
        g.self_t[:, rows] = value.T
        g.cot_t[:, rows] = g.cot[rows, :].astype(F32).T
        total = jnp.zeros((CH, C), F32)
        for h in range(z.local):
            part = slice(h * CAP, (h + 1) * CAP)
            block = g.counts[h, rows, :]
            total += mm(block, g.zhi[part, :]) + mm(block, g.zlo[part, :])
        g.acc[rows, :] = total

    loop(R // CH, own_part)
    ones = jnp.ones((16, 128), BF16)
    g.invs[...] = 2.0 / mm_nt(ones, g.wts[...].astype(BF16))

    def mine_t(i):
        cols = at(i, C)
        g.msg_t[cols, :] = g.msg[at(me_n, U), cols].astype(F32).T.astype(BF16)

    loop(D // C, mine_t)

    def take_z(d):
        s = behind_w(d)
        z_copy(d).wait_recv()

        def body(i):
            rows = at(i, CH)
            block = g.counts[z.local + s, rows, :]
            g.acc[rows, :] += mm(block, g.ztab[s, 0]) + mm(block, g.ztab[s, 1])

        loop(R // CH, body)

    loop(W, take_z, 1)

    which8 = lax.broadcasted_iota(I32, (8, CH), 0)

    def activate(i):
        rows = at(i, CH)
        pre = g.acc[rows, :].T * g.invs[0:1, rows] + g.self_t[:, rows]
        g.self_t[:, rows] = pre
        act = jnp.maximum(pre, 0.0)
        squares = jnp.sum(act * act, axis=0, keepdims=True)
        inner = jnp.sum(act * g.cot_t[:, rows], axis=0, keepdims=True)
        g.stat[:, rows] = jnp.where(which8 == 0, squares, jnp.where(which8 == 1, inner, 0.0))

    loop(R // CH, activate)
    loop(N, lambda d: stat_copy(d).start(), 1)
    loop(N, lambda d: stat_copy(d).wait_recv(), 1)
    g.stats[me_n] = g.stat[...]

    def norms(rows):
        total = g.stats[0, :, rows]
        for s in range(1, N):
            total += g.stats[s, :, rows]
        return lax.rsqrt(total[0:1] / D + EPSILON), total[1:2]

    def grad_act(i):
        rows = at(i, CH)
        inv, inner = norms(rows)
        pre = g.self_t[:, rows]
        act = jnp.maximum(pre, 0.0)
        grad = g.cot_t[:, rows] * inv - act * (inner * (inv * inv * inv) / D)
        grad = jnp.where(pre > 0, grad, 0.0)
        g.gp[:, rows] = grad.astype(BF16)
        g.gps[:, rows] = (grad * g.invs[0:1, rows]).astype(BF16)

    loop(R // CH, grad_act)
    loop(N, lambda d: gp_copy(d).start(), 1)

    def send_ret(d):
        peer = ahead_w(d)
        g.gsend[peer] = mm(g.gps[...], g.counts[z.local + peer]).astype(BF16)
        ret_copy(d).start()

    loop(W, send_ret, 1)

    join = max(1, 128 // CAP)
    for h in range(0, z.local, join):
        parts = [mm(g.gps[...], g.counts[h + q]) for q in range(join)]
        parts = jnp.concatenate(parts, axis=1) if join > 1 else parts[0]
        g.yacc[:, h * CAP : (h + join) * CAP] = parts

    def embed(i):
        rows = at(i, CH)
        inv, _ = norms(rows)
        value = jnp.maximum(g.self_t[:, rows], 0.0) * inv
        g.emb[rows, :] = value.T.astype(BF16)

    loop(R // CH, embed)
    emb_store = pltpu.make_async_copy(g.emb, g.emb_out, g.store.at[0])
    emb_store.start()

    def pass_weights(d):
        wt_arrive(d).wait_recv()
        wt_forward(d).start()

    loop(N, pass_weights, 1)

    LW = min(512, D)

    def grad_self(i):
        lanes = at(i, LW)
        g.gc[0, :, lanes] = mm(g.gp[...], g.feats[:, lanes]).astype(BF16)

    loop(D // LW, grad_self)
    ones_r = jnp.ones((8, R), BF16)
    g.gcb[...] = mm_nt(ones_r, g.gp[...])

    g.gprows[me_n] = g.gp[:, at(me_n, U)]

    def take_ret(d):
        s = behind_w(d)
        ret_copy(d).wait_recv()

        def body(i):
            lanes = at(i, CH)
            g.yacc[:, lanes] += mm(g.gret[s], g.sel[s, :, lanes])

        loop(R // CH, body)

    loop(W, take_ret, 1)

    def round_y(i):
        lanes = at(i, CH)
        g.y[:, lanes] = g.yacc[:, lanes].astype(BF16)

    loop(R // CH, round_y)
    loop(N, lambda d: y_copy(d).start(), 1)
    g.yrows[me_n] = g.y[:, at(me_n, U)]

    def grad_pool(i):
        lanes = at(i, LW)
        g.gc[1, :, lanes] = mm(g.y[...], g.msg[:, lanes]).astype(BF16)

    loop(D // LW, grad_pool)
    loop(W, lambda d: bias_copy("bc", g.gcb, g.gcb_in, d).start(), 1)
    loop(W, lambda d: rs_copy("rsc", g.gc, g.gc_in, d).start(), 1)

    loop(N, lambda d: gp_copy(d).wait_recv(), 1)
    loop(N, lambda d: wt_forward(d).wait_recv(), 1)

    def self_rows(i):
        rows = at(i, CH)
        total = jnp.zeros((CH, U), F32)
        for s in range(N):
            total += mm(g.wfull[s, rows, :], g.gprows[s])
        g.gf[rows, :] = total

    loop(D // CH, self_rows)
    loop(N, lambda d: y_copy(d).wait_recv(), 1)

    def hidden_rows(i):
        rows = at(i, CH)
        wrows = pl.ds(pl.multiple_of(D + i * CH, CH), CH)
        total = jnp.zeros((CH, U), F32)
        for s in range(N):
            total += mm(g.wfull[s, wrows, :], g.yrows[s])
        g.gh[rows, :] = jnp.where(g.msg_t[rows, :] > 0, total, 0.0).astype(BF16)

    loop(D // CH, hidden_rows)
    loop(N, lambda d: gh_copy(d).start(), 1)
    g.ghc[me_n] = g.gh[at(me_n, C), :]

    def feature_rows(i):
        rows = at(i, CH)
        total = g.gf[rows, :]
        for s in range(N):
            total += mm(g.nwfull[s, rows, :], g.gh[s * C : (s + 1) * C, :])
        g.gfb[rows, :] = total.astype(BF16)

    loop(D // CH, feature_rows)
    loop(N, lambda d: gf_copy(d).start(), 1)
    g.gfc[me_n] = g.gfb[at(me_n, C), :]

    def reduce_sum(own, arrived, out):
        mine = red_block(me_w)
        total = own[mine].astype(F32)

        def body(d, total):
            return total + arrived[behind_w(d)].astype(F32)

        out[mine] = lax.fori_loop(1, W, body, total).astype(BF16)

    loop(W, lambda d: rs_copy("rsc", g.gc, g.gc_in, d).wait_recv(), 1)
    reduce_sum(g.gc, g.gc_in, g.gc_sum)
    loop(W, lambda d: ag_copy("agc", g.gc_sum, d).start(), 1)

    loop(N, lambda d: gh_copy(d).wait_recv(), 1)

    def grad_neigh(i):
        lanes = at(i, LW)
        total = jnp.zeros((C, LW), F32)
        for s in range(N):
            total += mm(g.ghc[s], g.feats[s * U : (s + 1) * U, lanes])
        g.gn[0, :, lanes] = total.astype(BF16)

    loop(D // LW, grad_neigh)
    total = jnp.zeros((8, C), F32)
    ones_u = jnp.ones((8, U), BF16)
    for s in range(N):
        total += mm_nt(ones_u, g.ghc[s])
    g.gnb[...] = total
    loop(W, lambda d: rs_copy("rsn", g.gn, g.gn_in, d).start(), 1)
    loop(W, lambda d: bias_copy("bn", g.gnb, g.gnb_in, d).start(), 1)

    loop(N, lambda d: gf_copy(d).wait_recv(), 1)
    gf_store = pltpu.make_async_copy(g.gfc, g.gf_out, g.store.at[1])
    gf_store.start()

    loop(W, lambda d: rs_copy("rsn", g.gn, g.gn_in, d).wait_recv(), 1)
    reduce_sum(g.gn, g.gn_in, g.gn_sum)
    loop(W, lambda d: ag_copy("agn", g.gn_sum, d).start(), 1)

    def bias_sum(name, own, arrived):
        loop(W, lambda d: bias_copy(name, own, arrived, d).wait_recv(), 1)
        loop(W, lambda d: bias_copy(name, own, arrived, d).wait_send(), 1)

        def body(d, total):
            return total + arrived[behind_w(d)]

        own[...] = lax.fori_loop(1, W, body, own[...])

    bias_sum("bc", g.gcb, g.gcb_in)
    bias_sum("bn", g.gnb, g.gnb_in)

    def ag_arrive(name, ref, d):
        theirs = red_block(behind_w(d))
        return remote(name, d, ref.at[theirs], ref.at[theirs], "wide", behind_w(d))

    loop(W, lambda d: ag_arrive("agc", g.gc_sum, d).wait_recv(), 1)
    stores = [
        emb_store,
        gf_store,
        pltpu.make_async_copy(g.gc_sum, g.gc_out, g.store.at[2]),
        pltpu.make_async_copy(g.gcb, g.gcb_out, g.store.at[3]),
        pltpu.make_async_copy(g.gnb, g.gnb_out, g.store.at[4]),
        pltpu.make_async_copy(g.gn_sum, g.gn_out, g.store.at[5]),
    ]
    for store in stores[2:5]:
        store.start()
    loop(W, lambda d: ag_arrive("agn", g.gn_sum, d).wait_recv(), 1)
    stores[5].start()

    def drain_n(d):
        for copy in (nw_copy, nw_forward, nb_copy, wt_copy, wt_forward, stat_copy, gp_copy, y_copy, gh_copy, gf_copy):
            copy(d).wait_send()

    def drain_w(d):
        z_copy(d).wait_send()
        ret_copy(d).wait_send()
        rs_copy("rsc", g.gc, g.gc_in, d).wait_send()
        ag_copy("agc", g.gc_sum, d).wait_send()
        rs_copy("rsn", g.gn, g.gn_in, d).wait_send()
        ag_copy("agn", g.gn_sum, d).wait_send()

    loop(N, drain_n, 1)
    loop(W, drain_w, 1)
    for store in stores:
        store.wait()


def shards(wide, narrow, node_feats, neigh_weight, neigh_bias, combine_weight, combine_bias, cotangent,
           neighbour_slot, neighbour_mask, visit_count, send_rows):
    z = Sizes(node_feats, neigh_weight, send_rows, neighbour_slot, wide, narrow)
    R, D, C, W, N, U = z.rows, z.width, z.cols, z.wide, z.narrow, z.part
    bufs, sems = scratch(z)
    names = NAMES_IN + NAMES_OUT + list(bufs) + list(sems)
    rows8 = lambda b: jnp.broadcast_to(b.astype(F32)[None, :], (8, C))
    outs = (
        jax.ShapeDtypeStruct((R, C), BF16),
        jax.ShapeDtypeStruct((N, C, U), BF16),
        jax.ShapeDtypeStruct((1, C, D), BF16),
        jax.ShapeDtypeStruct((2, C, D), BF16),
        jax.ShapeDtypeStruct((8, C), F32),
        jax.ShapeDtypeStruct((8, C), F32),
    )
    emb, gf, gn, gc, gnb, gcb = pl.pallas_call(
        functools.partial(kernel, z, names),
        out_shape=outs,
        in_specs=[pl.BlockSpec(memory_space=pl.ANY)] * len(NAMES_IN),
        out_specs=[pl.BlockSpec(memory_space=pl.ANY)] * len(NAMES_OUT),
        scratch_shapes=list(bufs.values()) + list(sems.values()),
        compiler_params=pltpu.CompilerParams(
            collective_id=0, has_side_effects=True, vmem_limit_bytes=60 * 2**20
        ),
        cost_estimate=pl.CostEstimate(flops=2 * 10**10, bytes_accessed=2 * 10**7, transcendentals=0),
        name="layer",
    )(
        node_feats, neigh_weight, rows8(neigh_bias), combine_weight, rows8(combine_bias), cotangent,
        neighbour_slot, neighbour_mask, visit_count, send_rows.T,
    )
    grad_features = gf.transpose(0, 2, 1).reshape(R, C).astype(F32)
    grad_neigh = gn[0].T.astype(F32)
    grad_combine = gc.transpose(0, 2, 1).reshape(2 * D, C).astype(F32)
    return emb, grad_features, grad_neigh, gnb[0], grad_combine, gcb[0]


def solution(mesh):
    placed = (
        P("wide", None),
        P(None, "narrow"),
        P("narrow"),
        P(None, "narrow"),
        P("narrow"),
        P("wide", "narrow"),
        P("wide", None),
        P("wide", None),
        P("wide", None),
        P("wide", None),
    )
    return jax.shard_map(
        functools.partial(shards, mesh.shape["wide"], mesh.shape["narrow"]),
        mesh=mesh,
        in_specs=placed,
        out_specs=(
            P("wide", "narrow"),
            P("wide", "narrow"),
            P(None, "narrow"),
            P("narrow"),
            P(None, "narrow"),
            P("narrow"),
        ),
        check_vma=False,
    )
```

```python
import functools

import jax
import jax.numpy as jnp
from jax import lax
from jax.experimental import pallas as pl
from jax.experimental.pallas import tpu as pltpu
from jax.sharding import PartitionSpec as P

EPSILON = 1e-06
F32 = jnp.float32
BF16 = jnp.bfloat16
I32 = jnp.int32
MESH = pl.DeviceIdType.MESH


def mm(left, right):
    return jnp.dot(left, right, preferred_element_type=F32)


def mm_nt(left, right):
    return lax.dot_general(left, right, (((1,), (1,)), ((), ())), preferred_element_type=F32)


def at(index, size):
    return pl.ds(pl.multiple_of(index * size, size), size)


class Sizes:
    def __init__(self, feats, neigh, send, slot, wide, narrow):
        self.rows, self.width = feats.shape
        self.cols = neigh.shape[1]
        self.cap = send.shape[1]
        self.slots = slot.shape[0]
        self.wide, self.narrow = wide, narrow
        self.chunk = min(256, self.rows)
        self.part = self.rows // narrow
        self.local = self.rows // self.cap
        self.blocks = self.local + wide
        self.red_rows = max(16, self.cols // wide)
        self.red_down = self.cols // self.red_rows
        self.red_across = wide // self.red_down
        self.red_lanes = self.width // self.red_across


NAMES_IN = ["feats_in", "nw_in", "nb_in", "comb_in", "cb_in", "cot_in", "slot_in", "mask_in", "visit_in", "send_in"]
NAMES_OUT = ["emb_out", "gf_out", "gn_out", "gc_out", "gnb_out", "gcb_out"]


def scratch(z):
    R, D, C, W, N, U, CAP = z.rows, z.width, z.cols, z.wide, z.narrow, z.part, z.cap
    v = lambda *shape: pltpu.VMEM(shape[:-1], shape[-1])
    bufs = dict(
        feats=v(R, D, BF16),
        nwfull=v(N, D, C, BF16),
        nbfull=v(N, 8, C, F32),
        wfull=v(N, 2 * D, C, BF16),
        cot=v(R, C, BF16),
        slot=v(z.slots, R, I32),
        mask=v(z.slots, R, I32),
        visit=v(z.slots, R, I32),
        send=v(W, CAP, I32),
        send_t=v(CAP, W, I32),
        code=v(R, 128, I32),
        wts=v(R, 128, F32),
        counts=v(z.blocks, R, CAP, BF16),
        sel=v(W, CAP, R, BF16),
        msg=v(R, D, BF16),
        zacc=v(R, C, F32),
        zhi=v(R, C, BF16),
        zlo=v(R, C, BF16),
        zsend=v(W, 2, CAP, C, BF16),
        ztab=v(W, 2, CAP, C, BF16),
        acc=v(R, C, F32),
        self_t=v(C, R, F32),
        cot_t=v(C, R, F32),
        invs=v(16, R, F32),
        stat=v(8, R, F32),
        stats=v(N, 8, R, F32),
        emb=v(R, C, BF16),
        gp=v(C, R, BF16),
        gps=v(C, R, BF16),
        gprows=v(N, C, U, BF16),
        gsend=v(W, C, CAP, BF16),
        gret=v(W, C, CAP, BF16),
        yacc=v(C, R, F32),
        y=v(C, R, BF16),
        yrows=v(N, C, U, BF16),
        msg_t=v(D, U, BF16),
        gh=v(D, U, BF16),
        ghc=v(N, C, U, BF16),
        gf=v(D, U, F32),
        gfb=v(D, U, BF16),
        gfc=v(N, C, U, BF16),
        gc=v(2, C, D, BF16),
        gc_in=v(W, 2, z.red_rows, z.red_lanes, BF16),
        gc_sum=v(2, C, D, BF16),
        gn=v(1, C, D, BF16),
        gn_in=v(W, 1, z.red_rows, z.red_lanes, BF16),
        gn_sum=v(1, C, D, BF16),
        gcb=v(8, C, F32),
        gcb_in=v(W, 8, C, F32),
        gnb=v(8, C, F32),
        gnb_in=v(W, 8, C, F32),
    )
    sems = {}
    for name, count in dict(
        nw=N, nwp=(N, W // 2), nwf=N, nb=N, wt=N, wtf=N, st=N, gp_n=N, y_n=N, gh_n=N, gf_n=N,
        z_w=W, gr_w=W, rsc=W, agc=W, rsn=W, agn=W, bc=W, bn=W,
    ).items():
        sems[name + "_s"] = pltpu.SemaphoreType.DMA(count if isinstance(count, tuple) else (count,))
        sems[name + "_r"] = pltpu.SemaphoreType.DMA(count if isinstance(count, tuple) else (count,))
    sems["load"] = pltpu.SemaphoreType.DMA((10,))
    sems["store"] = pltpu.SemaphoreType.DMA((6,))
    return bufs, sems


class Refs:
    pass


def kernel(z, names, *refs):
    g = Refs()
    for name, ref in zip(names, refs):
        setattr(g, name, ref)
    R, D, C, W, N, U, CAP = z.rows, z.width, z.cols, z.wide, z.narrow, z.part, z.cap
    CH = z.chunk
    half = D // 2
    me_w, me_n = lax.axis_index("wide"), lax.axis_index("narrow")
    core = lax.rem(me_w, 2)
    sibling = me_w + 1 - 2 * core

    def loop(count, body, start=0):
        def step(i, carry):
            body(i)
            return carry

        lax.fori_loop(start, count, step, 0)

    def ahead_n(d):
        return lax.rem(me_n + d, N)

    def behind_n(d):
        return lax.rem(me_n - d + N, N)

    def ahead_w(d):
        return lax.rem(me_w + d, W)

    def behind_w(d):
        return lax.rem(me_w - d + W, W)

    def remote(name, index, src, dst, axis, peer):
        return pltpu.make_async_remote_copy(
            src_ref=src,
            dst_ref=dst,
            send_sem=getattr(g, name + "_s").at[index],
            recv_sem=getattr(g, name + "_r").at[index],
            device_id={axis: peer},
            device_id_type=MESH,
        )

    def share(w):
        return at(lax.rem(w, 2) * (W // 2) + w // 2, D // W)

    def nw_copy(d):
        mine = share(me_w)
        return remote("nw", d, g.nw_in.at[mine], g.nwfull.at[me_n, mine], "narrow", ahead_n(d))

    def nw_pass(d, e):
        part = g.nwfull.at[behind_n(d), share(me_w)]
        return remote("nwp", (d, e), part, part, "wide", ahead_w(2 * e))

    def nw_forward(d):
        part = g.nwfull.at[behind_n(d), at(core, half)]
        return remote("nwf", d, part, part, "wide", sibling)

    def nb_copy(d):
        return remote("nb", d, g.nbfull.at[me_n], g.nbfull.at[me_n], "narrow", ahead_n(d))

    def wt_copy(d):
        return remote("wt", d, g.comb_in.at[at(core, D)], g.wfull.at[me_n, at(core, D)], "narrow", ahead_n(d))

    def wt_arrive(d):
        s = behind_n(d)
        return remote("wt", d, g.wfull.at[s, at(core, D)], g.wfull.at[s, at(core, D)], "narrow", s)

    def wt_forward(d):
        s = behind_n(d)
        return remote("wtf", d, g.wfull.at[s, at(core, D)], g.wfull.at[s, at(core, D)], "wide", sibling)

    def z_copy(d):
        peer = ahead_w(d)
        return remote("z_w", d, g.zsend.at[peer], g.ztab.at[me_w], "wide", peer)

    def stat_copy(d):
        return remote("st", d, g.stat, g.stats.at[me_n], "narrow", ahead_n(d))

    def gp_copy(d):
        s = ahead_n(d)
        return remote("gp_n", d, g.gp.at[:, at(s, U)], g.gprows.at[me_n], "narrow", s)

    def ret_copy(d):
        peer = ahead_w(d)
        return remote("gr_w", d, g.gsend.at[peer], g.gret.at[me_w], "wide", peer)

    def y_copy(d):
        s = ahead_n(d)
        return remote("y_n", d, g.y.at[:, at(s, U)], g.yrows.at[me_n], "narrow", s)

    def gh_copy(d):
        s = ahead_n(d)
        return remote("gh_n", d, g.gh.at[at(s, C)], g.ghc.at[me_n], "narrow", s)

    def gf_copy(d):
        s = ahead_n(d)
        return remote("gf_n", d, g.gfb.at[at(s, C)], g.gfc.at[me_n], "narrow", s)

    def red_block(w):
        down, across = lax.rem(w, z.red_down), w // z.red_down
        return (slice(None), at(down, z.red_rows), at(across, z.red_lanes))

    def rs_copy(name, src, dst, d):
        peer = ahead_w(d)
        return remote(name, d, src.at[red_block(peer)], dst.at[me_w], "wide", peer)

    def ag_copy(name, ref, d):
        mine = red_block(me_w)
        return remote(name, d, ref.at[mine], ref.at[mine], "wide", ahead_w(d))

    def bias_copy(name, src, dst, d):
        return remote(name, d, src, dst.at[me_w], "wide", ahead_w(d))

    loads = [
        (g.feats_in, g.feats),
        (g.nw_in, g.nwfull.at[me_n]),
        (g.comb_in, g.wfull.at[me_n]),
        (g.slot_in, g.slot),
        (g.mask_in, g.mask),
        (g.visit_in, g.visit),
        (g.send_in, g.send),
        (g.cot_in, g.cot),
    ]

    def load(i):
        return pltpu.make_async_copy(loads[i][0], loads[i][1], g.load.at[i])

    barrier = pltpu.get_barrier_semaphore()
    loop(W, lambda d: pl.semaphore_signal(barrier, inc=1, device_id={"wide": ahead_w(d)}, device_id_type=MESH), 1)
    loop(N, lambda d: pl.semaphore_signal(barrier, inc=1, device_id={"narrow": ahead_n(d)}, device_id_type=MESH), 1)
    order = (3, 4, 5, 0, 1, 2, 6, 7)
    for i in order:
        load(i).start()
    pl.semaphore_wait(barrier, W - 1 + N - 1)
    loop(N, lambda d: nw_copy(d).start(), 1)
    g.nbfull[me_n] = jnp.broadcast_to(g.nb_in[...].astype(F32), (8, C))
    loop(N, lambda d: nb_copy(d).start(), 1)

    for i in (3, 4, 5):
        load(i).wait()
    K = z.slots
    shift = CAP.bit_length() - 1

    def fill(i):
        rows = at(i, CH)
        g.code[rows, :] = jnp.zeros((CH, 128), I32)
        g.wts[rows, :] = jnp.zeros((CH, 128), F32)
        code = g.slot[:, rows].T
        g.code[rows, 0:K] = code
        g.code[rows, 64 : 64 + K] = code
        weight = (g.mask[:, rows] * g.visit[:, rows]).astype(F32).T
        g.wts[rows, 0:K] = weight
        g.wts[rows, 64 : 64 + K] = weight

    loop(R // CH, fill)

    lane = lax.broadcasted_iota(I32, (8, 128), 1)
    sub = lax.broadcasted_iota(I32, (8, 128), 0)
    half_lane = jnp.where(lane >= 64, 1, 0)
    place = [sub == 2 * j + half_lane for j in range(4)]
    place_b = [jnp.where(m, 1.0, 0.0) for m in place]
    place_b = [jnp.concatenate([m, m], axis=0).astype(BF16) for m in place_b]
    low_row = lax.broadcasted_iota(I32, (CAP, 128), 0).astype(F32).astype(BF16)

    def count_group(i):
        start = pl.multiple_of(i * 16, 16)
        outs = []
        for p in range(2):
            rows = pl.ds(pl.multiple_of(start + 8 * p, 8), 8)
            code, weight = g.code[rows, :], g.wts[rows, :]
            high, low = code >> shift, (code & (CAP - 1)).astype(F32)
            left = []
            for h in range(0, z.blocks, 2):
                pair = [jnp.where(high == h + q, weight, 0.0) for q in range(2)]
                pair = jnp.concatenate(pair, axis=0).astype(BF16)
                left.append(jnp.concatenate([pair * place_b[j] for j in range(4)], axis=1))
            left = jnp.concatenate(left, axis=0)
            right = []
            for j in range(4):
                row = jnp.sum(jnp.where(place[j], low, 0.0), axis=0, keepdims=True)
                row = jnp.broadcast_to(row.astype(BF16), (CAP, 128))
                right.append(jnp.where(low_row == row, jnp.ones((), BF16), jnp.zeros((), BF16)))
            outs.append(mm_nt(left, jnp.concatenate(right, axis=1)))
        for h in range(z.blocks):
            block = [out[h * 8 : h * 8 + 8] for out in outs]
            g.counts[h, pl.ds(start, 16), :] = jnp.concatenate(block, axis=0).astype(BF16)

    UNROLL = 4
    groups = R // 16 // UNROLL

    def count_groups(first, last):
        def body(i):
            for q in range(UNROLL):
                count_group(i * UNROLL + q)

        loop(last, body, first)

    def hidden(s):
        def body(i):
            rows = at(i, CH)
            value = mm(g.feats[rows, :], g.nwfull[s]) + g.nbfull[s, 0:1, :]
            value = jnp.maximum(value, 0.0)
            top = value.astype(BF16)
            rest = (value - top.astype(F32)).astype(BF16)
            g.msg[rows, at(s, C)] = top
            weight = g.wfull[me_n, pl.ds(pl.multiple_of(D + s * C, C), C), :]
            g.zacc[rows, :] += mm(top, weight) + mm(rest, weight)

        loop(R // CH, body)

    def zero(i):
        g.zacc[at(i, CH), :] = jnp.zeros((CH, C), F32)

    count_groups(0, groups // 4)
    def pass_nw(d):
        nw_copy(d).wait_recv()
        loop(W // 2, lambda e: nw_pass(d, e).start(), 1)

    loop(N, pass_nw, 1)
    loop(N, lambda d: wt_copy(d).start(), 1)
    loop(R // CH, zero)
    for i in (0, 1, 2):
        load(i).wait()
    hidden(me_n)
    load(6).wait()
    g.send_t[...] = g.send[...].T

    def select(d):
        r = ahead_w(d)
        which = lax.broadcasted_iota(I32, (CAP, W), 1)
        col = jnp.sum(jnp.where(which == r, g.send_t[...], 0), axis=1, keepdims=True)
        place_u = lax.broadcasted_iota(I32, (CAP, R), 1)
        g.sel[r] = jnp.where(place_u == col, 1.0, 0.0).astype(BF16)

    loop(W, select, 1)
    count_groups(groups // 4, groups // 2)
    def forward_nw(d):
        loop(W // 2, lambda e: nw_pass(d, e).wait_recv(), 1)
        nw_forward(d).start()

    loop(N, forward_nw, 1)

    def take(d):
        s = behind_n(d)
        nw_forward(d).wait_recv()
        nb_copy(d).wait_recv()
        hidden(s)

    loop(N, take, 1)

    def split_z(i):
        rows = at(i, CH)
        value = g.zacc[rows, :]
        top = value.astype(BF16)
        g.zhi[rows, :] = top
        g.zlo[rows, :] = (value - top.astype(F32)).astype(BF16)

    loop(R // CH, split_z)

    def send_z(d):
        peer = ahead_w(d)
        g.zsend[peer, 0] = mm(g.sel[peer], g.zhi[...]).astype(BF16)
        g.zsend[peer, 1] = mm(g.sel[peer], g.zlo[...]).astype(BF16)
        z_copy(d).start()

    loop(W, send_z, 1)

    count_groups(groups // 2, groups)
    load(7).wait()

    def own_part(i):
        rows = at(i, CH)
        value = mm(g.feats[rows, :], g.wfull[me_n, 0:D, :]) + g.cb_in[...].astype(F32)
        g.self_t[:, rows] = value.T
        g.cot_t[:, rows] = g.cot[rows, :].astype(F32).T
        total = jnp.zeros((CH, C), F32)
        for h in range(z.local):
            part = slice(h * CAP, (h + 1) * CAP)
            block = g.counts[h, rows, :]
            total += mm(block, g.zhi[part, :]) + mm(block, g.zlo[part, :])
        g.acc[rows, :] = total

    loop(R // CH, own_part)
    ones = jnp.ones((16, 128), BF16)
    g.invs[...] = 2.0 / mm_nt(ones, g.wts[...].astype(BF16))

    def mine_t(i):
        cols = at(i, C)
        g.msg_t[cols, :] = g.msg[at(me_n, U), cols].astype(F32).T.astype(BF16)

    loop(D // C, mine_t)

    def take_z(d):
        s = behind_w(d)
        z_copy(d).wait_recv()

        def body(i):
            rows = at(i, CH)
            block = g.counts[z.local + s, rows, :]
            g.acc[rows, :] += mm(block, g.ztab[s, 0]) + mm(block, g.ztab[s, 1])

        loop(R // CH, body)

    loop(W, take_z, 1)

    which8 = lax.broadcasted_iota(I32, (8, CH), 0)

    def activate(i):
        rows = at(i, CH)
        pre = g.acc[rows, :].T * g.invs[0:1, rows] + g.self_t[:, rows]
        g.self_t[:, rows] = pre
        act = jnp.maximum(pre, 0.0)
        squares = jnp.sum(act * act, axis=0, keepdims=True)
        inner = jnp.sum(act * g.cot_t[:, rows], axis=0, keepdims=True)
        g.stat[:, rows] = jnp.where(which8 == 0, squares, jnp.where(which8 == 1, inner, 0.0))

    loop(R // CH, activate)
    loop(N, lambda d: stat_copy(d).start(), 1)
    loop(N, lambda d: stat_copy(d).wait_recv(), 1)
    g.stats[me_n] = g.stat[...]

    def norms(rows):
        total = g.stats[0, :, rows]
        for s in range(1, N):
            total += g.stats[s, :, rows]
        return lax.rsqrt(total[0:1] / D + EPSILON), total[1:2]

    def grad_act(i):
        rows = at(i, CH)
        inv, inner = norms(rows)
        pre = g.self_t[:, rows]
        act = jnp.maximum(pre, 0.0)
        grad = g.cot_t[:, rows] * inv - act * (inner * (inv * inv * inv) / D)
        grad = jnp.where(pre > 0, grad, 0.0)
        g.gp[:, rows] = grad.astype(BF16)
        g.gps[:, rows] = (grad * g.invs[0:1, rows]).astype(BF16)

    loop(R // CH, grad_act)
    loop(N, lambda d: gp_copy(d).start(), 1)

    def send_ret(d):
        peer = ahead_w(d)
        g.gsend[peer] = mm(g.gps[...], g.counts[z.local + peer]).astype(BF16)
        ret_copy(d).start()

    loop(W, send_ret, 1)

    join = max(1, 128 // CAP)
    for h in range(0, z.local, join):
        parts = [mm(g.gps[...], g.counts[h + q]) for q in range(join)]
        parts = jnp.concatenate(parts, axis=1) if join > 1 else parts[0]
        g.yacc[:, h * CAP : (h + join) * CAP] = parts

    def embed(i):
        rows = at(i, CH)
        inv, _ = norms(rows)
        value = jnp.maximum(g.self_t[:, rows], 0.0) * inv
        g.emb[rows, :] = value.T.astype(BF16)

    loop(R // CH, embed)
    emb_store = pltpu.make_async_copy(g.emb, g.emb_out, g.store.at[0])
    emb_store.start()

    def pass_weights(d):
        wt_arrive(d).wait_recv()
        wt_forward(d).start()

    loop(N, pass_weights, 1)

    LW = min(512, D)

    def grad_self(i):
        lanes = at(i, LW)
        g.gc[0, :, lanes] = mm(g.gp[...], g.feats[:, lanes]).astype(BF16)

    loop(D // LW, grad_self)
    ones_r = jnp.ones((8, R), BF16)
    g.gcb[...] = mm_nt(ones_r, g.gp[...])

    g.gprows[me_n] = g.gp[:, at(me_n, U)]

    def take_ret(d):
        s = behind_w(d)
        ret_copy(d).wait_recv()

        def body(i):
            lanes = at(i, CH)
            g.yacc[:, lanes] += mm(g.gret[s], g.sel[s, :, lanes])

        loop(R // CH, body)

    loop(W, take_ret, 1)

    def round_y(i):
        lanes = at(i, CH)
        g.y[:, lanes] = g.yacc[:, lanes].astype(BF16)

    loop(R // CH, round_y)
    loop(N, lambda d: y_copy(d).start(), 1)
    g.yrows[me_n] = g.y[:, at(me_n, U)]

    def grad_pool(i):
        lanes = at(i, LW)
        g.gc[1, :, lanes] = mm(g.y[...], g.msg[:, lanes]).astype(BF16)

    loop(D // LW, grad_pool)
    loop(W, lambda d: bias_copy("bc", g.gcb, g.gcb_in, d).start(), 1)
    loop(W, lambda d: rs_copy("rsc", g.gc, g.gc_in, d).start(), 1)

    loop(N, lambda d: gp_copy(d).wait_recv(), 1)
    loop(N, lambda d: wt_forward(d).wait_recv(), 1)

    def self_rows(i):
        rows = at(i, CH)
        total = jnp.zeros((CH, U), F32)
        for s in range(N):
            total += mm(g.wfull[s, rows, :], g.gprows[s])
        g.gf[rows, :] = total

    loop(D // CH, self_rows)
    loop(N, lambda d: y_copy(d).wait_recv(), 1)

    def hidden_rows(i):
        rows = at(i, CH)
        wrows = pl.ds(pl.multiple_of(D + i * CH, CH), CH)
        total = jnp.zeros((CH, U), F32)
        for s in range(N):
            total += mm(g.wfull[s, wrows, :], g.yrows[s])
        g.gh[rows, :] = jnp.where(g.msg_t[rows, :] > 0, total, 0.0).astype(BF16)

    loop(D // CH, hidden_rows)
    loop(N, lambda d: gh_copy(d).start(), 1)
    g.ghc[me_n] = g.gh[at(me_n, C), :]

    def feature_rows(i):
        rows = at(i, CH)
        total = g.gf[rows, :]
        for s in range(N):
            total += mm(g.nwfull[s, rows, :], g.gh[s * C : (s + 1) * C, :])
        g.gfb[rows, :] = total.astype(BF16)

    loop(D // CH, feature_rows)
    loop(N, lambda d: gf_copy(d).start(), 1)
    g.gfc[me_n] = g.gfb[at(me_n, C), :]

    def reduce_sum(own, arrived, out):
        mine = red_block(me_w)
        total = own[mine].astype(F32)

        def body(d, total):
            return total + arrived[behind_w(d)].astype(F32)

        out[mine] = lax.fori_loop(1, W, body, total).astype(BF16)

    loop(W, lambda d: rs_copy("rsc", g.gc, g.gc_in, d).wait_recv(), 1)
    reduce_sum(g.gc, g.gc_in, g.gc_sum)
    loop(W, lambda d: ag_copy("agc", g.gc_sum, d).start(), 1)

    loop(N, lambda d: gh_copy(d).wait_recv(), 1)

    def grad_neigh(i):
        lanes = at(i, LW)
        total = jnp.zeros((C, LW), F32)
        for s in range(N):
            total += mm(g.ghc[s], g.feats[s * U : (s + 1) * U, lanes])
        g.gn[0, :, lanes] = total.astype(BF16)

    loop(D // LW, grad_neigh)
    total = jnp.zeros((8, C), F32)
    ones_u = jnp.ones((8, U), BF16)
    for s in range(N):
        total += mm_nt(ones_u, g.ghc[s])
    g.gnb[...] = total
    loop(W, lambda d: rs_copy("rsn", g.gn, g.gn_in, d).start(), 1)
    loop(W, lambda d: bias_copy("bn", g.gnb, g.gnb_in, d).start(), 1)

    loop(N, lambda d: gf_copy(d).wait_recv(), 1)
    gf_store = pltpu.make_async_copy(g.gfc, g.gf_out, g.store.at[1])
    gf_store.start()

    loop(W, lambda d: rs_copy("rsn", g.gn, g.gn_in, d).wait_recv(), 1)
    reduce_sum(g.gn, g.gn_in, g.gn_sum)
    loop(W, lambda d: ag_copy("agn", g.gn_sum, d).start(), 1)

    def bias_sum(name, own, arrived):
        loop(W, lambda d: bias_copy(name, own, arrived, d).wait_recv(), 1)
        loop(W, lambda d: bias_copy(name, own, arrived, d).wait_send(), 1)

        def body(d, total):
            return total + arrived[behind_w(d)]

        own[...] = lax.fori_loop(1, W, body, own[...])

    bias_sum("bc", g.gcb, g.gcb_in)
    bias_sum("bn", g.gnb, g.gnb_in)

    def ag_arrive(name, ref, d):
        theirs = red_block(behind_w(d))
        return remote(name, d, ref.at[theirs], ref.at[theirs], "wide", behind_w(d))

    loop(W, lambda d: ag_arrive("agc", g.gc_sum, d).wait_recv(), 1)
    stores = [
        emb_store,
        gf_store,
        pltpu.make_async_copy(g.gc_sum, g.gc_out, g.store.at[2]),
        pltpu.make_async_copy(g.gcb, g.gcb_out, g.store.at[3]),
        pltpu.make_async_copy(g.gnb, g.gnb_out, g.store.at[4]),
        pltpu.make_async_copy(g.gn_sum, g.gn_out, g.store.at[5]),
    ]
    for store in stores[2:5]:
        store.start()
    loop(W, lambda d: ag_arrive("agn", g.gn_sum, d).wait_recv(), 1)
    stores[5].start()

    def drain_n(d):
        loop(W // 2, lambda e: nw_pass(d, e).wait_send(), 1)
        for copy in (nw_copy, nw_forward, nb_copy, wt_copy, wt_forward, stat_copy, gp_copy, y_copy, gh_copy, gf_copy):
            copy(d).wait_send()

    def drain_w(d):
        z_copy(d).wait_send()
        ret_copy(d).wait_send()
        rs_copy("rsc", g.gc, g.gc_in, d).wait_send()
        ag_copy("agc", g.gc_sum, d).wait_send()
        rs_copy("rsn", g.gn, g.gn_in, d).wait_send()
        ag_copy("agn", g.gn_sum, d).wait_send()

    loop(N, drain_n, 1)
    loop(W, drain_w, 1)
    for store in stores:
        store.wait()


def finish(emb_in, gf, gn, gc, gnb, gcb, emb_out, gf_out, gn_out, gc_out, gnb_out, gcb_out):
    gf_out[...] = gf[0].astype(F32).T
    gn_out[...] = gn[0].astype(F32).T
    for i in range(2):
        gc_out[i] = gc[i].astype(F32).T
    gnb_out[...] = gnb[0:1, :]
    gcb_out[...] = gcb[0:1, :]


def shards(wide, narrow, node_feats, neigh_weight, neigh_bias, combine_weight, combine_bias, cotangent,
           neighbour_slot, neighbour_mask, visit_count, send_rows):
    z = Sizes(node_feats, neigh_weight, send_rows, neighbour_slot.T, wide, narrow)
    R, D, C, W, N, U = z.rows, z.width, z.cols, z.wide, z.narrow, z.part
    bufs, sems = scratch(z)
    names = NAMES_IN + NAMES_OUT + list(bufs) + list(sems)
    outs = (
        jax.ShapeDtypeStruct((R, C), BF16),
        jax.ShapeDtypeStruct((N, C, U), BF16),
        jax.ShapeDtypeStruct((1, C, D), BF16),
        jax.ShapeDtypeStruct((2, C, D), BF16),
        jax.ShapeDtypeStruct((8, C), F32),
        jax.ShapeDtypeStruct((8, C), F32),
    )
    emb, gf, gn, gc, gnb, gcb = pl.pallas_call(
        functools.partial(kernel, z, names),
        out_shape=outs,
        in_specs=[
            pl.BlockSpec(memory_space=pltpu.VMEM if name in ("nb_in", "cb_in") else pl.ANY) for name in NAMES_IN
        ],
        out_specs=[pl.BlockSpec(memory_space=pl.ANY)] * len(NAMES_OUT),
        scratch_shapes=list(bufs.values()) + list(sems.values()),
        compiler_params=pltpu.CompilerParams(
            collective_id=0, has_side_effects=True, vmem_limit_bytes=60 * 2**20
        ),
        cost_estimate=pl.CostEstimate(flops=2 * 10**10, bytes_accessed=2 * 10**7, transcendentals=0),
        name="layer",
    )(
        node_feats, neigh_weight, neigh_bias.reshape(1, C), combine_weight, combine_bias.reshape(1, C), cotangent,
        neighbour_slot.T, neighbour_mask.T, visit_count.T, send_rows,
    )
    Q = D // N
    whole = pl.BlockSpec((8, C), lambda i: (0, 0))
    line = pl.BlockSpec((1, C), lambda i: (0, 0))
    emb, grad_features, grad_neigh, grad_combine, gnb, gcb = pl.pallas_call(
        finish,
        grid=(N,),
        out_shape=(
            jax.ShapeDtypeStruct((R, C), BF16),
            jax.ShapeDtypeStruct((R, C), F32),
            jax.ShapeDtypeStruct((D, C), F32),
            jax.ShapeDtypeStruct((2, D, C), F32),
            jax.ShapeDtypeStruct((1, C), F32),
            jax.ShapeDtypeStruct((1, C), F32),
        ),
        in_specs=[
            pl.BlockSpec(memory_space=pl.ANY),
            pl.BlockSpec((1, C, U), lambda i: (i, 0, 0)),
            pl.BlockSpec((1, C, Q), lambda i: (0, 0, i)),
            pl.BlockSpec((2, C, Q), lambda i: (0, 0, i)),
            whole,
            whole,
        ],
        out_specs=[
            pl.BlockSpec(memory_space=pl.ANY),
            pl.BlockSpec((U, C), lambda i: (i, 0)),
            pl.BlockSpec((Q, C), lambda i: (i, 0)),
            pl.BlockSpec((2, Q, C), lambda i: (0, i, 0)),
            line,
            line,
        ],
        input_output_aliases={0: 0},
        compiler_params=pltpu.CompilerParams(vmem_limit_bytes=16 * 2**20),
        name="finish",
    )(emb, gf, gn, gc, gnb, gcb)
    return emb, grad_features, grad_neigh, gnb.reshape(C), grad_combine.reshape(2 * D, C), gcb.reshape(C)


def solution(mesh):
    placed = (
        P("wide", None),
        P(None, "narrow"),
        P("narrow"),
        P(None, "narrow"),
        P("narrow"),
        P("wide", "narrow"),
        P("wide", None),
        P("wide", None),
        P("wide", None),
        P("wide", None),
    )
    return jax.shard_map(
        functools.partial(shards, mesh.shape["wide"], mesh.shape["narrow"]),
        mesh=mesh,
        in_specs=placed,
        out_specs=(
            P("wide", "narrow"),
            P("wide", "narrow"),
            P(None, "narrow"),
            P("narrow"),
            P(None, "narrow"),
            P("narrow"),
        ),
        check_vma=False,
    )
```

```python
import functools

import jax
import jax.numpy as jnp
from jax import lax
from jax.experimental import pallas as pl
from jax.experimental.pallas import tpu as pltpu
from jax.sharding import PartitionSpec as P

EPSILON = 1e-06
F32 = jnp.float32
BF16 = jnp.bfloat16
I32 = jnp.int32
I16 = jnp.int16
MESH = pl.DeviceIdType.MESH


def mm(left, right):
    return jnp.dot(left, right, preferred_element_type=F32)


def mm_nt(left, right):
    return lax.dot_general(left, right, (((1,), (1,)), ((), ())), preferred_element_type=F32)


def at(index, size):
    if isinstance(index, int):
        return slice(index * size, (index + 1) * size)
    return pl.ds(pl.multiple_of(index * size, size), size)


class Sizes:
    def __init__(self, feats, neigh, send, slot, wide, narrow):
        self.rows, self.width = feats.shape
        self.cols = neigh.shape[1]
        self.cap = send.shape[1]
        self.slots = slot.shape[0]
        self.wide, self.narrow = wide, narrow
        self.chunk = min(256, self.rows)
        self.part = self.rows // narrow
        self.local = self.rows // self.cap
        self.blocks = self.local + wide
        self.pairs = wide // 2
        self.red_rows = max(16, self.cols // 2 // self.pairs)
        self.red_down = self.cols // 2 // self.red_rows
        self.red_across = self.pairs // self.red_down
        self.red_lanes = self.width // self.red_across


NAMES_IN = ["feats_in", "nw_in", "nb_in", "comb_in", "cb_in", "cot_in", "slot_in", "mask_in", "visit_in", "send_in"]
NAMES_OUT = ["emb_out", "gf_out", "gn_out", "gc_out", "gnb_out", "gcb_out"]


def scratch(z):
    R, D, C, W, N, U, CAP = z.rows, z.width, z.cols, z.wide, z.narrow, z.part, z.cap
    v = lambda *shape: pltpu.VMEM(shape[:-1], shape[-1])
    bufs = dict(
        feats=v(R, D, BF16),
        nwfull=v(N, D, C, BF16),
        nbfull=v(N, 8, C, F32),
        wfull=v(N, 2 * D, C, BF16),
        cot=v(R, C, BF16),
        slot=v(z.slots, R, I32),
        mask=v(z.slots, R, I32),
        visit=v(z.slots, R, I32),
        send=v(W, CAP, I32),
        send_t=v(CAP, W, I32),
        code=v(R, 128, I32),
        wts=v(R, 128, F32),
        counts=v(z.blocks, R, CAP, BF16),
        sel=v(W, CAP, R, BF16),
        msg=v(R, D, BF16),
        zacc=v(R, C, F32),
        zhi=v(R, C, BF16),
        zlo=v(R, C, BF16),
        zqa=v(R, C, BF16),
        zqb=v(R, C, BF16),
        zscale=v(8, C, F32),
        zscales=v(W, 8, C, F32),
        zsend=v(W, CAP, C, I16),
        ztab=v(W, CAP, C, I16),
        acc=v(R, C, F32),
        self_t=v(C, R, F32),
        cot_t=v(C, R, F32),
        invs=v(16, R, F32),
        stat=v(8, R, F32),
        stats=v(N, 8, R, F32),
        emb=v(R, C, BF16),
        gp=v(C, R, BF16),
        gps=v(C, R, BF16),
        gprows=v(N, C, U, BF16),
        gsend=v(W, C, CAP, BF16),
        gret=v(W, C, CAP, BF16),
        yacc=v(C, R, F32),
        y=v(C, R, BF16),
        yrows=v(N, C, U, BF16),
        msg_t=v(D, U, BF16),
        gh=v(D, U, BF16),
        ghc=v(N, C, U, BF16),
        gf=v(D, U, F32),
        gfb=v(D, U, BF16),
        gfc=v(N, C, U, BF16),
        gc=v(2, C, D, BF16),
        gc_half=v(2, C // 2, D, BF16),
        gc_in=v(W // 2, 2, z.red_rows, z.red_lanes, BF16),
        gc_sum=v(2, C, D, BF16),
        gn=v(1, C, D, BF16),
        gn_half=v(1, C // 2, D, BF16),
        gn_in=v(W // 2, 1, z.red_rows, z.red_lanes, BF16),
        gn_sum=v(1, C, D, BF16),
        gcb=v(8, C, F32),
        gcb_in=v(W, 8, C, F32),
        gnb=v(8, C, F32),
        gnb_in=v(W, 8, C, F32),
    )
    sems = {}
    for name, count in dict(
        nw=N, nwp=(N, W // 2), nwf=N, nb=N, wt=(2, N), wtp=(2, N), wtf=(2, N), st=N, gp_n=N, y_n=(2, N), gh_n=N, gf_n=N,
        z_w=W, zs_w=W, gr_w=(2, W), hsc=1, rsc=W // 2, agc=W // 2, fwc=W // 2, hsn=1, rsn=W // 2, agn=W // 2, fwn=W // 2, bc=W, bn=W,
    ).items():
        sems[name + "_s"] = pltpu.SemaphoreType.DMA(count if isinstance(count, tuple) else (count,))
        sems[name + "_r"] = pltpu.SemaphoreType.DMA(count if isinstance(count, tuple) else (count,))
    sems["load"] = pltpu.SemaphoreType.DMA((10,))
    sems["store"] = pltpu.SemaphoreType.DMA((6,))
    return bufs, sems


class Refs:
    pass


def kernel(z, names, *refs):
    g = Refs()
    for name, ref in zip(names, refs):
        setattr(g, name, ref)
    R, D, C, W, N, U, CAP = z.rows, z.width, z.cols, z.wide, z.narrow, z.part, z.cap
    CH = z.chunk
    half = D // 2
    me_w, me_n = lax.axis_index("wide"), lax.axis_index("narrow")
    core = lax.rem(me_w, 2)
    sibling = me_w + 1 - 2 * core

    def loop(count, body, start=0):
        def step(i, carry):
            body(i)
            return carry

        lax.fori_loop(start, count, step, 0)

    def sweep(count, body):
        for i in range(count):
            body(i)

    def ahead_n(d):
        return lax.rem(me_n + d, N)

    def behind_n(d):
        return lax.rem(me_n - d + N, N)

    def ahead_w(d):
        return lax.rem(me_w + d, W)

    def behind_w(d):
        return lax.rem(me_w - d + W, W)

    def remote(name, index, src, dst, axis, peer):
        return pltpu.make_async_remote_copy(
            src_ref=src,
            dst_ref=dst,
            send_sem=getattr(g, name + "_s").at[index],
            recv_sem=getattr(g, name + "_r").at[index],
            device_id={axis: peer},
            device_id_type=MESH,
        )

    def share(w):
        return at(lax.rem(w, 2) * (W // 2) + w // 2, D // W)

    def nw_copy(d):
        mine = share(me_w)
        return remote("nw", d, g.nw_in.at[mine], g.nwfull.at[me_n, mine], "narrow", ahead_n(d))

    def nw_pass(d, e):
        part = g.nwfull.at[behind_n(d), share(me_w)]
        return remote("nwp", (d, e), part, part, "wide", ahead_w(2 * e))

    def nw_forward(d):
        part = g.nwfull.at[behind_n(d), at(core, half)]
        return remote("nwf", d, part, part, "wide", sibling)

    def nb_copy(d):
        return remote("nb", d, g.nbfull.at[me_n], g.nbfull.at[me_n], "narrow", ahead_n(d))

    step = (2, 4)

    def wt_bit(k):
        return lax.rem(me_w // step[k], 2)

    def wt_partner(k):
        return me_w + step[k] - 2 * step[k] * wt_bit(k)

    def wt_rows(k):
        return pl.ds(pl.multiple_of(k * D + (2 * core + wt_bit(k)) * (D // 4), D // 4), D // 4)

    def wt_copy(k, d):
        mine = wt_rows(k)
        return remote("wt", (k, d), g.comb_in.at[mine], g.wfull.at[me_n, mine], "narrow", ahead_n(d))

    def wt_pass(k, d):
        part = g.wfull.at[behind_n(d), wt_rows(k)]
        return remote("wtp", (k, d), part, part, "wide", wt_partner(k))

    def wt_forward(k, d):
        part = g.wfull.at[behind_n(d), pl.ds(pl.multiple_of(k * D + core * half, half), half)]
        return remote("wtf", (k, d), part, part, "wide", sibling)

    def z_copy(d):
        peer = ahead_w(d)
        return remote("z_w", d, g.zsend.at[peer], g.ztab.at[me_w], "wide", peer)

    def zscale_copy(d):
        return remote("zs_w", d, g.zscale, g.zscales.at[me_w], "wide", ahead_w(d))

    def stat_copy(d):
        return remote("st", d, g.stat, g.stats.at[me_n], "narrow", ahead_n(d))

    def gp_copy(d):
        s = ahead_n(d)
        return remote("gp_n", d, g.gp.at[:, at(s, U)], g.gprows.at[me_n], "narrow", s)

    def ret_copy(p, d):
        peer, rows = ahead_w(d), at(p, C // 2)
        return remote("gr_w", (p, d), g.gsend.at[peer, rows], g.gret.at[me_w, rows], "wide", peer)

    def y_copy(p, d):
        s, rows = ahead_n(d), at(p, C // 2)
        return remote("y_n", (p, d), g.y.at[rows, at(s, U)], g.yrows.at[me_n, rows], "narrow", s)

    def gh_copy(d):
        s = ahead_n(d)
        return remote("gh_n", d, g.gh.at[at(s, C)], g.ghc.at[me_n], "narrow", s)

    def gf_copy(d):
        s = ahead_n(d)
        return remote("gf_n", d, g.gfb.at[at(s, C)], g.gfc.at[me_n], "narrow", s)

    def red_block(w):
        q = w // 2
        row = lax.rem(w, 2) * (C // 2) + lax.rem(q, z.red_down) * z.red_rows
        return (slice(None), pl.ds(pl.multiple_of(row, z.red_rows), z.red_rows), at(q // z.red_down, z.red_lanes))

    def half_copy(k):
        src = getattr(g, "g" + k)
        return remote("hs" + k, 0, src.at[:, at(1 - core, C // 2)], getattr(g, "g" + k + "_half"), "wide", sibling)

    def rs_copy(k, e):
        peer = ahead_w(2 * e)
        return remote("rs" + k, e, getattr(g, "g" + k).at[red_block(peer)], getattr(g, "g" + k + "_in").at[me_w // 2], "wide", peer)

    def ag_copy(k, e):
        part = getattr(g, "g" + k + "_sum").at[red_block(me_w)]
        return remote("ag" + k, e, part, part, "wide", ahead_w(2 * e))

    def ag_forward(k, e):
        part = getattr(g, "g" + k + "_sum").at[red_block(behind_w(2 * e))]
        return remote("fw" + k, e, part, part, "wide", sibling)

    def reduce_pair(k):
        own, other = getattr(g, "g" + k), getattr(g, "g" + k + "_half")
        half_copy(k).wait_recv()
        mine = (slice(None), at(core, C // 2))
        own[mine] = (own[mine].astype(F32) + other[...].astype(F32)).astype(BF16)
        loop(W // 2, lambda e: rs_copy(k, e).start(), 1)

    def reduce_sum(k):
        own, arrived, out = getattr(g, "g" + k), getattr(g, "g" + k + "_in"), getattr(g, "g" + k + "_sum")
        loop(W // 2, lambda e: rs_copy(k, e).wait_recv(), 1)
        mine = red_block(me_w)
        total = lax.fori_loop(
            1, W // 2, lambda e, t: t + arrived[behind_w(2 * e) // 2].astype(F32), own[mine].astype(F32)
        )
        out[mine] = total.astype(BF16)
        loop(W // 2, lambda e: ag_copy(k, e).start(), 1)
        ag_forward(k, 0).start()

    def gather_pass(k):
        def body(e):
            ag_copy(k, e).wait_recv()
            ag_forward(k, e).start()

        loop(W // 2, body, 1)

    def drain_reduce(k):
        half_copy(k).wait_send()

        def body(e):
            rs_copy(k, e).wait_send()
            ag_copy(k, e).wait_send()

        loop(W // 2, body, 1)
        loop(W // 2, lambda e: ag_forward(k, e).wait_send())

    def bias_copy(name, src, dst, d):
        return remote(name, d, src, dst.at[me_w], "wide", ahead_w(d))

    loads = [
        (g.feats_in, g.feats),
        (g.nw_in, g.nwfull.at[me_n]),
        (g.comb_in, g.wfull.at[me_n]),
        (g.slot_in, g.slot),
        (g.mask_in, g.mask),
        (g.visit_in, g.visit),
        (g.send_in, g.send),
        (g.cot_in, g.cot),
    ]

    def load(i):
        return pltpu.make_async_copy(loads[i][0], loads[i][1], g.load.at[i])

    barrier = pltpu.get_barrier_semaphore()
    loop(W, lambda d: pl.semaphore_signal(barrier, inc=1, device_id={"wide": ahead_w(d)}, device_id_type=MESH), 1)
    loop(N, lambda d: pl.semaphore_signal(barrier, inc=1, device_id={"narrow": ahead_n(d)}, device_id_type=MESH), 1)
    order = (6, 3, 4, 5, 0, 1, 2, 7)
    for i in order:
        load(i).start()
    load(6).wait()
    g.send_t[...] = g.send[...].T

    def select(d):
        r = ahead_w(d)
        which = lax.broadcasted_iota(I32, (CAP, W), 1)
        col = jnp.sum(jnp.where(which == r, g.send_t[...], 0), axis=1, keepdims=True)
        place_u = lax.broadcasted_iota(I32, (CAP, R), 1)
        g.sel[r] = jnp.where(place_u == col, 1.0, 0.0).astype(BF16)

    loop(W, select, 1)
    pl.semaphore_wait(barrier, W - 1 + N - 1)
    loop(N, lambda d: nw_copy(d).start(), 1)
    g.nbfull[me_n] = jnp.broadcast_to(g.nb_in[...].astype(F32).reshape(1, C), (8, C))
    loop(N, lambda d: nb_copy(d).start(), 1)

    for i in (3, 4, 5):
        load(i).wait()
    K = z.slots
    shift = CAP.bit_length() - 1

    def fill(i):
        rows = at(i, CH)
        g.code[rows, :] = jnp.zeros((CH, 128), I32)
        g.wts[rows, :] = jnp.zeros((CH, 128), F32)
        code = g.slot[:, rows].T
        g.code[rows, 0:K] = code
        g.code[rows, 64 : 64 + K] = code
        weight = (g.mask[:, rows] * g.visit[:, rows]).astype(F32).T
        g.wts[rows, 0:K] = weight
        g.wts[rows, 64 : 64 + K] = weight

    loop(R // CH, fill)

    lane = lax.broadcasted_iota(I32, (8, 128), 1)
    sub = lax.broadcasted_iota(I32, (8, 128), 0)
    half_lane = jnp.where(lane >= 64, 1, 0)
    place = [sub == 2 * j + half_lane for j in range(4)]
    place_b = [jnp.where(m, 1.0, 0.0) for m in place]
    place_b = [jnp.concatenate([m, m], axis=0).astype(BF16) for m in place_b]
    low_row = lax.broadcasted_iota(I32, (CAP, 128), 0).astype(F32).astype(BF16)

    def count_group(i):
        start = pl.multiple_of(i * 16, 16)
        outs = []
        for p in range(2):
            rows = pl.ds(pl.multiple_of(start + 8 * p, 8), 8)
            code, weight = g.code[rows, :], g.wts[rows, :]
            high, low = code >> shift, (code & (CAP - 1)).astype(F32)
            left = []
            for h in range(0, z.blocks, 2):
                pair = [jnp.where(high == h + q, weight, 0.0) for q in range(2)]
                pair = jnp.concatenate(pair, axis=0).astype(BF16)
                left.append(jnp.concatenate([pair * place_b[j] for j in range(4)], axis=1))
            left = jnp.concatenate(left, axis=0)
            right = []
            for j in range(4):
                row = jnp.sum(jnp.where(place[j], low, 0.0), axis=0, keepdims=True)
                row = jnp.broadcast_to(row.astype(BF16), (CAP, 128))
                right.append(jnp.where(low_row == row, jnp.ones((), BF16), jnp.zeros((), BF16)))
            outs.append(mm_nt(left, jnp.concatenate(right, axis=1)))
        for h in range(z.blocks):
            block = [out[h * 8 : h * 8 + 8] for out in outs]
            g.counts[h, pl.ds(start, 16), :] = jnp.concatenate(block, axis=0).astype(BF16)

    UNROLL = 4
    groups = R // 16 // UNROLL

    def count_groups(first, last):
        def body(i):
            for q in range(UNROLL):
                count_group(i * UNROLL + q)

        loop(last, body, first)

    def hidden(s):
        def body(i):
            rows = at(i, CH)
            value = mm(g.feats[rows, :], g.nwfull[s]) + g.nbfull[s, 0:1, :]
            value = jnp.maximum(value, 0.0)
            top = value.astype(BF16)
            rest = (value - top.astype(F32)).astype(BF16)
            g.msg[rows, at(s, C)] = top
            weight = g.wfull[me_n, pl.ds(pl.multiple_of(D + s * C, C), C), :]
            g.zacc[rows, :] += mm(top, weight) + mm(rest, weight)

        sweep(R // CH, body)

    def zero(i):
        g.zacc[at(i, CH), :] = jnp.zeros((CH, C), F32)

    loop(R // CH, zero)
    for i in (0, 1, 2):
        load(i).wait()
    hidden(me_n)
    fifth = groups // 16

    def share_pass(k, d):
        wt_copy(k, d).wait_recv()
        wt_pass(k, d).start()

    count_groups(0, 4 * fifth)
    def pass_nw(d):
        nw_copy(d).wait_recv()
        loop(W // 2, lambda e: nw_pass(d, e).start(), 1)

    loop(N, pass_nw, 1)
    for k in range(2):
        loop(N, lambda d: wt_copy(k, d).start(), 1)
    count_groups(4 * fifth, 8 * fifth)

    def forward_nw(d):
        loop(W // 2, lambda e: nw_pass(d, e).wait_recv(), 1)
        nw_forward(d).start()

    def take(d):
        nw_forward(d).wait_recv()
        nb_copy(d).wait_recv()
        hidden(behind_n(d))

    forward_nw(1)
    count_groups(8 * fifth, 11 * fifth)
    loop(N, forward_nw, 2)
    count_groups(11 * fifth, groups)
    take(1)
    loop(N, take, 2)

    def column_max(i, most):
        return jnp.maximum(most, jnp.max(jnp.abs(g.zacc[at(i, CH), :]), axis=0, keepdims=True))

    most = lax.fori_loop(0, R // CH, column_max, jnp.full((1, C), 1e-30, F32))
    scale = most * (1.0 / 32766.0)
    g.zscale[...] = jnp.broadcast_to(scale, (8, C))
    loop(W, lambda d: zscale_copy(d).start(), 1)
    inv_scale = 1.0 / scale

    def code_z(i):
        rows = at(i, CH)
        whole = jnp.round(g.zacc[rows, :] * inv_scale)
        high = jnp.floor(whole * (1.0 / 256.0))
        g.zqa[rows, :] = high.astype(BF16)
        g.zqb[rows, :] = (whole - high * 256.0).astype(BF16)

    loop(R // CH, code_z)

    def send_z(d):
        peer = ahead_w(d)
        picked = mm(g.sel[peer], g.zqa[...]) * 256.0 + mm(g.sel[peer], g.zqb[...])
        g.zsend[peer] = picked.astype(I32).astype(I16)
        z_copy(d).start()

    loop(W, send_z, 1)

    def split_z(i):
        rows = at(i, CH)
        value = g.zacc[rows, :]
        top = value.astype(BF16)
        g.zhi[rows, :] = top
        g.zlo[rows, :] = (value - top.astype(F32)).astype(BF16)

    loop(R // CH, split_z)
    load(7).wait()

    def own_part(i):
        rows = at(i, CH)
        value = mm(g.feats[rows, :], g.wfull[me_n, 0:D, :]) + g.cb_in[...].astype(F32).reshape(1, C)
        g.self_t[:, rows] = value.T
        g.cot_t[:, rows] = g.cot[rows, :].astype(F32).T
        total = jnp.zeros((CH, C), F32)
        for h in range(z.local):
            part = slice(h * CAP, (h + 1) * CAP)
            block = g.counts[h, rows, :]
            total += mm(block, g.zhi[part, :]) + mm(block, g.zlo[part, :])
        g.acc[rows, :] = total

    sweep(R // CH, own_part)
    ones = jnp.ones((16, 128), BF16)
    g.invs[...] = 2.0 / mm_nt(ones, g.wts[...].astype(BF16))

    def mine_t(i):
        cols = at(i, C)
        g.msg_t[cols, :] = g.msg[at(me_n, U), cols].astype(F32).T.astype(BF16)

    loop(D // C, mine_t)

    def take_z(d):
        s = behind_w(d)
        z_copy(d).wait_recv()
        value = g.ztab[s].astype(I32).astype(F32) * g.zscales[s, 0:1, :]
        top = value.astype(BF16)
        rest = (value - top.astype(F32)).astype(BF16)

        def body(i):
            rows = at(i, CH)
            block = g.counts[z.local + s, rows, :]
            g.acc[rows, :] += mm(block, top) + mm(block, rest)

        sweep(R // CH, body)

    loop(W, lambda d: zscale_copy(d).wait_recv(), 1)
    loop(W, take_z, 1)

    which8 = lax.broadcasted_iota(I32, (8, CH), 0)

    def activate(i):
        rows = at(i, CH)
        pre = g.acc[rows, :].T * g.invs[0:1, rows] + g.self_t[:, rows]
        g.self_t[:, rows] = pre
        act = jnp.maximum(pre, 0.0)
        squares = jnp.sum(act * act, axis=0, keepdims=True)
        inner = jnp.sum(act * g.cot_t[:, rows], axis=0, keepdims=True)
        g.stat[:, rows] = jnp.where(which8 == 0, squares, jnp.where(which8 == 1, inner, 0.0))

    for k in range(2):
        loop(N, functools.partial(share_pass, k), 1)
    loop(R // CH, activate)
    loop(N, lambda d: stat_copy(d).start(), 1)
    loop(N, lambda d: stat_copy(d).wait_recv(), 1)
    g.stats[me_n] = g.stat[...]

    def norms(rows):
        total = g.stats[0, :, rows]
        for s in range(1, N):
            total += g.stats[s, :, rows]
        return lax.rsqrt(total[0:1] / D + EPSILON), total[1:2]

    def grad_act(i):
        rows = at(i, CH)
        inv, inner = norms(rows)
        pre = g.self_t[:, rows]
        act = jnp.maximum(pre, 0.0)
        grad = g.cot_t[:, rows] * inv - act * (inner * (inv * inv * inv) / D)
        grad = jnp.where(pre > 0, grad, 0.0)
        g.gp[:, rows] = grad.astype(BF16)
        g.gps[:, rows] = (grad * g.invs[0:1, rows]).astype(BF16)

    loop(R // CH, grad_act)
    loop(N, lambda d: gp_copy(d).start(), 1)

    def send_ret(p, d):
        peer, rows = ahead_w(d), at(p, C // 2)
        g.gsend[peer, rows, :] = mm(g.gps[rows, :], g.counts[z.local + peer]).astype(BF16)
        ret_copy(p, d).start()

    for p in range(2):
        loop(W, functools.partial(send_ret, p), 1)

    join = max(1, 128 // CAP)
    for h in range(0, z.local, join):
        parts = [mm(g.gps[...], g.counts[h + q]) for q in range(join)]
        parts = jnp.concatenate(parts, axis=1) if join > 1 else parts[0]
        g.yacc[:, h * CAP : (h + join) * CAP] = parts

    def embed(i):
        rows = at(i, CH)
        inv, _ = norms(rows)
        value = jnp.maximum(g.self_t[:, rows], 0.0) * inv
        g.emb[rows, :] = value.T.astype(BF16)

    loop(R // CH, embed)
    emb_store = pltpu.make_async_copy(g.emb, g.emb_out, g.store.at[0])
    emb_store.start()

    def pass_weights(k, d):
        wt_pass(k, d).wait_recv()
        wt_forward(k, d).start()

    for k in range(2):
        loop(N, functools.partial(pass_weights, k), 1)

    LW = min(512, D)

    def grad_self(i):
        lanes = at(i, LW)
        g.gc[0, :, lanes] = mm(g.gp[...], g.feats[:, lanes]).astype(BF16)

    sweep(D // LW, grad_self)
    ones_r = jnp.ones((8, R), BF16)
    g.gcb[...] = mm_nt(ones_r, g.gp[...])

    g.gprows[me_n] = g.gp[:, at(me_n, U)]

    def take_ret(p, d):
        s, half_rows = behind_w(d), at(p, C // 2)
        ret_copy(p, d).wait_recv()

        def body(i):
            lanes = at(i, CH)
            g.yacc[half_rows, lanes] += mm(g.gret[s, half_rows, :], g.sel[s, :, lanes])

        sweep(R // CH, body)

    for p in range(2):
        loop(W, functools.partial(take_ret, p), 1)
        half_rows = at(p, C // 2)
        g.y[half_rows, :] = g.yacc[half_rows, :].astype(BF16)
        loop(N, lambda d: y_copy(p, d).start(), 1)
    g.yrows[me_n] = g.y[:, at(me_n, U)]

    def grad_pool(i):
        lanes = at(i, LW)
        g.gc[1, :, lanes] = mm(g.y[...], g.msg[:, lanes]).astype(BF16)

    sweep(D // LW, grad_pool)
    loop(W, lambda d: bias_copy("bc", g.gcb, g.gcb_in, d).start(), 1)
    half_copy("c").start()

    loop(N, lambda d: gp_copy(d).wait_recv(), 1)
    for k in range(2):
        loop(N, lambda d: wt_forward(k, d).wait_recv(), 1)

    def self_rows(i):
        rows = at(i, CH)
        total = jnp.zeros((CH, U), F32)
        for s in range(N):
            total += mm(g.wfull[s, rows, :], g.gprows[s])
        g.gf[rows, :] = total

    sweep(D // CH, self_rows)
    reduce_pair("c")
    for p in range(2):
        loop(N, lambda d: y_copy(p, d).wait_recv(), 1)

    def hidden_rows(i):
        rows = at(i, CH)
        wrows = slice(D + i * CH, D + (i + 1) * CH)
        total = jnp.zeros((CH, U), F32)
        for s in range(N):
            total += mm(g.wfull[s, wrows, :], g.yrows[s])
        g.gh[rows, :] = jnp.where(g.msg_t[rows, :] > 0, total, 0.0).astype(BF16)

    sweep(D // CH, hidden_rows)
    loop(N, lambda d: gh_copy(d).start(), 1)
    g.ghc[me_n] = g.gh[at(me_n, C), :]

    def feature_rows(i):
        rows = at(i, CH)
        total = g.gf[rows, :]
        for s in range(N):
            total += mm(g.nwfull[s, rows, :], g.gh[s * C : (s + 1) * C, :])
        g.gfb[rows, :] = total.astype(BF16)

    sweep(D // CH, feature_rows)
    g.gfc[me_n] = g.gfb[at(me_n, C), :]

    reduce_sum("c")

    loop(N, lambda d: gh_copy(d).wait_recv(), 1)
    loop(N, lambda d: gf_copy(d).start(), 1)

    def grad_neigh(i):
        lanes = at(i, LW)
        total = jnp.zeros((C, LW), F32)
        for s in range(N):
            total += mm(g.ghc[s], g.feats[s * U : (s + 1) * U, lanes])
        g.gn[0, :, lanes] = total.astype(BF16)

    sweep(D // LW, grad_neigh)
    total = jnp.zeros((8, C), F32)
    ones_u = jnp.ones((8, U), BF16)
    for s in range(N):
        total += mm_nt(ones_u, g.ghc[s])
    g.gnb[...] = total
    half_copy("n").start()
    loop(W, lambda d: bias_copy("bn", g.gnb, g.gnb_in, d).start(), 1)

    gather_pass("c")
    reduce_pair("n")
    reduce_sum("n")

    def bias_sum(name, own, arrived):
        loop(W, lambda d: bias_copy(name, own, arrived, d).wait_recv(), 1)
        loop(W, lambda d: bias_copy(name, own, arrived, d).wait_send(), 1)

        def body(d, total):
            return total + arrived[behind_w(d)]

        own[...] = lax.fori_loop(1, W, body, own[...])

    bias_sum("bc", g.gcb, g.gcb_in)
    bias_sum("bn", g.gnb, g.gnb_in)

    loop(N, lambda d: gf_copy(d).wait_recv(), 1)
    gf_store = pltpu.make_async_copy(g.gfc, g.gf_out, g.store.at[1])
    gf_store.start()

    loop(W // 2, lambda e: ag_forward("c", e).wait_recv())
    stores = [
        emb_store,
        gf_store,
        pltpu.make_async_copy(g.gc_sum, g.gc_out, g.store.at[2]),
        pltpu.make_async_copy(g.gcb, g.gcb_out, g.store.at[3]),
        pltpu.make_async_copy(g.gnb, g.gnb_out, g.store.at[4]),
        pltpu.make_async_copy(g.gn_sum, g.gn_out, g.store.at[5]),
    ]
    for store in stores[2:5]:
        store.start()
    gather_pass("n")
    loop(W // 2, lambda e: ag_forward("n", e).wait_recv())
    stores[5].start()

    def drain_n(d):
        loop(W // 2, lambda e: nw_pass(d, e).wait_send(), 1)
        for copy in (nw_copy, nw_forward, nb_copy, stat_copy, gp_copy, gh_copy, gf_copy):
            copy(d).wait_send()
        for k in range(2):
            wt_copy(k, d).wait_send()
            wt_pass(k, d).wait_send()
            wt_forward(k, d).wait_send()
        for p in range(2):
            y_copy(p, d).wait_send()

    def drain_w(d):
        z_copy(d).wait_send()
        zscale_copy(d).wait_send()
        for p in range(2):
            ret_copy(p, d).wait_send()

    loop(N, drain_n, 1)
    loop(W, drain_w, 1)
    drain_reduce("c")
    drain_reduce("n")
    for store in stores:
        store.wait()


def finish(emb_in, gf, gn, gc, gnb, gcb, emb_out, gf_out, gn_out, gc_out, gnb_out, gcb_out):
    emb_out[...] = emb_in[...]
    gf_out[...] = gf[0].astype(F32).T
    gn_out[...] = gn[0].astype(F32).T
    for i in range(2):
        gc_out[i] = gc[i].astype(F32).T
    gnb_out[...] = gnb[0:1, :]
    gcb_out[...] = gcb[0:1, :]


def shards(wide, narrow, node_feats, neigh_weight, neigh_bias, combine_weight, combine_bias, cotangent,
           neighbour_slot, neighbour_mask, visit_count, send_rows):
    z = Sizes(node_feats, neigh_weight, send_rows, neighbour_slot.T, wide, narrow)
    R, D, C, W, N, U = z.rows, z.width, z.cols, z.wide, z.narrow, z.part
    bufs, sems = scratch(z)
    names = NAMES_IN + NAMES_OUT + list(bufs) + list(sems)
    outs = (
        jax.ShapeDtypeStruct((R, C), BF16),
        jax.ShapeDtypeStruct((N, C, U), BF16),
        jax.ShapeDtypeStruct((1, C, D), BF16),
        jax.ShapeDtypeStruct((2, C, D), BF16),
        jax.ShapeDtypeStruct((8, C), F32),
        jax.ShapeDtypeStruct((8, C), F32),
    )
    emb, gf, gn, gc, gnb, gcb = pl.pallas_call(
        functools.partial(kernel, z, names),
        out_shape=outs,
        in_specs=[
            pl.BlockSpec(memory_space=pltpu.VMEM if name in ("nb_in", "cb_in") else pl.ANY) for name in NAMES_IN
        ],
        out_specs=[pl.BlockSpec(memory_space=pl.ANY)] * len(NAMES_OUT),
        scratch_shapes=list(bufs.values()) + list(sems.values()),
        compiler_params=pltpu.CompilerParams(
            collective_id=0, has_side_effects=True, vmem_limit_bytes=60 * 2**20
        ),
        cost_estimate=pl.CostEstimate(flops=2 * 10**10, bytes_accessed=2 * 10**7, transcendentals=0),
        name="layer",
    )(
        node_feats, neigh_weight, neigh_bias, combine_weight, combine_bias, cotangent,
        neighbour_slot.T, neighbour_mask.T, visit_count.T, send_rows,
    )
    Q = D // N
    whole = pl.BlockSpec((8, C), lambda i: (0, 0))
    line = pl.BlockSpec((1, C), lambda i: (0, 0))
    emb, grad_features, grad_neigh, grad_combine, gnb, gcb = pl.pallas_call(
        finish,
        grid=(N,),
        out_shape=(
            jax.ShapeDtypeStruct((R, C), BF16),
            jax.ShapeDtypeStruct((R, C), F32),
            jax.ShapeDtypeStruct((D, C), F32),
            jax.ShapeDtypeStruct((2, D, C), F32),
            jax.ShapeDtypeStruct((1, C), F32),
            jax.ShapeDtypeStruct((1, C), F32),
        ),
        in_specs=[
            pl.BlockSpec((U, C), lambda i: (i, 0)),
            pl.BlockSpec((1, C, U), lambda i: (i, 0, 0)),
            pl.BlockSpec((1, C, Q), lambda i: (0, 0, i)),
            pl.BlockSpec((2, C, Q), lambda i: (0, 0, i)),
            whole,
            whole,
        ],
        out_specs=[
            pl.BlockSpec((U, C), lambda i: (i, 0)),
            pl.BlockSpec((U, C), lambda i: (i, 0)),
            pl.BlockSpec((Q, C), lambda i: (i, 0)),
            pl.BlockSpec((2, Q, C), lambda i: (0, i, 0)),
            line,
            line,
        ],
        compiler_params=pltpu.CompilerParams(vmem_limit_bytes=60 * 2**20),
        name="finish",
    )(emb, gf, gn, gc, gnb, gcb)
    return emb, grad_features, grad_neigh, gnb.reshape(C), grad_combine.reshape(2 * D, C), gcb.reshape(C)


def solution(mesh):
    placed = (
        P("wide", None),
        P(None, "narrow"),
        P("narrow"),
        P(None, "narrow"),
        P("narrow"),
        P("wide", "narrow"),
        P("wide", None),
        P("wide", None),
        P("wide", None),
        P("wide", None),
    )
    return jax.shard_map(
        functools.partial(shards, mesh.shape["wide"], mesh.shape["narrow"]),
        mesh=mesh,
        in_specs=placed,
        out_specs=(
            P("wide", "narrow"),
            P("wide", "narrow"),
            P(None, "narrow"),
            P("narrow"),
            P(None, "narrow"),
            P("narrow"),
        ),
        check_vma=False,
    )
```

```python
import functools

import jax
import jax.numpy as jnp
from jax import lax
from jax.experimental import pallas as pl
from jax.experimental.pallas import tpu as pltpu
from jax.sharding import PartitionSpec as P

EPSILON = 1e-06
PARTS = 4
SUMS = ("c", "n0", "n1")
F32 = jnp.float32
BF16 = jnp.bfloat16
I32 = jnp.int32
I16 = jnp.int16
MESH = pl.DeviceIdType.MESH


def mm(left, right):
    return jnp.dot(left, right, preferred_element_type=F32)


def mm_nt(left, right):
    return lax.dot_general(left, right, (((1,), (1,)), ((), ())), preferred_element_type=F32)


def at(index, size):
    if isinstance(index, int):
        return slice(index * size, (index + 1) * size)
    return pl.ds(pl.multiple_of(index * size, size), size)


class Sizes:
    def __init__(self, feats, neigh, send, slot, wide, narrow):
        self.rows, self.width = feats.shape
        self.cols = neigh.shape[1]
        self.cap = send.shape[1]
        self.slots = slot.shape[0]
        self.wide, self.narrow = wide, narrow
        self.chunk = min(256, self.rows)
        self.part = self.rows // narrow
        self.local = self.rows // self.cap
        self.blocks = self.local + wide
        self.pairs = wide // 2

    def red(self, rows):
        size = max(16, rows // 2 // self.pairs)
        down = rows // 2 // size
        return size, down, self.width * down // self.pairs


NAMES_IN = ["feats_in", "nw_in", "nb_in", "comb_in", "cb_in", "cot_in", "slot_in", "mask_in", "visit_in", "send_in"]
NAMES_OUT = ["emb_out", "gf_out", "gn_out", "gc_out", "gnb_out", "gcb_out"]


def scratch(z):
    R, D, C, W, N, U, CAP = z.rows, z.width, z.cols, z.wide, z.narrow, z.part, z.cap
    v = lambda *shape: pltpu.VMEM(shape[:-1], shape[-1])
    bufs = dict(
        feats=v(R, D, BF16),
        nwfull=v(N, D, C, BF16),
        nbfull=v(N, 8, C, F32),
        nb=v(C, BF16),
        cb=v(C, BF16),
        wfull=v(N, 2 * D, C, BF16),
        cot=v(R, C, BF16),
        slot=v(z.slots, R, I32),
        mask=v(z.slots, R, I32),
        visit=v(z.slots, R, I32),
        send=v(W, CAP, I32),
        send_t=v(CAP, W, I32),
        code=v(R, 128, I32),
        wts=v(R, 128, F32),
        counts=v(z.blocks, R, CAP, BF16),
        sel=v(W, CAP, R, BF16),
        msg=v(R, D, BF16),
        zacc=v(R, C, F32),
        zhi=v(R, C, BF16),
        zlo=v(R, C, BF16),
        zqa=v(R, C, BF16),
        zqb=v(R, C, BF16),
        zscale=v(8, C, F32),
        thi=v(W, CAP, C, BF16),
        tlo=v(W, CAP, C, BF16),
        zscales=v(W, 8, C, F32),
        zsend=v(W, CAP, C, I16),
        ztab=v(W, CAP, C, I16),
        acc=v(R, C, F32),
        self_t=v(C, R, F32),
        cot_t=v(C, R, F32),
        invs=v(16, R, F32),
        stat=v(2 * (R // z.chunk), z.chunk, F32),
        stats=v(N, 2 * (R // z.chunk), z.chunk, F32),
        emb=v(R, C, BF16),
        gp=v(C, R, BF16),
        gps=v(C, R, BF16),
        gprows=v(N, C, U, BF16),
        gsend=v(W, C, CAP, BF16),
        gret=v(W, C, CAP, BF16),
        yacc=v(C, R, F32),
        y=v(C, R, BF16),
        yrows=v(N, C, U, BF16),
        msg_t=v(D, U, BF16),
        gh=v(D, U, BF16),
        ghc=v(N, C, U, BF16),
        gfb=v(D, U, BF16),
        gc=v(2, C, D, BF16),
        gc_half=v(2, C // 2, D, BF16),
        gc_in=v(W // 2, 2, z.red(C)[0], z.red(C)[2], BF16),
        gc_sum=v(2, C, D, BF16),
        gn0=v(1, C // 2, D, BF16),
        gn0_half=v(1, C // 4, D, BF16),
        gn0_in=v(W // 2, 1, z.red(C // 2)[0], z.red(C // 2)[2], BF16),
        gn0_sum=v(1, C // 2, D, BF16),
        gn1=v(1, C // 2, D, BF16),
        gn1_half=v(1, C // 4, D, BF16),
        gn1_in=v(W // 2, 1, z.red(C // 2)[0], z.red(C // 2)[2], BF16),
        gn1_sum=v(1, C // 2, D, BF16),
        gcb=v(8, C, F32),
        gcb_in=v(W, 8, C, F32),
        gnb=v(8, C, F32),
        gnb_in=v(W, 8, C, F32),
    )
    kinds = dict(
        sh0=N, sh1=N, sh2=N, sp0=N, sp1=N, sp2=N, sf0=N, sf1=1, sf2=1, nb=1, st=1, gp=1, y=1, gh=2, gf=1,
        z=W, zs=1, gr=PARTS, bc=1, bn=1,
    )
    for k in SUMS:
        kinds.update({"hs" + k: 1, "rs" + k: 1, "ag" + k: 1, "fw" + k: 1})
    sems = {name + "_r": pltpu.SemaphoreType.DMA((count,)) for name, count in kinds.items()}
    sems["sent"] = pltpu.SemaphoreType.DMA((len(kinds),))
    sems["load"] = pltpu.SemaphoreType.DMA((10,))
    sems["store"] = pltpu.SemaphoreType.DMA((7,))
    return bufs, sems, list(kinds)


class Refs:
    pass


def kernel(z, names, kinds, *refs):
    g = Refs()
    for name, ref in zip(names, refs):
        setattr(g, name, ref)
    R, D, C, W, N, U, CAP = z.rows, z.width, z.cols, z.wide, z.narrow, z.part, z.cap
    CH = z.chunk
    half = D // 2
    me_w, me_n = lax.axis_index("wide"), lax.axis_index("narrow")
    core = lax.rem(me_w, 2)
    sibling = me_w + 1 - 2 * core

    def loop(count, body, start=0):
        def step(i, carry):
            body(i)
            return carry

        lax.fori_loop(start, count, step, 0)

    def sweep(count, body):
        for i in range(count):
            body(i)

    def flip(me, e, size):
        peer, bit = 0, 1
        while bit < size:
            peer = peer + bit * lax.rem(me // bit + e // bit, 2)
            bit *= 2
        return peer

    def peer_n(d):
        return flip(me_n, N - d, N)

    def peer_w(d):
        return flip(me_w, W - d, W)

    def ahead_n(d):
        return lax.rem(me_n + d, N)

    def behind_n(d):
        return lax.rem(me_n - d + N, N)

    def across(e):
        return flip(me_w, e, W)

    def remote(name, index, src, dst, axis="narrow", peer=0):
        return pltpu.make_async_remote_copy(
            src_ref=src,
            dst_ref=dst,
            send_sem=g.sent.at[kinds.index(name)],
            recv_sem=getattr(g, name + "_r").at[index],
            device_id={axis: peer},
            device_id_type=MESH,
        )

    def arrived(name, index, ref):
        remote(name, index, ref, ref, "narrow", peer_n(1)).wait_recv()

    def left(name, ref):
        remote(name, 0, ref, ref, "narrow", peer_n(1)).wait_send()

    hops = (2, 4)
    first = (None, D, 0)
    eighth = D // 8

    def rows_at(start, size):
        return pl.ds(pl.multiple_of(start, size), size)

    def hop_bit(h):
        return lax.rem(me_w // hops[h], 2)

    def quarter(k, h):
        return rows_at(first[k] + h * half + (2 * core + hop_bit(h)) * eighth, eighth)

    def quarter_copy(k, d, h):
        mine = quarter(k, h)
        return remote("sh%d" % k, d, g.comb_in.at[mine], g.wfull.at[me_n, mine], "narrow", ahead_n(d))

    def quarter_send(k):
        def body(d):
            for h in range(2):
                quarter_copy(k, d, h).start()

        loop(N, body, 1)

    def quarter_pass(k, d):
        s = behind_n(d)
        arrived("sh%d" % k, d, g.wfull.at[s, 0 : 2 * eighth])
        for h in range(2):
            part = g.wfull.at[s, quarter(k, h)]
            remote("sp%d" % k, d, part, part, "wide", me_w + hops[h] - 2 * hops[h] * hop_bit(h)).start()

    def quarter_forward(k, d):
        s = behind_n(d)
        arrived("sp%d" % k, d, g.wfull.at[s, 0 : 2 * eighth])
        for h in range(2):
            part = g.wfull.at[s, rows_at(first[k] + h * half + 2 * core * eighth, 2 * eighth)]
            remote("sf%d" % k, 0, part, part, "wide", sibling).start()

    part_w = D // W

    def share():
        return rows_at((core * (W // 2) + me_w // 2) * part_w, part_w)

    def share_send(d):
        remote("sh0", d, g.nw_in.at[share()], g.nwfull.at[me_n, share()], "narrow", ahead_n(d)).start()

    def share_pass(d):
        part = g.nwfull.at[behind_n(d), share()]
        arrived("sh0", d, part)
        loop(W // 2, lambda e: remote("sp0", d, part, part, "wide", across(2 * e)).start(), 1)

    def share_forward(d):
        s = behind_n(d)
        arrived("sp0", d, g.nwfull.at[s, 0 : (W // 2 - 1) * part_w])
        part = g.nwfull.at[s, rows_at(core * half, half)]
        remote("sf0", d, part, part, "wide", sibling).start()

    def nb_copy(d):
        return remote("nb", 0, g.nbfull.at[me_n], g.nbfull.at[me_n], "narrow", peer_n(d))

    def z_copy(d):
        peer = peer_w(d)
        return remote("z", d, g.zsend.at[peer], g.ztab.at[me_w], "wide", peer)

    def zscale_copy(d):
        return remote("zs", 0, g.zscale, g.zscales.at[me_w], "wide", peer_w(d))

    def stat_copy(d):
        return remote("st", 0, g.stat, g.stats.at[me_n], "narrow", peer_n(d))

    def gp_copy(d):
        s = peer_n(d)
        return remote("gp", 0, g.gp.at[:, at(s, U)], g.gprows.at[me_n], "narrow", s)

    def ret_copy(p, d):
        peer, rows = peer_w(d), at(p, C // PARTS)
        return remote("gr", p, g.gsend.at[peer, rows], g.gret.at[me_w, rows], "wide", peer)

    def y_copy(p, d):
        s, rows = peer_n(d), at(p, C // PARTS)
        return remote("y", 0, g.y.at[rows, at(s, U)], g.yrows.at[me_n, rows], "narrow", s)

    def gh_copy(q, d):
        s = peer_n(d)
        return remote("gh", q, g.gh.at[rows_at(s * C + q * (C // 2), C // 2)], g.ghc.at[me_n, at(q, C // 2)], "narrow", s)

    def gf_copy(d):
        s = peer_n(d)
        return remote("gf", 0, g.gfb.at[at(s, C)], g.gf_out.at[me_n], "narrow", s)

    def bias_copy(name, src, dst, d):
        return remote(name, 0, src, dst.at[me_w], "wide", peer_w(d))

    def grad(k, suffix=""):
        return getattr(g, "g" + k + suffix)

    def core_rows(k, which):
        return (slice(None), at(which, grad(k).shape[1] // 2))

    def red_block(k, w):
        rows = grad(k).shape[1]
        size, down, lanes = z.red(rows)
        q = w // 2
        row = lax.rem(w, 2) * (rows // 2) + lax.rem(q, down) * size
        return (slice(None), rows_at(row, size), at(q // down, lanes))

    def out_rows(k, which):
        rows = grad(k).shape[1]
        if k == "c":
            return g.gc_out.at[:, at(which, rows // 2)]
        return g.gn_out.at[:, rows_at(int(k[1]) * rows + which * (rows // 2), rows // 2)]

    def pair_start(k):
        remote("hs" + k, 0, grad(k).at[core_rows(k, 1 - core)], grad(k, "_half"), "wide", sibling).start()

    def reduce_pair(k):
        arrived("hs" + k, 0, grad(k, "_half"))
        own, mine = grad(k), core_rows(k, core)
        own[mine] = (own[mine].astype(F32) + grad(k, "_half")[...].astype(F32)).astype(BF16)

        def body(e):
            peer = across(2 * e)
            remote("rs" + k, 0, own.at[red_block(k, peer)], grad(k, "_in").at[me_w // 2], "wide", peer).start()

        loop(W // 2, body, 1)

    def reduce_sum(k):
        others = grad(k, "_in")
        arrived("rs" + k, 0, others.at[0 : W // 2 - 1])
        mine = red_block(k, me_w)
        total = lax.fori_loop(
            1, W // 2, lambda e, t: t + others[across(2 * e) // 2].astype(F32), grad(k)[mine].astype(F32), unroll=W <= 8
        )
        grad(k, "_sum")[mine] = total.astype(BF16)
        part = grad(k, "_sum").at[mine]
        loop(W // 2, lambda e: remote("ag" + k, 0, part, part, "wide", across(2 * e)).start(), 1)

    def gather_pass(k):
        arrived("ag" + k, 0, grad(k, "_in").at[0 : W // 2 - 1])
        part = grad(k, "_sum").at[core_rows(k, core)]
        remote("fw" + k, 0, part, out_rows(k, core), "wide", sibling).start()
        store = pltpu.make_async_copy(part, out_rows(k, core), g.store.at[SUMS.index(k)])
        store.start()
        return store

    def gather_wait(k):
        arrived("fw" + k, 0, out_rows(k, 1 - core))

    loads = [
        (g.feats_in, g.feats),
        (g.nw_in, g.nwfull.at[me_n]),
        (g.comb_in, g.wfull.at[me_n]),
        (g.slot_in, g.slot),
        (g.mask_in, g.mask),
        (g.visit_in, g.visit),
        (g.send_in, g.send),
        (g.cot_in, g.cot),
        (g.nb_in, g.nb),
        (g.cb_in, g.cb),
    ]

    def load(i):
        return pltpu.make_async_copy(loads[i][0], loads[i][1], g.load.at[i])

    barrier = pltpu.get_barrier_semaphore()
    loop(W, lambda d: pl.semaphore_signal(barrier, inc=1, device_id={"wide": peer_w(d)}, device_id_type=MESH), 1)
    loop(N, lambda d: pl.semaphore_signal(barrier, inc=1, device_id={"narrow": peer_n(d)}, device_id_type=MESH), 1)
    order = (6, 8, 3, 4, 5, 0, 1, 2, 7, 9)
    for i in order:
        load(i).start()
    load(6).wait()
    g.send_t[...] = g.send[...].T

    def select(d):
        r = peer_w(d)
        which = lax.broadcasted_iota(I32, (CAP, W), 1)
        col = jnp.sum(jnp.where(which == r, g.send_t[...], 0), axis=1, keepdims=True)
        place_u = lax.broadcasted_iota(I32, (CAP, R), 1)
        g.sel[r] = jnp.where(place_u == col, 1.0, 0.0).astype(BF16)

    loop(W, select, 1)
    pl.semaphore_wait(barrier, W - 1 + N - 1)
    loop(N, share_send, 1)
    load(8).wait()
    g.nbfull[me_n] = jnp.broadcast_to(g.nb[...].astype(F32).reshape(1, C), (8, C))
    loop(N, lambda d: nb_copy(d).start(), 1)

    for i in (3, 4, 5):
        load(i).wait()
    K = z.slots
    shift = CAP.bit_length() - 1

    def fill(i):
        rows = at(i, CH)
        g.code[rows, :] = jnp.zeros((CH, 128), I32)
        g.wts[rows, :] = jnp.zeros((CH, 128), F32)
        code = g.slot[:, rows].T
        g.code[rows, 0:K] = code
        g.code[rows, 64 : 64 + K] = code
        weight = (g.mask[:, rows] * g.visit[:, rows]).astype(F32).T
        g.wts[rows, 0:K] = weight
        g.wts[rows, 64 : 64 + K] = weight

    loop(R // CH, fill)

    lane = lax.broadcasted_iota(I32, (8, 128), 1)
    sub = lax.broadcasted_iota(I32, (8, 128), 0)
    half_lane = jnp.where(lane >= 64, 1, 0)
    place = [sub == 2 * j + half_lane for j in range(4)]
    place_b = [jnp.where(m, 1.0, 0.0) for m in place]
    place_b = [jnp.concatenate([m, m], axis=0).astype(BF16) for m in place_b]
    low_row = lax.broadcasted_iota(I32, (CAP, 128), 0).astype(F32).astype(BF16)

    def count_group(i):
        start = pl.multiple_of(i * 16, 16)
        outs = []
        for p in range(2):
            rows = pl.ds(pl.multiple_of(start + 8 * p, 8), 8)
            code, weight = g.code[rows, :], g.wts[rows, :]
            high, low = code >> shift, (code & (CAP - 1)).astype(F32)
            left = []
            for h in range(0, z.blocks, 2):
                pair = [jnp.where(high == h + q, weight, 0.0) for q in range(2)]
                pair = jnp.concatenate(pair, axis=0).astype(BF16)
                left.append(jnp.concatenate([pair * place_b[j] for j in range(4)], axis=1))
            left = jnp.concatenate(left, axis=0)
            right = []
            for j in range(4):
                row = jnp.sum(jnp.where(place[j], low, 0.0), axis=0, keepdims=True)
                row = jnp.broadcast_to(row.astype(BF16), (CAP, 128))
                right.append(jnp.where(low_row == row, jnp.ones((), BF16), jnp.zeros((), BF16)))
            outs.append(mm_nt(left, jnp.concatenate(right, axis=1)))
        for h in range(z.blocks):
            block = [out[h * 8 : h * 8 + 8] for out in outs]
            g.counts[h, pl.ds(start, 16), :] = jnp.concatenate(block, axis=0).astype(BF16)

    UNROLL = 4
    groups = R // 16 // UNROLL

    def count_groups(first, last):
        def body(i):
            for q in range(UNROLL):
                count_group(i * UNROLL + q)

        loop(last, body, first)

    def hidden(s):
        def body(i):
            rows = at(i, CH)
            value = mm(g.feats[rows, :], g.nwfull[s]) + g.nbfull[s, 0:1, :]
            value = jnp.maximum(value, 0.0)
            top = value.astype(BF16)
            rest = (value - top.astype(F32)).astype(BF16)
            g.msg[rows, at(s, C)] = top
            weight = g.wfull[me_n, pl.ds(pl.multiple_of(D + s * C, C), C), :]
            g.zacc[rows, :] += mm(top, weight) + mm(rest, weight)

        sweep(R // CH, body)

    done = [0]

    def counts_until(last):
        last = groups * last // 16
        count_groups(done[0], last)
        done[0] = last

    def zero(i):
        g.zacc[at(i, CH), :] = jnp.zeros((CH, C), F32)

    loop(R // CH, zero)
    for i in (0, 1, 2):
        load(i).wait()
    hidden(me_n)
    counts_until(4)
    loop(N, share_pass, 1)
    quarter_send(1)
    counts_until(8)
    share_forward(1)

    def take(d):
        arrived("sf0", d, g.nwfull.at[0, 0:half])
        hidden(behind_n(d))

    share_forward(2)
    arrived("nb", 0, g.nbfull.at[0 : N - 1])
    take(1)
    loop(N, share_forward, 3)
    take(2)
    quarter_send(2)
    loop(N, take, 3)

    def column_max(i, most):
        return jnp.maximum(most, jnp.max(jnp.abs(g.zacc[at(i, CH), :]), axis=0, keepdims=True))

    most = lax.fori_loop(0, R // CH, column_max, jnp.full((1, C), 1e-30, F32))
    scale = most * (1.0 / 32766.0)
    g.zscale[...] = jnp.broadcast_to(scale, (8, C))
    loop(W, lambda d: zscale_copy(d).start(), 1)
    inv_scale = 1.0 / scale

    def code_z(i):
        rows = at(i, CH)
        whole = jnp.round(g.zacc[rows, :] * inv_scale)
        high = jnp.floor(whole * (1.0 / 256.0))
        g.zqa[rows, :] = high.astype(BF16)
        g.zqb[rows, :] = (whole - high * 256.0).astype(BF16)

    loop(R // CH, code_z)

    def send_z(d):
        peer = peer_w(d)
        picked = mm(g.sel[peer], g.zqa[...]) * 256.0 + mm(g.sel[peer], g.zqb[...])
        g.zsend[peer] = picked.astype(I32).astype(I16)
        z_copy(d).start()

    near = W // 4 + 1
    loop(near, send_z, 1)
    counts_until(10)
    loop(W, send_z, near)

    def split_z(i):
        rows = at(i, CH)
        value = g.zacc[rows, :]
        top = value.astype(BF16)
        g.zhi[rows, :] = top
        g.zlo[rows, :] = (value - top.astype(F32)).astype(BF16)

    loop(R // CH, split_z)
    counts_until(16)
    load(7).wait()
    load(9).wait()

    def own_part(i):
        rows = at(i, CH)
        value = mm(g.feats[rows, :], g.wfull[me_n, 0:D, :]) + g.cb[...].astype(F32).reshape(1, C)
        g.self_t[:, rows] = value.T
        g.cot_t[:, rows] = g.cot[rows, :].astype(F32).T
        total = jnp.zeros((CH, C), F32)
        for h in range(z.local):
            part = slice(h * CAP, (h + 1) * CAP)
            block = g.counts[h, rows, :]
            total += mm(block, g.zhi[part, :]) + mm(block, g.zlo[part, :])
        g.acc[rows, :] = total

    sweep(R // CH, own_part)
    ones = jnp.ones((16, 128), BF16)
    g.invs[...] = 2.0 / mm_nt(ones, g.wts[...].astype(BF16))

    def mine_t(i):
        cols = at(i, C)
        g.msg_t[cols, :] = g.msg[at(me_n, U), cols].astype(F32).T.astype(BF16)

    loop(D // C, mine_t)

    def take_z(d):
        s = peer_w(d)
        piece = min(32, CAP)
        for i in range(CAP // piece):
            rows = at(i, piece)
            value = g.ztab[s, rows, :].astype(I32).astype(F32) * g.zscales[s, 0:1, :]
            top = value.astype(BF16)
            g.thi[s, rows, :] = top
            g.tlo[s, rows, :] = (value - top.astype(F32)).astype(BF16)

    def pool(first, last):
        loop(last, take_z, first)

        def body(i):
            rows = at(i, CH)

            def add(d, total):
                s = peer_w(d)
                block = g.counts[z.local + s, rows, :]
                return total + mm(block, g.thi[s]) + mm(block, g.tlo[s])

            g.acc[rows, :] = lax.fori_loop(first, last, add, g.acc[rows, :], unroll=W <= 8)

        sweep(R // CH, body)

    arrived("zs", 0, g.zscales.at[0 : W - 1])
    loop(near, lambda d: z_copy(d).wait_recv(), 1)
    pool(1, near)
    loop(W, lambda d: z_copy(d).wait_recv(), near)
    for k in (1, 2):
        loop(N, functools.partial(quarter_pass, k), 1)
    pool(near, W)
    def activate(i):
        rows = at(i, CH)
        pre = g.acc[rows, :].T * g.invs[0:1, rows] + g.self_t[:, rows]
        g.self_t[:, rows] = pre
        act = jnp.maximum(pre, 0.0)
        squares = jnp.sum(act * act, axis=0, keepdims=True)
        inner = jnp.sum(act * g.cot_t[:, rows], axis=0, keepdims=True)
        g.stat[2 * i : 2 * i + 2, :] = jnp.concatenate([squares, inner], axis=0)

    sweep(R // CH, activate)
    loop(N, lambda d: stat_copy(d).start(), 1)
    arrived("st", 0, g.stats.at[0 : N - 1])
    g.stats[me_n] = g.stat[...]

    def norms(i):
        total = g.stats[0, 2 * i : 2 * i + 2, :]
        for s in range(1, N):
            total += g.stats[s, 2 * i : 2 * i + 2, :]
        return lax.rsqrt(total[0:1] / D + EPSILON), total[1:2]

    def grad_act(i):
        rows = at(i, CH)
        inv, inner = norms(i)
        pre = g.self_t[:, rows]
        act = jnp.maximum(pre, 0.0)
        grad = g.cot_t[:, rows] * inv - act * (inner * (inv * inv * inv) / D)
        grad = jnp.where(pre > 0, grad, 0.0)
        g.gp[:, rows] = grad.astype(BF16)
        g.gps[:, rows] = (grad * g.invs[0:1, rows]).astype(BF16)

    sweep(R // CH, grad_act)
    loop(N, lambda d: gp_copy(d).start(), 1)

    def send_ret(d):
        peer = peer_w(d)
        g.gsend[peer] = mm(g.gps[...], g.counts[z.local + peer]).astype(BF16)
        ret_copy(0, d).start()

    loop(W, send_ret, 1)

    def more_ret(p):
        loop(W, lambda d: ret_copy(p, d).start(), 1)

    more_ret(1)
    for k in (1, 2):
        loop(N, functools.partial(quarter_forward, k), 1)
    join = max(1, 128 // CAP)
    for h in range(0, z.local, join):
        parts = [mm(g.gps[...], g.counts[h + q]) for q in range(join)]
        parts = jnp.concatenate(parts, axis=1) if join > 1 else parts[0]
        g.yacc[:, h * CAP : (h + join) * CAP] = parts

    def embed(i):
        rows = at(i, CH)
        inv, _ = norms(i)
        value = jnp.maximum(g.self_t[:, rows], 0.0) * inv
        g.emb[rows, :] = value.T.astype(BF16)

    sweep(R // CH, embed)
    emb_store = pltpu.make_async_copy(g.emb, g.emb_out, g.store.at[4])
    emb_store.start()
    more_ret(2)

    LW = min(512, D)

    def grad_self(i):
        lanes = at(i, LW)
        g.gc[0, :, lanes] = mm(g.gp[...], g.feats[:, lanes]).astype(BF16)

    sweep(D // LW, grad_self)
    ones_r = jnp.ones((8, R), BF16)
    g.gcb[...] = mm_nt(ones_r, g.gp[...])

    g.gprows[me_n] = g.gp[:, at(me_n, U)]

    def take_ret(p):
        part = at(p, C // PARTS)
        arrived("gr", p, g.gret.at[0 : W - 1, part])

        def body(i):
            lanes = at(i, CH)

            def add(d, total):
                s = peer_w(d)
                return total + mm(g.gret[s, part, :], g.sel[s, :, lanes])

            total = lax.fori_loop(1, W, add, g.yacc[part, lanes], unroll=W <= 8)
            g.y[part, lanes] = total.astype(BF16)

        sweep(R // CH, body)
        loop(N, lambda d: y_copy(p, d).start(), 1)

    for p in range(PARTS):
        take_ret(p)
        if p + 3 < PARTS:
            more_ret(p + 3)
    g.yrows[me_n] = g.y[:, at(me_n, U)]

    def grad_pool(i):
        lanes = at(i, LW)
        g.gc[1, :, lanes] = mm(g.y[...], g.msg[:, lanes]).astype(BF16)

    sweep(D // LW, grad_pool)
    loop(W, lambda d: bias_copy("bc", g.gcb, g.gcb_in, d).start(), 1)
    pair_start("c")

    reduce_pair("c")
    arrived("sf1", 0, g.wfull.at[0 : N - 1, 0:half])
    arrived("y", 0, g.yrows.at[0 : N - 1])

    def hidden_rows(i):
        rows = at(i, CH)
        wrows = slice(D + i * CH, D + (i + 1) * CH)
        total = jnp.zeros((CH, U), F32)
        for s in range(N):
            total += mm(g.wfull[s, wrows, :], g.yrows[s])
        g.gh[rows, :] = jnp.where(g.msg_t[rows, :] > 0, total, 0.0).astype(BF16)

    sweep(D // CH, hidden_rows)
    loop(N, lambda d: gh_copy(0, d).start(), 1)
    g.ghc[me_n] = g.gh[at(me_n, C), :]

    def feature_rows(i):
        rows = at(i, CH)
        total = jnp.zeros((CH, U), F32)
        for s in range(N):
            total += mm(g.wfull[s, rows, :], g.gprows[s]) + mm(g.nwfull[s, rows, :], g.gh[s * C : (s + 1) * C, :])
        g.gfb[rows, :] = total.astype(BF16)

    arrived("gp", 0, g.gprows.at[0 : N - 1])
    arrived("sf2", 0, g.wfull.at[0 : N - 1, 0:half])
    sweep(D // CH, feature_rows)
    gf_store = pltpu.make_async_copy(g.gfb.at[at(me_n, C)], g.gf_out.at[me_n], g.store.at[3])
    gf_store.start()

    reduce_sum("c")

    def grad_neigh(q):
        rows = at(q, C // 2)
        out = (g.gn0, g.gn1)[q]

        def body(i):
            lanes = at(i, LW)
            total = jnp.zeros((C // 2, LW), F32)
            for s in range(N):
                total += mm(g.ghc[s, rows, :], g.feats[s * U : (s + 1) * U, lanes])
            out[0, :, lanes] = total.astype(BF16)

        sweep(D // LW, body)

    loop(N, lambda d: gh_copy(1, d).start(), 1)
    arrived("gh", 0, g.ghc.at[0 : N - 1, 0 : C // 2])
    grad_neigh(0)
    pair_start("n0")
    arrived("gh", 1, g.ghc.at[0 : N - 1, 0 : C // 2])
    loop(N, lambda d: gf_copy(d).start(), 1)
    reduce_pair("n0")
    grad_neigh(1)
    pair_start("n1")
    total = jnp.zeros((8, C), F32)
    ones_u = jnp.ones((8, U), BF16)
    for s in range(N):
        total += mm_nt(ones_u, g.ghc[s])
    g.gnb[...] = total
    loop(W, lambda d: bias_copy("bn", g.gnb, g.gnb_in, d).start(), 1)
    gc_store = gather_pass("c")
    reduce_pair("n1")
    reduce_sum("n0")
    def bias_sum(name, own, others):
        arrived(name, 0, others.at[0 : W - 1])
        left(name, others.at[0 : W - 1])
        own[...] = lax.fori_loop(1, W, lambda d, total: total + others[peer_w(d)], own[...])

    bias_sum("bc", g.gcb, g.gcb_in)
    bias_sum("bn", g.gnb, g.gnb_in)
    gcb_store = pltpu.make_async_copy(g.gcb, g.gcb_out, g.store.at[5])
    gnb_store = pltpu.make_async_copy(g.gnb, g.gnb_out, g.store.at[6])
    gcb_store.start()
    gnb_store.start()
    reduce_sum("n1")
    gn0_store = gather_pass("n0")
    gn1_store = gather_pass("n1")
    for k in SUMS:
        gather_wait(k)
    arrived("gf", 0, g.gf_out.at[0 : N - 1])

    left("sh0", g.nwfull.at[0 : N - 1, 0:part_w])
    left("sp0", g.nwfull.at[0 : N - 1, 0 : (W // 2 - 1) * part_w])
    left("sf0", g.nwfull.at[0 : N - 1, 0:half])
    for k in (1, 2):
        left("sh%d" % k, g.wfull.at[0 : N - 1, 0 : 2 * eighth])
        left("sp%d" % k, g.wfull.at[0 : N - 1, 0 : 2 * eighth])
        left("sf%d" % k, g.wfull.at[0 : N - 1, 0:half])
    left("nb", g.nbfull.at[0 : N - 1])
    left("z", g.zsend.at[0 : W - 1])
    left("zs", g.zscales.at[0 : W - 1])
    left("st", g.stats.at[0 : N - 1])
    left("gp", g.gprows.at[0 : N - 1])
    left("gr", g.gsend.at[0 : W - 1])
    left("y", g.yrows.at[0 : N - 1])
    left("gh", g.ghc.at[0 : N - 1])
    left("gf", g.gf_out.at[0 : N - 1])
    for k in SUMS:
        left("hs" + k, grad(k, "_half"))
        left("rs" + k, grad(k, "_in").at[0 : W // 2 - 1])
        left("ag" + k, grad(k, "_in").at[0 : W // 2 - 1])
        left("fw" + k, grad(k, "_sum").at[core_rows(k, core)])
    for store in (emb_store, gf_store, gc_store, gcb_store, gnb_store, gn0_store, gn1_store):
        store.wait()


def finish(z, *refs):
    names = ["emb", "gf", "gn", "gc", "gnb", "gcb"]
    ins = dict(zip(names, refs[:6]))
    outs = dict(zip(names, refs[6:12]))
    emb, gf, gn, gc, nb, cb, gf_t, gn_t, gc_t, nb_t, cb_t, load, store = refs[12:]
    D, C, N, U = z.width, z.cols, z.narrow, z.part
    step = D // N
    emb_load = pltpu.make_async_copy(ins["emb"], emb, load.at[4 * N + 2])
    emb_load.start()
    jobs = []
    for p in range(2):
        for i in range(N):
            lanes = slice(i * step, (i + 1) * step)
            jobs.append((ins["gc"].at[p, :, lanes], gc.at[p, :, lanes], gc_t.at[p, lanes], outs["gc"].at[p, lanes]))
    for i in range(N):
        lanes = slice(i * step, (i + 1) * step)
        jobs.append((ins["gn"].at[0, :, lanes], gn.at[:, lanes], gn_t.at[lanes], outs["gn"].at[lanes]))
    for i in range(N):
        rows = slice(i * U, (i + 1) * U)
        jobs.append((ins["gf"].at[i], gf.at[i], gf_t.at[rows], outs["gf"].at[rows]))
    loads = [pltpu.make_async_copy(src, held, load.at[i]) for i, (src, held, _, _) in enumerate(jobs)]
    loads += [pltpu.make_async_copy(ins[k], v, load.at[len(jobs) + i]) for i, (k, v) in enumerate((("gnb", nb), ("gcb", cb)))]
    for copy in loads:
        copy.start()
    stores = [pltpu.make_async_copy(emb, outs["emb"], store.at[0])]
    emb_load.wait()
    stores[0].start()
    for i, (_, held, turned, out) in enumerate(jobs):
        loads[i].wait()
        turned[...] = held[...].astype(F32).T
        stores.append(pltpu.make_async_copy(turned, out, store.at[1 + i]))
        stores[-1].start()
    for i, (k, v, t) in enumerate((("gnb", nb, nb_t), ("gcb", cb, cb_t))):
        loads[len(jobs) + i].wait()
        t[...] = v[0:1, :]
        stores.append(pltpu.make_async_copy(t, outs[k], store.at[1 + len(jobs) + i]))
        stores[-1].start()
    for copy in stores:
        copy.wait()


def shards(wide, narrow, node_feats, neigh_weight, neigh_bias, combine_weight, combine_bias, cotangent,
           neighbour_slot, neighbour_mask, visit_count, send_rows):
    z = Sizes(node_feats, neigh_weight, send_rows, neighbour_slot.T, wide, narrow)
    R, D, C, W, N, U = z.rows, z.width, z.cols, z.wide, z.narrow, z.part
    bufs, sems, kinds = scratch(z)
    names = NAMES_IN + NAMES_OUT + list(bufs) + list(sems)
    outs = (
        jax.ShapeDtypeStruct((R, C), BF16),
        jax.ShapeDtypeStruct((N, C, U), BF16),
        jax.ShapeDtypeStruct((1, C, D), BF16),
        jax.ShapeDtypeStruct((2, C, D), BF16),
        jax.ShapeDtypeStruct((8, C), F32),
        jax.ShapeDtypeStruct((8, C), F32),
    )
    emb, gf, gn, gc, gnb, gcb = pl.pallas_call(
        functools.partial(kernel, z, names, kinds),
        out_shape=outs,
        in_specs=[pl.BlockSpec(memory_space=pl.ANY)] * len(NAMES_IN),
        out_specs=[pl.BlockSpec(memory_space=pl.ANY)] * len(NAMES_OUT),
        scratch_shapes=list(bufs.values()) + list(sems.values()),
        compiler_params=pltpu.CompilerParams(
            collective_id=0, has_side_effects=True, vmem_limit_bytes=60 * 2**20
        ),
        cost_estimate=pl.CostEstimate(flops=2 * 10**10, bytes_accessed=2 * 10**7, transcendentals=0),
        name="layer",
    )(
        node_feats, neigh_weight, neigh_bias, combine_weight, combine_bias, cotangent,
        neighbour_slot.T, neighbour_mask.T, visit_count.T, send_rows,
    )
    hbm = pl.BlockSpec(memory_space=pl.ANY)
    emb, grad_features, grad_neigh, grad_combine, gnb, gcb = pl.pallas_call(
        functools.partial(finish, z),
        out_shape=(
            jax.ShapeDtypeStruct((R, C), BF16),
            jax.ShapeDtypeStruct((R, C), F32),
            jax.ShapeDtypeStruct((D, C), F32),
            jax.ShapeDtypeStruct((2, D, C), F32),
            jax.ShapeDtypeStruct((1, C), F32),
            jax.ShapeDtypeStruct((1, C), F32),
        ),
        in_specs=[hbm] * 6,
        out_specs=[hbm] * 6,
        scratch_shapes=[
            pltpu.VMEM((R, C), BF16),
            pltpu.VMEM((N, C, U), BF16),
            pltpu.VMEM((C, D), BF16),
            pltpu.VMEM((2, C, D), BF16),
            pltpu.VMEM((8, C), F32),
            pltpu.VMEM((8, C), F32),
            pltpu.VMEM((R, C), F32),
            pltpu.VMEM((D, C), F32),
            pltpu.VMEM((2, D, C), F32),
            pltpu.VMEM((1, C), F32),
            pltpu.VMEM((1, C), F32),
            pltpu.SemaphoreType.DMA((4 * N + 3,)),
            pltpu.SemaphoreType.DMA((4 * N + 3,)),
        ],
        compiler_params=pltpu.CompilerParams(vmem_limit_bytes=60 * 2**20),
        name="finish",
    )(emb, gf, gn, gc, gnb, gcb)
    return emb, grad_features, grad_neigh, gnb.reshape(C), grad_combine.reshape(2 * D, C), gcb.reshape(C)


def solution(mesh):
    placed = (
        P("wide", None),
        P(None, "narrow"),
        P("narrow"),
        P(None, "narrow"),
        P("narrow"),
        P("wide", "narrow"),
        P("wide", None),
        P("wide", None),
        P("wide", None),
        P("wide", None),
    )
    return jax.shard_map(
        functools.partial(shards, mesh.shape["wide"], mesh.shape["narrow"]),
        mesh=mesh,
        in_specs=placed,
        out_specs=(
            P("wide", "narrow"),
            P("wide", "narrow"),
            P(None, "narrow"),
            P("narrow"),
            P(None, "narrow"),
            P("narrow"),
        ),
        check_vma=False,
    )
```

```python
import functools

import jax
import jax.numpy as jnp
from jax import lax
from jax.experimental import pallas as pl
from jax.experimental.pallas import tpu as pltpu
from jax.sharding import PartitionSpec as P

EPSILON = 1e-06
PARTS = 4
SUMS = ("c", "n0", "n1")
F32 = jnp.float32
BF16 = jnp.bfloat16
I32 = jnp.int32
I16 = jnp.int16
MESH = pl.DeviceIdType.MESH


def mm(left, right):
    return jnp.dot(left, right, preferred_element_type=F32)


def mm_nt(left, right):
    return lax.dot_general(left, right, (((1,), (1,)), ((), ())), preferred_element_type=F32)


def at(index, size):
    if isinstance(index, int):
        return slice(index * size, (index + 1) * size)
    return pl.ds(pl.multiple_of(index * size, size), size)


class Sizes:
    def __init__(self, feats, neigh, send, slot, wide, narrow):
        self.rows, self.width = feats.shape
        self.cols = neigh.shape[1]
        self.cap = send.shape[1]
        self.slots = slot.shape[0]
        self.wide, self.narrow = wide, narrow
        self.chunk = min(256, self.rows)
        self.part = self.rows // narrow
        self.local = self.rows // self.cap
        self.blocks = self.local + wide
        self.pairs = wide // 2

    def red(self, rows):
        size = max(16, rows // 2 // self.pairs)
        down = rows // 2 // size
        return size, down, self.width * down // self.pairs


NAMES_IN = ["feats_in", "nw_in", "nb_in", "comb_in", "cb_in", "cot_in", "slot_in", "mask_in", "visit_in", "send_in"]
NAMES_OUT = ["emb_out", "gf_out", "gn_out", "gc_out", "gnb_out", "gcb_out"]


def scratch(z):
    R, D, C, W, N, U, CAP = z.rows, z.width, z.cols, z.wide, z.narrow, z.part, z.cap
    v = lambda *shape: pltpu.VMEM(shape[:-1], shape[-1])
    bufs = dict(
        feats=v(R, D, BF16),
        nwfull=v(N, D, C, BF16),
        nbfull=v(N, 8, C, F32),
        nb=v(C, BF16),
        cb=v(C, BF16),
        wfull=v(N, 2 * D, C, BF16),
        cot=v(R, C, BF16),
        slot=v(z.slots, R, I32),
        mask=v(z.slots, R, I32),
        visit=v(z.slots, R, I32),
        send=v(W, CAP, I32),
        send_t=v(CAP, W, I32),
        code=v(R, 128, I32),
        wts=v(R, 128, F32),
        counts=v(z.blocks, R, CAP, BF16),
        sel=v(W, CAP, R, BF16),
        msg=v(R, D, BF16),
        zacc=v(R, C, F32),
        zhi=v(R, C, BF16),
        zlo=v(R, C, BF16),
        zqa=v(R, C, BF16),
        zqb=v(R, C, BF16),
        zscale=v(8, C, F32),
        thi=v(W, CAP, C, BF16),
        tlo=v(W, CAP, C, BF16),
        zscales=v(W, 8, C, F32),
        zsend=v(W, CAP, C, I16),
        ztab=v(W, CAP, C, I16),
        acc=v(R, C, F32),
        self_t=v(C, R, F32),
        cot_t=v(C, R, F32),
        invs=v(16, R, F32),
        stat=v(2 * (R // z.chunk), z.chunk, F32),
        stats=v(N, 2 * (R // z.chunk), z.chunk, F32),
        emb=v(R, C, BF16),
        gp=v(C, R, BF16),
        gps=v(C, R, BF16),
        act=v(C, R, BF16),
        actrows=v(N, C, U, BF16),
        cotrows=v(N, U, C, BF16),
        cotrows_t=v(N, C, U, F32),
        gprows=v(N, C, U, BF16),
        gsend=v(W, C, CAP, BF16),
        gret=v(W, C, CAP, BF16),
        yacc=v(C, R, F32),
        y=v(C, R, BF16),
        yrows=v(N, C, U, BF16),
        msg_t=v(D, U, BF16),
        gh=v(D, U, BF16),
        ghc=v(N, C, U, BF16),
        gft=v(N, U, C, BF16),
        gct=v(2, D, C, BF16),
        gc=v(2, C, D, BF16),
        gc_half=v(2, C // 2, D, BF16),
        gc_in=v(W // 2, 2, z.red(C)[0], z.red(C)[2], BF16),
        gc_sum=v(2, C, D, BF16),
        gn0=v(1, C // 2, D, BF16),
        gn0_half=v(1, C // 4, D, BF16),
        gn0_in=v(W // 2, 1, z.red(C // 2)[0], z.red(C // 2)[2], BF16),
        gn0_sum=v(1, C // 2, D, BF16),
        gn1=v(1, C // 2, D, BF16),
        gn1_half=v(1, C // 4, D, BF16),
        gn1_in=v(W // 2, 1, z.red(C // 2)[0], z.red(C // 2)[2], BF16),
        gn1_sum=v(1, C // 2, D, BF16),
        gcb=v(8, C, F32),
        gcb_in=v(W, 8, C, F32),
        gnb=v(8, C, F32),
        gnb_in=v(W, 8, C, F32),
    )
    kinds = dict(
        sh0=N, sh1=N, sh2=N, sp0=N, sp1=N, sp2=N, sf0=N, sf1=1, sf2=1, nb=1, st=1, ct=1, ac=1, y=1, gh=2, gf=1,
        z=W, zs=1, gr=PARTS, bc=1, bn=1,
    )
    for k in SUMS:
        kinds.update({"hs" + k: 1, "rs" + k: 1, "ag" + k: 1, "fw" + k: 1})
    sems = {name + "_r": pltpu.SemaphoreType.DMA((count,)) for name, count in kinds.items()}
    sems["turn"] = pltpu.SemaphoreType.REGULAR
    sems["sent"] = pltpu.SemaphoreType.DMA((len(kinds),))
    sems["load"] = pltpu.SemaphoreType.DMA((10,))
    sems["store"] = pltpu.SemaphoreType.DMA((7,))
    return bufs, sems, list(kinds)


class Refs:
    pass


def kernel(z, names, kinds, *refs):
    g = Refs()
    for name, ref in zip(names, refs):
        setattr(g, name, ref)
    R, D, C, W, N, U, CAP = z.rows, z.width, z.cols, z.wide, z.narrow, z.part, z.cap
    CH = z.chunk
    half = D // 2
    me_w, me_n = lax.axis_index("wide"), lax.axis_index("narrow")
    core = lax.rem(me_w, 2)
    sibling = me_w + 1 - 2 * core

    def loop(count, body, start=0):
        def step(i, carry):
            body(i)
            return carry

        lax.fori_loop(start, count, step, 0)

    def sweep(count, body):
        for i in range(count):
            body(i)

    def flip(me, e, size):
        peer, bit = 0, 1
        while bit < size:
            peer = peer + bit * lax.rem(me // bit + e // bit, 2)
            bit *= 2
        return peer

    def peer_n(d):
        return flip(me_n, N - d, N)

    def peer_w(d):
        return flip(me_w, W - d, W)

    def ahead_n(d):
        return lax.rem(me_n + d, N)

    def behind_n(d):
        return lax.rem(me_n - d + N, N)

    def across(e):
        return flip(me_w, e, W)

    def remote(name, index, src, dst, axis="narrow", peer=0):
        return pltpu.make_async_remote_copy(
            src_ref=src,
            dst_ref=dst,
            send_sem=g.sent.at[kinds.index(name)],
            recv_sem=getattr(g, name + "_r").at[index],
            device_id={axis: peer},
            device_id_type=MESH,
        )

    def arrived(name, index, ref):
        remote(name, index, ref, ref, "narrow", peer_n(1)).wait_recv()

    def left(name, ref):
        remote(name, 0, ref, ref, "narrow", peer_n(1)).wait_send()

    def rows_at(start, size):
        return pl.ds(pl.multiple_of(start, size), size)

    sources = (g.nw_in, None, g.comb_in)
    fulls = (g.nwfull, None, g.wfull)
    part_w = D // W

    def share():
        return rows_at((core * (W // 2) + me_w // 2) * part_w, part_w)

    def share_send(k):
        def body(d):
            remote("sh%d" % k, d, sources[k].at[share()], fulls[k].at[me_n, share()], "narrow", ahead_n(d)).start()

        loop(N, body, 1)

    def share_pass(k):
        def body(d):
            part = fulls[k].at[behind_n(d), share()]
            arrived("sh%d" % k, d, part)
            loop(W // 2, lambda e: remote("sp%d" % k, d, part, part, "wide", across(2 * e)).start(), 1)

        loop(N, body, 1)

    def share_forward(k, d):
        s = behind_n(d)
        arrived("sp%d" % k, d, fulls[k].at[s, 0 : (W // 2 - 1) * part_w])
        part = fulls[k].at[s, rows_at(core * half, half)]
        remote("sf%d" % k, d if k == 0 else 0, part, part, "wide", sibling).start()

    hops = (2, 4)
    eighth = D // 8

    def hop_bit(h):
        return lax.rem(me_w // hops[h], 2)

    def quarter(h):
        return rows_at(D + h * half + (2 * core + hop_bit(h)) * eighth, eighth)

    def quarter_send(d):
        for h in range(2):
            mine = quarter(h)
            remote("sh1", d, g.comb_in.at[mine], g.wfull.at[me_n, mine], "narrow", ahead_n(d)).start()

    def quarter_pass(d):
        s = behind_n(d)
        arrived("sh1", d, g.wfull.at[s, 0 : 2 * eighth])
        for h in range(2):
            part = g.wfull.at[s, quarter(h)]
            remote("sp1", d, part, part, "wide", me_w + hops[h] - 2 * hops[h] * hop_bit(h)).start()

    def quarter_forward(d):
        s = behind_n(d)
        arrived("sp1", d, g.wfull.at[s, 0 : 2 * eighth])
        for h in range(2):
            part = g.wfull.at[s, rows_at(D + h * half + 2 * core * eighth, 2 * eighth)]
            remote("sf1", 0, part, part, "wide", sibling).start()

    def nb_copy(d):
        return remote("nb", 0, g.nbfull.at[me_n], g.nbfull.at[me_n], "narrow", peer_n(d))

    def z_copy(d):
        peer = peer_w(d)
        return remote("z", d, g.zsend.at[peer], g.ztab.at[me_w], "wide", peer)

    def zscale_copy(d):
        return remote("zs", 0, g.zscale, g.zscales.at[me_w], "wide", peer_w(d))

    def stat_copy(d):
        return remote("st", 0, g.stat, g.stats.at[me_n], "narrow", peer_n(d))

    def cot_copy(d):
        s = peer_n(d)
        return remote("ct", 0, g.cot_in.at[at(s, U)], g.cotrows.at[me_n], "narrow", s)

    def act_copy(d):
        s = peer_n(d)
        return remote("ac", 0, g.act.at[:, at(s, U)], g.actrows.at[me_n], "narrow", s)

    def ret_copy(p, d):
        peer, rows = peer_w(d), at(p, C // PARTS)
        return remote("gr", p, g.gsend.at[peer, rows], g.gret.at[me_w, rows], "wide", peer)

    def y_copy(p, d):
        s, rows = peer_n(d), at(p, C // PARTS)
        return remote("y", 0, g.y.at[rows, at(s, U)], g.yrows.at[me_n, rows], "narrow", s)

    def gh_copy(q, d):
        s = peer_n(d)
        return remote("gh", q, g.gh.at[rows_at(s * C + q * (C // 2), C // 2)], g.ghc.at[me_n, at(q, C // 2)], "narrow", s)

    def gf_copy(d):
        s = peer_n(d)
        return remote("gf", 0, g.gft.at[s], g.gf_out.at[me_n], "narrow", s)

    def bias_copy(name, src, dst, d):
        return remote(name, 0, src, dst.at[me_w], "wide", peer_w(d))

    def grad(k, suffix=""):
        return getattr(g, "g" + k + suffix)

    def core_rows(k, which):
        return (slice(None), at(which, grad(k).shape[1] // 2))

    def red_block(k, w):
        rows = grad(k).shape[1]
        size, down, lanes = z.red(rows)
        q = w // 2
        row = lax.rem(w, 2) * (rows // 2) + lax.rem(q, down) * size
        return (slice(None), rows_at(row, size), at(q // down, lanes))

    def out_rows(k, which):
        rows = grad(k).shape[1]
        if k == "c":
            return g.gc_sum.at[:, at(which, rows // 2)]
        return g.gn_out.at[:, rows_at(int(k[1]) * rows + which * (rows // 2), rows // 2)]

    def pair_start(k):
        remote("hs" + k, 0, grad(k).at[core_rows(k, 1 - core)], grad(k, "_half"), "wide", sibling).start()

    def reduce_pair(k):
        arrived("hs" + k, 0, grad(k, "_half"))
        own, mine = grad(k), core_rows(k, core)
        own[mine] = (own[mine].astype(F32) + grad(k, "_half")[...].astype(F32)).astype(BF16)

        def body(e):
            peer = across(2 * e)
            remote("rs" + k, 0, own.at[red_block(k, peer)], grad(k, "_in").at[me_w // 2], "wide", peer).start()

        loop(W // 2, body, 1)

    def reduce_sum(k):
        others = grad(k, "_in")
        arrived("rs" + k, 0, others.at[0 : W // 2 - 1])
        mine = red_block(k, me_w)
        total = lax.fori_loop(
            1, W // 2, lambda e, t: t + others[across(2 * e) // 2].astype(F32), grad(k)[mine].astype(F32), unroll=W <= 8
        )
        grad(k, "_sum")[mine] = total.astype(BF16)
        part = grad(k, "_sum").at[mine]
        loop(W // 2, lambda e: remote("ag" + k, 0, part, part, "wide", across(2 * e)).start(), 1)

    def gather_pass(k):
        arrived("ag" + k, 0, grad(k, "_in").at[0 : W // 2 - 1])
        part = grad(k, "_sum").at[core_rows(k, core)]
        remote("fw" + k, 0, part, out_rows(k, core), "wide", sibling).start()
        if k == "c":
            return None
        store = pltpu.make_async_copy(part, out_rows(k, core), g.store.at[SUMS.index(k)])
        store.start()
        return store

    def gather_wait(k):
        arrived("fw" + k, 0, out_rows(k, 1 - core))

    loads = [
        (g.feats_in, g.feats),
        (g.nw_in, g.nwfull.at[me_n]),
        (g.comb_in, g.wfull.at[me_n]),
        (g.slot_in, g.slot),
        (g.mask_in, g.mask),
        (g.visit_in, g.visit),
        (g.send_in, g.send),
        (g.cot_in, g.cot),
        (g.nb_in, g.nb),
        (g.cb_in, g.cb),
    ]

    def load(i):
        return pltpu.make_async_copy(loads[i][0], loads[i][1], g.load.at[i])

    barrier = pltpu.get_barrier_semaphore()
    loop(W, lambda d: pl.semaphore_signal(barrier, inc=1, device_id={"wide": peer_w(d)}, device_id_type=MESH), 1)
    loop(N, lambda d: pl.semaphore_signal(barrier, inc=1, device_id={"narrow": peer_n(d)}, device_id_type=MESH), 1)
    order = (6, 8, 3, 4, 5, 0, 1, 2, 7, 9)
    for i in order:
        load(i).start()
    pl.semaphore_wait(barrier, W - 1 + N - 1)
    share_send(0)
    load(8).wait()
    g.nbfull[me_n] = jnp.broadcast_to(g.nb[...].astype(F32).reshape(1, C), (8, C))
    loop(N, lambda d: nb_copy(d).start(), 1)

    for i in (3, 4, 5):
        load(i).wait()
    K = z.slots
    shift = CAP.bit_length() - 1

    def fill(i):
        rows = at(i, CH)
        g.code[rows, :] = jnp.zeros((CH, 128), I32)
        g.wts[rows, :] = jnp.zeros((CH, 128), F32)
        code = g.slot[:, rows].T
        g.code[rows, 0:K] = code
        g.code[rows, 64 : 64 + K] = code
        weight = (g.mask[:, rows] * g.visit[:, rows]).astype(F32).T
        g.wts[rows, 0:K] = weight
        g.wts[rows, 64 : 64 + K] = weight

    loop(R // CH, fill)

    lane = lax.broadcasted_iota(I32, (8, 128), 1)
    sub = lax.broadcasted_iota(I32, (8, 128), 0)
    half_lane = jnp.where(lane >= 64, 1, 0)
    place = [sub == 2 * j + half_lane for j in range(4)]
    place_b = [jnp.where(m, 1.0, 0.0) for m in place]
    place_b = [jnp.concatenate([m, m], axis=0).astype(BF16) for m in place_b]
    low_row = lax.broadcasted_iota(I32, (CAP, 128), 0).astype(F32).astype(BF16)

    def count_group(i):
        start = pl.multiple_of(i * 16, 16)
        outs = []
        for p in range(2):
            rows = pl.ds(pl.multiple_of(start + 8 * p, 8), 8)
            code, weight = g.code[rows, :], g.wts[rows, :]
            high, low = code >> shift, (code & (CAP - 1)).astype(F32)
            left = []
            for h in range(0, z.blocks, 2):
                pair = [jnp.where(high == h + q, weight, 0.0) for q in range(2)]
                pair = jnp.concatenate(pair, axis=0).astype(BF16)
                left.append(jnp.concatenate([pair * place_b[j] for j in range(4)], axis=1))
            left = jnp.concatenate(left, axis=0)
            right = []
            for j in range(4):
                row = jnp.sum(jnp.where(place[j], low, 0.0), axis=0, keepdims=True)
                row = jnp.broadcast_to(row.astype(BF16), (CAP, 128))
                right.append(jnp.where(low_row == row, jnp.ones((), BF16), jnp.zeros((), BF16)))
            outs.append(mm_nt(left, jnp.concatenate(right, axis=1)))
        for h in range(z.blocks):
            block = [out[h * 8 : h * 8 + 8] for out in outs]
            g.counts[h, pl.ds(start, 16), :] = jnp.concatenate(block, axis=0).astype(BF16)

    UNROLL = 4
    groups = R // 16 // UNROLL

    def count_groups(first, last):
        def body(i):
            for q in range(UNROLL):
                count_group(i * UNROLL + q)

        loop(last, body, first)

    def hidden(s):
        def body(i):
            rows = at(i, CH)
            value = mm(g.feats[rows, :], g.nwfull[s]) + g.nbfull[s, 0:1, :]
            value = jnp.maximum(value, 0.0)
            top = value.astype(BF16)
            rest = (value - top.astype(F32)).astype(BF16)
            g.msg[rows, at(s, C)] = top
            weight = g.wfull[me_n, pl.ds(pl.multiple_of(D + s * C, C), C), :]
            g.zacc[rows, :] += mm(top, weight) + mm(rest, weight)

        sweep(R // CH, body)

    done = [0]

    def counts_until(last):
        last = groups * last // 16
        count_groups(done[0], last)
        done[0] = last

    def zero(i):
        g.zacc[at(i, CH), :] = jnp.zeros((CH, C), F32)

    loop(R // CH, zero)
    for i in (0, 1, 2):
        load(i).wait()
    hidden(me_n)
    counts_until(2)
    load(6).wait()
    g.send_t[...] = g.send[...].T

    def select(d):
        r = peer_w(d)
        which = lax.broadcasted_iota(I32, (CAP, W), 1)
        col = jnp.sum(jnp.where(which == r, g.send_t[...], 0), axis=1, keepdims=True)
        place_u = lax.broadcasted_iota(I32, (CAP, R), 1)
        g.sel[r] = jnp.where(place_u == col, 1.0, 0.0).astype(BF16)

    loop(W, select, 1)
    share_pass(0)
    loop(N, quarter_send, 1)
    counts_until(8)
    share_forward(0, 1)

    def take(d):
        arrived("sf0", d, g.nwfull.at[0, 0:half])
        hidden(behind_n(d))

    counts_until(10)
    share_forward(0, 2)
    loop(N, lambda d: cot_copy(d).start(), 1)
    arrived("nb", 0, g.nbfull.at[0 : N - 1])
    take(1)
    loop(N, functools.partial(share_forward, 0), 3)
    take(2)
    share_send(2)
    loop(N, take, 3)

    def column_max(i, most):
        return jnp.maximum(most, jnp.max(jnp.abs(g.zacc[at(i, CH), :]), axis=0, keepdims=True))

    most = lax.fori_loop(0, R // CH, column_max, jnp.full((1, C), 1e-30, F32))
    scale = most * (1.0 / 32766.0)
    g.zscale[...] = jnp.broadcast_to(scale, (8, C))
    loop(W, lambda d: zscale_copy(d).start(), 1)
    inv_scale = 1.0 / scale

    def code_z(i):
        rows = at(i, CH)
        whole = jnp.round(g.zacc[rows, :] * inv_scale)
        high = jnp.floor(whole * (1.0 / 256.0))
        g.zqa[rows, :] = high.astype(BF16)
        g.zqb[rows, :] = (whole - high * 256.0).astype(BF16)

    loop(R // CH, code_z)

    def send_z(d):
        peer = peer_w(d)
        picked = mm(g.sel[peer], g.zqa[...]) * 256.0 + mm(g.sel[peer], g.zqb[...])
        g.zsend[peer] = picked.astype(I32).astype(I16)
        z_copy(d).start()

    near = W // 4 + 1
    loop(near, send_z, 1)
    counts_until(12)
    loop(W, send_z, near)

    def split_z(i):
        rows = at(i, CH)
        value = g.zacc[rows, :]
        top = value.astype(BF16)
        g.zhi[rows, :] = top
        g.zlo[rows, :] = (value - top.astype(F32)).astype(BF16)

    loop(R // CH, split_z)
    counts_until(16)
    load(7).wait()
    load(9).wait()

    def own_part(i):
        rows = at(i, CH)
        value = mm(g.feats[rows, :], g.wfull[me_n, 0:D, :]) + g.cb[...].astype(F32).reshape(1, C)
        g.self_t[:, rows] = value.T
        g.cot_t[:, rows] = g.cot[rows, :].astype(F32).T
        total = jnp.zeros((CH, C), F32)
        for h in range(z.local):
            part = slice(h * CAP, (h + 1) * CAP)
            block = g.counts[h, rows, :]
            total += mm(block, g.zhi[part, :]) + mm(block, g.zlo[part, :])
        g.acc[rows, :] = total

    sweep(R // CH, own_part)
    ones = jnp.ones((16, 128), BF16)
    g.invs[...] = 2.0 / mm_nt(ones, g.wts[...].astype(BF16))

    def mine_t(i):
        cols = at(i, C)
        g.msg_t[cols, :] = g.msg[at(me_n, U), cols].astype(F32).T.astype(BF16)

    loop(D // C, mine_t)

    def take_z(d):
        s = peer_w(d)
        piece = min(32, CAP)
        for i in range(CAP // piece):
            rows = at(i, piece)
            value = g.ztab[s, rows, :].astype(I32).astype(F32) * g.zscales[s, 0:1, :]
            top = value.astype(BF16)
            g.thi[s, rows, :] = top
            g.tlo[s, rows, :] = (value - top.astype(F32)).astype(BF16)

    def pool(first, last):
        loop(last, take_z, first)

        def body(i):
            rows = at(i, CH)

            def add(d, total):
                s = peer_w(d)
                block = g.counts[z.local + s, rows, :]
                return total + mm(block, g.thi[s]) + mm(block, g.tlo[s])

            g.acc[rows, :] = lax.fori_loop(first, last, add, g.acc[rows, :], unroll=W <= 8)

        return body

    arrived("zs", 0, g.zscales.at[0 : W - 1])
    for first_d, last_d in ((1, near), (W - 1, W)):
        loop(last_d, lambda d: z_copy(d).wait_recv(), first_d)
        sweep(R // CH, pool(first_d, last_d))
    loop(W - 1, lambda d: z_copy(d).wait_recv(), near)
    loop(N, quarter_pass, 1)
    pool_rest = pool(near, W - 1)

    def activate(i):
        pool_rest(i)
        rows = at(i, CH)
        pre = g.acc[rows, :].T * g.invs[0:1, rows] + g.self_t[:, rows]
        g.self_t[:, rows] = pre
        act = jnp.maximum(pre, 0.0)
        g.act[:, rows] = act.astype(BF16)
        squares = jnp.sum(act * act, axis=0, keepdims=True)
        inner = jnp.sum(act * g.cot_t[:, rows], axis=0, keepdims=True)
        g.stat[2 * i : 2 * i + 2, :] = jnp.concatenate([squares, inner], axis=0)

    sweep(R // CH, activate)
    loop(N, lambda d: stat_copy(d).start(), 1)
    pl.semaphore_signal(g.turn, inc=1, device_id={"wide": sibling}, device_id_type=MESH)
    g.actrows[me_n] = g.act[:, at(me_n, U)]
    pl.semaphore_wait(g.turn, 1)
    loop(N, lambda d: act_copy(d).start(), 1)
    arrived("st", 0, g.stats.at[0 : N - 1])
    g.stats[me_n] = g.stat[...]

    def norms(i):
        total = g.stats[0, 2 * i : 2 * i + 2, :]
        for s in range(1, N):
            total += g.stats[s, 2 * i : 2 * i + 2, :]
        return lax.rsqrt(total[0:1] / D + EPSILON), total[1:2]

    def grad_act(i):
        rows = at(i, CH)
        inv, inner = norms(i)
        pre = g.self_t[:, rows]
        act = jnp.maximum(pre, 0.0)
        grad = g.cot_t[:, rows] * inv - act * (inner * (inv * inv * inv) / D)
        grad = jnp.where(pre > 0, grad, 0.0)
        g.gp[:, rows] = grad.astype(BF16)
        g.gps[:, rows] = (grad * g.invs[0:1, rows]).astype(BF16)

    sweep(R // CH, grad_act)

    def send_ret(d):
        peer = peer_w(d)
        g.gsend[peer] = mm(g.gps[...], g.counts[z.local + peer]).astype(BF16)
        ret_copy(0, d).start()

    loop(W, send_ret, 1)

    def more_ret(p):
        loop(W, lambda d: ret_copy(p, d).start(), 1)

    more_ret(1)
    more_ret(2)
    join = max(1, 128 // CAP)
    for h in range(0, z.local, join):
        parts = [mm(g.gps[...], g.counts[h + q]) for q in range(join)]
        parts = jnp.concatenate(parts, axis=1) if join > 1 else parts[0]
        g.yacc[:, h * CAP : (h + join) * CAP] = parts

    def embed(i):
        rows = at(i, CH)
        inv, _ = norms(i)
        value = jnp.maximum(g.self_t[:, rows], 0.0) * inv
        g.emb[rows, :] = value.T.astype(BF16)

    sweep(R // CH, embed)
    emb_store = pltpu.make_async_copy(g.emb, g.emb_out, g.store.at[4])
    emb_store.start()
    more_ret(3)

    LW = min(512, D)

    def grad_self(i):
        lanes = at(i, LW)
        g.gc[0, :, lanes] = mm(g.gp[...], g.feats[:, lanes]).astype(BF16)

    sweep(D // LW, grad_self)
    ones_r = jnp.ones((8, R), BF16)
    g.gcb[...] = mm_nt(ones_r, g.gp[...])


    def take_ret(p):
        part = at(p, C // PARTS)
        arrived("gr", p, g.gret.at[0 : W - 1, part])

        def body(i):
            lanes = at(i, CH)

            def add(d, total):
                s = peer_w(d)
                return total + mm(g.gret[s, part, :], g.sel[s, :, lanes])

            total = lax.fori_loop(1, W, add, g.yacc[part, lanes], unroll=W <= 8)
            g.y[part, lanes] = total.astype(BF16)

        sweep(R // CH, body)
        loop(N, lambda d: y_copy(p, d).start(), 1)

    take_ret(0)
    loop(N, quarter_forward, 1)
    share_pass(2)
    for p in range(1, PARTS):
        take_ret(p)
    g.yrows[me_n] = g.y[:, at(me_n, U)]

    def grad_pool(i):
        lanes = at(i, LW)
        g.gc[1, :, lanes] = mm(g.y[...], g.msg[:, lanes]).astype(BF16)

    sweep(D // LW, grad_pool)
    loop(W, lambda d: bias_copy("bc", g.gcb, g.gcb_in, d).start(), 1)
    pair_start("c")

    reduce_pair("c")
    arrived("ct", 0, g.cotrows.at[0 : N - 1])
    g.cotrows[me_n] = g.cot[at(me_n, U), :]
    for s in range(N):
        g.cotrows_t[s] = g.cotrows[s].astype(F32).T
    arrived("sf1", 0, g.wfull.at[0 : N - 1, 0:half])
    arrived("y", 0, g.yrows.at[0 : N - 1])

    def hidden_rows(i):
        rows = at(i, CH)
        wrows = slice(D + i * CH, D + (i + 1) * CH)
        total = jnp.zeros((CH, U), F32)
        for s in range(N):
            total += mm(g.wfull[s, wrows, :], g.yrows[s])
        g.gh[rows, :] = jnp.where(g.msg_t[rows, :] > 0, total, 0.0).astype(BF16)

    sweep(D // CH, hidden_rows)
    loop(N, lambda d: gh_copy(0, d).start(), 1)
    g.ghc[me_n] = g.gh[at(me_n, C), :]

    def feature_rows(i):
        rows = at(i, C)
        total = jnp.zeros((C, U), F32)
        for s in range(N):
            total += mm(g.wfull[s, rows, :], g.gprows[s]) + mm(g.nwfull[s, rows, :], g.gh[s * C : (s + 1) * C, :])
        g.gft[i] = total.T.astype(BF16)

    loop(N, functools.partial(share_forward, 2), 1)
    arrived("ac", 0, g.actrows.at[0 : N - 1])
    per = CH // U
    lanes = at(lax.rem(me_n, per), U) if per > 1 else slice(None)
    total = g.stats[0, :, lanes]
    for s in range(1, N):
        total += g.stats[s, :, lanes]
    row = lax.broadcasted_iota(I32, total.shape, 0) - 2 * (me_n // per)
    inv = lax.rsqrt(jnp.sum(jnp.where(row == 0, total, 0.0), axis=0, keepdims=True) / D + EPSILON)
    inner = jnp.sum(jnp.where(row == 1, total, 0.0), axis=0, keepdims=True)
    factor = inner * (inv * inv * inv) / D
    for s in range(N):
        act = g.actrows[s].astype(F32)
        grad_rows = jnp.where(act > 0, g.cotrows_t[s] * inv - act * factor, 0.0)
        g.gprows[s] = grad_rows.astype(BF16)
    arrived("sf2", 0, g.wfull.at[0 : N - 1, 0:half])
    loop(N, lambda d: gh_copy(1, d).start(), 1)
    sweep(N, feature_rows)
    gf_store = pltpu.make_async_copy(g.gft.at[me_n], g.gf_out.at[me_n], g.store.at[3])
    gf_store.start()

    reduce_sum("c")

    def grad_neigh(q):
        rows = at(q, C // 2)
        out = (g.gn0, g.gn1)[q]

        def body(i):
            lanes = at(i, LW)
            total = jnp.zeros((C // 2, LW), F32)
            for s in range(N):
                total += mm(g.ghc[s, rows, :], g.feats[s * U : (s + 1) * U, lanes])
            out[0, :, lanes] = total.astype(BF16)

        sweep(D // LW, body)

    arrived("gh", 0, g.ghc.at[0 : N - 1, 0 : C // 2])
    grad_neigh(0)
    pair_start("n0")
    arrived("gh", 1, g.ghc.at[0 : N - 1, 0 : C // 2])
    loop(N, lambda d: gf_copy(d).start(), 1)
    reduce_pair("n0")
    grad_neigh(1)
    pair_start("n1")
    total = jnp.zeros((8, C), F32)
    ones_u = jnp.ones((8, U), BF16)
    for s in range(N):
        total += mm_nt(ones_u, g.ghc[s])
    g.gnb[...] = total
    loop(W, lambda d: bias_copy("bn", g.gnb, g.gnb_in, d).start(), 1)
    reduce_pair("n1")
    reduce_sum("n0")
    def bias_sum(name, own, others):
        arrived(name, 0, others.at[0 : W - 1])
        left(name, others.at[0 : W - 1])
        own[...] = lax.fori_loop(1, W, lambda d, total: total + others[peer_w(d)], own[...])

    bias_sum("bc", g.gcb, g.gcb_in)
    bias_sum("bn", g.gnb, g.gnb_in)
    gcb_store = pltpu.make_async_copy(g.gcb, g.gcb_out, g.store.at[5])
    gnb_store = pltpu.make_async_copy(g.gnb, g.gnb_out, g.store.at[6])
    gcb_store.start()
    gnb_store.start()
    gather_pass("c")
    reduce_sum("n1")
    gn0_store = gather_pass("n0")
    gn1_store = gather_pass("n1")
    gather_wait("c")
    for p in range(2):
        for i in range(D // CH):
            g.gct[p, at(i, CH), :] = g.gc_sum[p, :, at(i, CH)].astype(F32).T.astype(BF16)
    gc_store = pltpu.make_async_copy(g.gct, g.gc_out, g.store.at[0])
    gc_store.start()
    for k in SUMS[1:]:
        gather_wait(k)
    arrived("gf", 0, g.gf_out.at[0 : N - 1])

    for k in (0, 2):
        left("sh%d" % k, fulls[k].at[0 : N - 1, 0:part_w])
        left("sp%d" % k, fulls[k].at[0 : N - 1, 0 : (W // 2 - 1) * part_w])
        left("sf%d" % k, fulls[k].at[0 : N - 1, 0:half])
    left("sh1", g.wfull.at[0 : N - 1, 0 : 2 * eighth])
    left("sp1", g.wfull.at[0 : N - 1, 0 : 2 * eighth])
    left("sf1", g.wfull.at[0 : N - 1, 0:half])
    left("nb", g.nbfull.at[0 : N - 1])
    left("z", g.zsend.at[0 : W - 1])
    left("zs", g.zscales.at[0 : W - 1])
    left("st", g.stats.at[0 : N - 1])
    left("ct", g.cotrows.at[0 : N - 1])
    left("ac", g.actrows.at[0 : N - 1])
    left("gr", g.gsend.at[0 : W - 1])
    left("y", g.yrows.at[0 : N - 1])
    left("gh", g.ghc.at[0 : N - 1])
    left("gf", g.gf_out.at[0 : N - 1])
    for k in SUMS:
        left("hs" + k, grad(k, "_half"))
        left("rs" + k, grad(k, "_in").at[0 : W // 2 - 1])
        left("ag" + k, grad(k, "_in").at[0 : W // 2 - 1])
        left("fw" + k, grad(k, "_sum").at[core_rows(k, core)])
    for store in (emb_store, gf_store, gc_store, gcb_store, gnb_store, gn0_store, gn1_store):
        store.wait()


def finish(z, *refs):
    names = ["emb", "gf", "gn", "gc", "gnb", "gcb"]
    ins = dict(zip(names, refs[:6]))
    outs = dict(zip(names, refs[6:12]))
    emb, gf, gn, gc, nb, cb, gf_t, gn_t, gc_t, nb_t, cb_t, load, store = refs[12:]
    D, C, N, U = z.width, z.cols, z.narrow, z.part
    step = D // N
    emb_load = pltpu.make_async_copy(ins["emb"], emb, load.at[6])
    emb_load.start()
    jobs = [
        (ins["gn"].at[0], gn, [(gn.at[:, at(i, step)], gn_t.at[at(i, step)], outs["gn"].at[at(i, step)]) for i in range(N)]),
        (ins["gf"], gf, [(gf.at[i], gf_t.at[at(i, U)], outs["gf"].at[at(i, U)]) for i in range(N)]),
    ]
    for p in range(2):
        parts = [(gc.at[p, at(i, step)], gc_t.at[p, at(i, step)], outs["gc"].at[p, at(i, step)]) for i in range(N)]
        jobs.append((ins["gc"].at[p], gc.at[p], parts))
    loads = [pltpu.make_async_copy(src, held, load.at[i]) for i, (src, held, _) in enumerate(jobs)]
    small = (("gnb", nb, nb_t), ("gcb", cb, cb_t))
    loads += [pltpu.make_async_copy(ins[k], held, load.at[4 + i]) for i, (k, held, _) in enumerate(small)]
    for copy in loads:
        copy.start()
    stores = [pltpu.make_async_copy(emb, outs["emb"], store.at[0])]

    def keep(src, dst):
        stores.append(pltpu.make_async_copy(src, dst, store.at[len(stores)]))
        stores[-1].start()

    for i, (_, _, parts) in enumerate(jobs):
        loads[i].wait()
        for k, (part, turned, out) in enumerate(parts):
            turned[...] = part[...].astype(F32).T if i == 0 else part[...].astype(F32)
            keep(turned, out)
        if i == 0:
            emb_load.wait()
            stores[0].start()
    for i, (k, held, turned) in enumerate(small):
        loads[4 + i].wait()
        turned[...] = held[0:1, :]
        keep(turned, outs[k])
    for copy in stores:
        copy.wait()


def shards(wide, narrow, node_feats, neigh_weight, neigh_bias, combine_weight, combine_bias, cotangent,
           neighbour_slot, neighbour_mask, visit_count, send_rows):
    z = Sizes(node_feats, neigh_weight, send_rows, neighbour_slot.T, wide, narrow)
    R, D, C, W, N, U = z.rows, z.width, z.cols, z.wide, z.narrow, z.part
    bufs, sems, kinds = scratch(z)
    names = NAMES_IN + NAMES_OUT + list(bufs) + list(sems)
    outs = (
        jax.ShapeDtypeStruct((R, C), BF16),
        jax.ShapeDtypeStruct((N, U, C), BF16),
        jax.ShapeDtypeStruct((1, C, D), BF16),
        jax.ShapeDtypeStruct((2, D, C), BF16),
        jax.ShapeDtypeStruct((8, C), F32),
        jax.ShapeDtypeStruct((8, C), F32),
    )
    emb, gf, gn, gc, gnb, gcb = pl.pallas_call(
        functools.partial(kernel, z, names, kinds),
        out_shape=outs,
        in_specs=[pl.BlockSpec(memory_space=pl.ANY)] * len(NAMES_IN),
        out_specs=[pl.BlockSpec(memory_space=pl.ANY)] * len(NAMES_OUT),
        scratch_shapes=list(bufs.values()) + list(sems.values()),
        compiler_params=pltpu.CompilerParams(
            collective_id=0, has_side_effects=True, vmem_limit_bytes=60 * 2**20
        ),
        cost_estimate=pl.CostEstimate(flops=2 * 10**10, bytes_accessed=2 * 10**7, transcendentals=0),
        name="layer",
    )(
        node_feats, neigh_weight, neigh_bias, combine_weight, combine_bias, cotangent,
        neighbour_slot.T, neighbour_mask.T, visit_count.T, send_rows,
    )
    hbm = pl.BlockSpec(memory_space=pl.ANY)
    emb, grad_features, grad_neigh, grad_combine, gnb, gcb = pl.pallas_call(
        functools.partial(finish, z),
        out_shape=(
            jax.ShapeDtypeStruct((R, C), BF16),
            jax.ShapeDtypeStruct((R, C), F32),
            jax.ShapeDtypeStruct((D, C), F32),
            jax.ShapeDtypeStruct((2, D, C), F32),
            jax.ShapeDtypeStruct((1, C), F32),
            jax.ShapeDtypeStruct((1, C), F32),
        ),
        in_specs=[hbm] * 6,
        out_specs=[hbm] * 6,
        scratch_shapes=[
            pltpu.VMEM((R, C), BF16),
            pltpu.VMEM((N, U, C), BF16),
            pltpu.VMEM((C, D), BF16),
            pltpu.VMEM((2, D, C), BF16),
            pltpu.VMEM((8, C), F32),
            pltpu.VMEM((8, C), F32),
            pltpu.VMEM((R, C), F32),
            pltpu.VMEM((D, C), F32),
            pltpu.VMEM((2, D, C), F32),
            pltpu.VMEM((1, C), F32),
            pltpu.VMEM((1, C), F32),
            pltpu.SemaphoreType.DMA((7,)),
            pltpu.SemaphoreType.DMA((4 * N + 3,)),
        ],
        compiler_params=pltpu.CompilerParams(vmem_limit_bytes=60 * 2**20),
        name="finish",
    )(emb, gf, gn, gc, gnb, gcb)
    return emb, grad_features, grad_neigh, gnb.reshape(C), grad_combine.reshape(2 * D, C), gcb.reshape(C)


def solution(mesh):
    placed = (
        P("wide", None),
        P(None, "narrow"),
        P("narrow"),
        P(None, "narrow"),
        P("narrow"),
        P("wide", "narrow"),
        P("wide", None),
        P("wide", None),
        P("wide", None),
        P("wide", None),
    )
    return jax.shard_map(
        functools.partial(shards, mesh.shape["wide"], mesh.shape["narrow"]),
        mesh=mesh,
        in_specs=placed,
        out_specs=(
            P("wide", "narrow"),
            P("wide", "narrow"),
            P(None, "narrow"),
            P("narrow"),
            P(None, "narrow"),
            P("narrow"),
        ),
        check_vma=False,
    )
```

```python
import functools

import jax
import jax.numpy as jnp
from jax import lax
from jax.experimental import pallas as pl
from jax.experimental.pallas import tpu as pltpu
from jax.sharding import PartitionSpec as P

EPSILON = 1e-06
PARTS = 4
SUMS = ("c", "n0", "n1")
F32 = jnp.float32
BF16 = jnp.bfloat16
I32 = jnp.int32
I16 = jnp.int16
MESH = pl.DeviceIdType.MESH


def mm(left, right):
    return jnp.dot(left, right, preferred_element_type=F32)


def mm_nt(left, right):
    return lax.dot_general(left, right, (((1,), (1,)), ((), ())), preferred_element_type=F32)


def at(index, size):
    if isinstance(index, int):
        return slice(index * size, (index + 1) * size)
    return pl.ds(pl.multiple_of(index * size, size), size)


class Sizes:
    def __init__(self, feats, neigh, send, slot, wide, narrow):
        self.rows, self.width = feats.shape
        self.cols = neigh.shape[1]
        self.cap = send.shape[1]
        self.slots = slot.shape[0]
        self.wide, self.narrow = wide, narrow
        self.chunk = min(256, self.rows)
        self.part = self.rows // narrow
        self.local = self.rows // self.cap
        self.blocks = self.local + wide
        self.pairs = wide // 2

    def red(self, rows):
        size = max(16, rows // 2 // self.pairs)
        down = rows // 2 // size
        return size, down, self.width * down // self.pairs


NAMES_IN = ["feats_in", "nw_in", "nb_in", "comb_in", "cb_in", "cot_in", "slot_in", "mask_in", "visit_in", "send_in"]
NAMES_OUT = ["emb_out", "gf_out", "gn_out", "gc_out", "gnb_out", "gcb_out"]


def scratch(z):
    R, D, C, W, N, U, CAP = z.rows, z.width, z.cols, z.wide, z.narrow, z.part, z.cap
    v = lambda *shape: pltpu.VMEM(shape[:-1], shape[-1])
    bufs = dict(
        feats=v(R, D, BF16),
        nwfull=v(N, D, C, BF16),
        nbfull=v(N, 8, C, F32),
        nb=v(C, BF16),
        cb=v(C, BF16),
        wfull=v(N, 2 * D, C, BF16),
        cot=v(R, C, BF16),
        slot=v(z.slots, R, I32),
        mask=v(z.slots, R, I32),
        visit=v(z.slots, R, I32),
        send=v(W, CAP, I32),
        send_t=v(CAP, W, I32),
        code=v(R, 128, I32),
        wts=v(R, 128, F32),
        counts=v(z.blocks, R, CAP, BF16),
        counts_lo=v(z.blocks, R, CAP, BF16),
        sel=v(W, CAP, R, BF16),
        msg=v(R, D, BF16),
        zacc=v(R, C, F32),
        zhi=v(R, C, BF16),
        zlo=v(R, C, BF16),
        zqa=v(R, C, BF16),
        zqb=v(R, C, BF16),
        zscale=v(8, C, F32),
        thi=v(W, CAP, C, BF16),
        tlo=v(W, CAP, C, BF16),
        zscales=v(W, 8, C, F32),
        zsend=v(W, CAP, C, I16),
        ztab=v(W, CAP, C, I16),
        acc=v(R, C, F32),
        self_t=v(C, R, F32),
        cot_t=v(C, R, F32),
        invs=v(16, R, F32),
        stat=v(2 * (R // z.chunk), z.chunk, F32),
        stats=v(N, 2 * (R // z.chunk), z.chunk, F32),
        emb=v(R, C, BF16),
        gp=v(C, R, BF16),
        gps=v(C, R, BF16),
        act=v(C, R, BF16),
        actrows=v(N, C, U, BF16),
        cotrows=v(N, U, C, BF16),
        cotrows_t=v(N, C, U, F32),
        gprows=v(N, C, U, BF16),
        gsend=v(W, C, CAP, BF16),
        gret=v(W, C, CAP, BF16),
        yacc=v(C, R, F32),
        y=v(C, R, BF16),
        yrows=v(N, C, U, BF16),
        msg_t=v(D, U, BF16),
        gh=v(D, U, BF16),
        ghc=v(N, C, U, BF16),
        gft=v(N, U, C, BF16),
        gct=v(2, D, C, BF16),
        gc=v(2, C, D, BF16),
        gc_half=v(2, C // 2, D, BF16),
        gc_in=v(W // 2, 2, z.red(C)[0], z.red(C)[2], BF16),
        gc_sum=v(2, C, D, BF16),
        gn0=v(1, C // 2, D, BF16),
        gn0_half=v(1, C // 4, D, BF16),
        gn0_in=v(W // 2, 1, z.red(C // 2)[0], z.red(C // 2)[2], BF16),
        gn0_sum=v(1, C // 2, D, BF16),
        gn1=v(1, C // 2, D, BF16),
        gn1_half=v(1, C // 4, D, BF16),
        gn1_in=v(W // 2, 1, z.red(C // 2)[0], z.red(C // 2)[2], BF16),
        gn1_sum=v(1, C // 2, D, BF16),
        gcb=v(8, C, F32),
        gcb_in=v(W, 8, C, F32),
        gnb=v(8, C, F32),
        gnb_in=v(W, 8, C, F32),
    )
    kinds = dict(
        sh0=N, sh1=N, sh2=N, sp0=N, sp1=N, sp2=N, sf0=N, sf1=1, sf2=1, nb=1, st=1, ct=1, ac=1, y=1, gh=2, gf=1,
        z=W, zs=1, gr=PARTS, bc=1, bn=1,
    )
    for k in SUMS:
        kinds.update({"hs" + k: 1, "rs" + k: 1, "ag" + k: 1, "fw" + k: 1})
    sems = {name + "_r": pltpu.SemaphoreType.DMA((count,)) for name, count in kinds.items()}
    sems["turn"] = pltpu.SemaphoreType.REGULAR
    sems["sent"] = pltpu.SemaphoreType.DMA((len(kinds),))
    sems["load"] = pltpu.SemaphoreType.DMA((10,))
    sems["store"] = pltpu.SemaphoreType.DMA((7,))
    return bufs, sems, list(kinds)


class Refs:
    pass


def kernel(z, names, kinds, *refs):
    g = Refs()
    for name, ref in zip(names, refs):
        setattr(g, name, ref)
    R, D, C, W, N, U, CAP = z.rows, z.width, z.cols, z.wide, z.narrow, z.part, z.cap
    CH = z.chunk
    half = D // 2
    me_w, me_n = lax.axis_index("wide"), lax.axis_index("narrow")
    core = lax.rem(me_w, 2)
    sibling = me_w + 1 - 2 * core

    def loop(count, body, start=0):
        def step(i, carry):
            body(i)
            return carry

        lax.fori_loop(start, count, step, 0)

    def sweep(count, body):
        for i in range(count):
            body(i)

    def flip(me, e, size):
        peer, bit = 0, 1
        while bit < size:
            peer = peer + bit * lax.rem(me // bit + e // bit, 2)
            bit *= 2
        return peer

    def peer_n(d):
        return flip(me_n, N - d, N)

    def peer_w(d):
        return flip(me_w, W - d, W)

    def ahead_n(d):
        return lax.rem(me_n + d, N)

    def behind_n(d):
        return lax.rem(me_n - d + N, N)

    def across(e):
        return flip(me_w, e, W)

    def remote(name, index, src, dst, axis="narrow", peer=0):
        return pltpu.make_async_remote_copy(
            src_ref=src,
            dst_ref=dst,
            send_sem=g.sent.at[kinds.index(name)],
            recv_sem=getattr(g, name + "_r").at[index],
            device_id={axis: peer},
            device_id_type=MESH,
        )

    def arrived(name, index, ref):
        remote(name, index, ref, ref, "narrow", peer_n(1)).wait_recv()

    def left(name, ref):
        remote(name, 0, ref, ref, "narrow", peer_n(1)).wait_send()

    def rows_at(start, size):
        return pl.ds(pl.multiple_of(start, size), size)

    sources = (g.nw_in, None, g.comb_in)
    fulls = (g.nwfull, None, g.wfull)
    part_w = D // W

    def share():
        return rows_at((core * (W // 2) + me_w // 2) * part_w, part_w)

    def share_send(k):
        def body(d):
            remote("sh%d" % k, d, sources[k].at[share()], fulls[k].at[me_n, share()], "narrow", ahead_n(d)).start()

        loop(N, body, 1)

    def share_pass(k):
        def body(d):
            part = fulls[k].at[behind_n(d), share()]
            arrived("sh%d" % k, d, part)
            loop(W // 2, lambda e: remote("sp%d" % k, d, part, part, "wide", across(2 * e)).start(), 1)

        loop(N, body, 1)

    def share_forward(k, d):
        s = behind_n(d)
        arrived("sp%d" % k, d, fulls[k].at[s, 0 : (W // 2 - 1) * part_w])
        part = fulls[k].at[s, rows_at(core * half, half)]
        remote("sf%d" % k, d if k == 0 else 0, part, part, "wide", sibling).start()

    hops = (2, 4)
    eighth = D // 8

    def hop_bit(h):
        return lax.rem(me_w // hops[h], 2)

    def quarter(h):
        return rows_at(D + h * half + (2 * core + hop_bit(h)) * eighth, eighth)

    def quarter_send(d):
        for h in range(2):
            mine = quarter(h)
            remote("sh1", d, g.comb_in.at[mine], g.wfull.at[me_n, mine], "narrow", ahead_n(d)).start()

    def quarter_pass(d):
        s = behind_n(d)
        arrived("sh1", d, g.wfull.at[s, 0 : 2 * eighth])
        for h in range(2):
            part = g.wfull.at[s, quarter(h)]
            remote("sp1", d, part, part, "wide", me_w + hops[h] - 2 * hops[h] * hop_bit(h)).start()

    def quarter_forward(d):
        s = behind_n(d)
        arrived("sp1", d, g.wfull.at[s, 0 : 2 * eighth])
        for h in range(2):
            part = g.wfull.at[s, rows_at(D + h * half + 2 * core * eighth, 2 * eighth)]
            remote("sf1", 0, part, part, "wide", sibling).start()

    def nb_copy(d):
        return remote("nb", 0, g.nbfull.at[me_n], g.nbfull.at[me_n], "narrow", peer_n(d))

    def z_copy(d):
        peer = peer_w(d)
        return remote("z", d, g.zsend.at[peer], g.ztab.at[me_w], "wide", peer)

    def zscale_copy(d):
        return remote("zs", 0, g.zscale, g.zscales.at[me_w], "wide", peer_w(d))

    def stat_copy(d):
        return remote("st", 0, g.stat, g.stats.at[me_n], "narrow", peer_n(d))

    def cot_copy(d):
        s = peer_n(d)
        return remote("ct", 0, g.cot_in.at[at(s, U)], g.cotrows.at[me_n], "narrow", s)

    def act_copy(d):
        s = peer_n(d)
        return remote("ac", 0, g.act.at[:, at(s, U)], g.actrows.at[me_n], "narrow", s)

    def ret_copy(p, d):
        peer, rows = peer_w(d), at(p, C // PARTS)
        return remote("gr", p, g.gsend.at[peer, rows], g.gret.at[me_w, rows], "wide", peer)

    def y_copy(p, d):
        s, rows = peer_n(d), at(p, C // PARTS)
        return remote("y", 0, g.y.at[rows, at(s, U)], g.yrows.at[me_n, rows], "narrow", s)

    def gh_copy(q, d):
        s = peer_n(d)
        return remote("gh", q, g.gh.at[rows_at(s * C + q * (C // 2), C // 2)], g.ghc.at[me_n, at(q, C // 2)], "narrow", s)

    def gf_copy(d):
        s = peer_n(d)
        return remote("gf", 0, g.gft.at[s], g.gf_out.at[me_n], "narrow", s)

    def bias_copy(name, src, dst, d):
        return remote(name, 0, src, dst.at[me_w], "wide", peer_w(d))

    def grad(k, suffix=""):
        return getattr(g, "g" + k + suffix)

    def core_rows(k, which):
        return (slice(None), at(which, grad(k).shape[1] // 2))

    def red_block(k, w):
        rows = grad(k).shape[1]
        size, down, lanes = z.red(rows)
        q = w // 2
        row = lax.rem(w, 2) * (rows // 2) + lax.rem(q, down) * size
        return (slice(None), rows_at(row, size), at(q // down, lanes))

    def out_rows(k, which):
        rows = grad(k).shape[1]
        if k == "c":
            return g.gc_sum.at[:, at(which, rows // 2)]
        return g.gn_out.at[:, rows_at(int(k[1]) * rows + which * (rows // 2), rows // 2)]

    def pair_start(k):
        remote("hs" + k, 0, grad(k).at[core_rows(k, 1 - core)], grad(k, "_half"), "wide", sibling).start()

    def reduce_pair(k):
        arrived("hs" + k, 0, grad(k, "_half"))
        own, mine = grad(k), core_rows(k, core)
        own[mine] = (own[mine].astype(F32) + grad(k, "_half")[...].astype(F32)).astype(BF16)

        def body(e):
            peer = across(2 * e)
            remote("rs" + k, 0, own.at[red_block(k, peer)], grad(k, "_in").at[me_w // 2], "wide", peer).start()

        loop(W // 2, body, 1)

    def reduce_sum(k):
        others = grad(k, "_in")
        arrived("rs" + k, 0, others.at[0 : W // 2 - 1])
        mine = red_block(k, me_w)
        total = lax.fori_loop(
            1, W // 2, lambda e, t: t + others[across(2 * e) // 2].astype(F32), grad(k)[mine].astype(F32), unroll=W <= 8
        )
        grad(k, "_sum")[mine] = total.astype(BF16)
        part = grad(k, "_sum").at[mine]
        loop(W // 2, lambda e: remote("ag" + k, 0, part, part, "wide", across(2 * e)).start(), 1)

    def gather_pass(k):
        arrived("ag" + k, 0, grad(k, "_in").at[0 : W // 2 - 1])
        part = grad(k, "_sum").at[core_rows(k, core)]
        remote("fw" + k, 0, part, out_rows(k, core), "wide", sibling).start()
        if k == "c":
            return None
        store = pltpu.make_async_copy(part, out_rows(k, core), g.store.at[SUMS.index(k)])
        store.start()
        return store

    def gather_wait(k):
        arrived("fw" + k, 0, out_rows(k, 1 - core))

    loads = [
        (g.feats_in, g.feats),
        (g.nw_in, g.nwfull.at[me_n]),
        (g.comb_in, g.wfull.at[me_n]),
        (g.slot_in, g.slot),
        (g.mask_in, g.mask),
        (g.visit_in, g.visit),
        (g.send_in, g.send),
        (g.cot_in, g.cot),
        (g.nb_in, g.nb),
        (g.cb_in, g.cb),
    ]

    def load(i):
        return pltpu.make_async_copy(loads[i][0], loads[i][1], g.load.at[i])

    barrier = pltpu.get_barrier_semaphore()
    loop(W, lambda d: pl.semaphore_signal(barrier, inc=1, device_id={"wide": peer_w(d)}, device_id_type=MESH), 1)
    loop(N, lambda d: pl.semaphore_signal(barrier, inc=1, device_id={"narrow": peer_n(d)}, device_id_type=MESH), 1)
    order = (6, 8, 3, 4, 5, 0, 1, 2, 7, 9)
    for i in order:
        load(i).start()
    pl.semaphore_wait(barrier, W - 1 + N - 1)
    share_send(0)
    load(8).wait()
    g.nbfull[me_n] = jnp.broadcast_to(g.nb[...].astype(F32).reshape(1, C), (8, C))
    loop(N, lambda d: nb_copy(d).start(), 1)

    for i in (3, 4, 5):
        load(i).wait()
    K = z.slots
    shift = CAP.bit_length() - 1

    def fill(i):
        rows = at(i, CH)
        g.code[rows, :] = jnp.zeros((CH, 128), I32)
        g.wts[rows, :] = jnp.zeros((CH, 128), F32)
        code = g.slot[:, rows].T
        g.code[rows, 0:K] = code
        g.code[rows, 64 : 64 + K] = code
        weight = (g.mask[:, rows] * g.visit[:, rows]).astype(F32).T
        g.wts[rows, 0:K] = weight
        g.wts[rows, 64 : 64 + K] = weight

    loop(R // CH, fill)

    lane = lax.broadcasted_iota(I32, (8, 128), 1)
    sub = lax.broadcasted_iota(I32, (8, 128), 0)
    half_lane = jnp.where(lane >= 64, 1, 0)
    place = [sub == 2 * j + half_lane for j in range(4)]
    place_b = [jnp.where(m, 1.0, 0.0) for m in place]
    place_b = [jnp.concatenate([m, m], axis=0).astype(BF16) for m in place_b]
    low_row = lax.broadcasted_iota(I32, (CAP, 128), 0).astype(F32).astype(BF16)

    def count_group(i):
        start = pl.multiple_of(i * 16, 16)
        outs = []
        for p in range(2):
            rows = pl.ds(pl.multiple_of(start + 8 * p, 8), 8)
            code, weight = g.code[rows, :], g.wts[rows, :]
            high, low = code >> shift, (code & (CAP - 1)).astype(F32)
            left = []
            for h in range(0, z.blocks, 2):
                pair = [jnp.where(high == h + q, weight, 0.0) for q in range(2)]
                pair = jnp.concatenate(pair, axis=0).astype(BF16)
                left.append(jnp.concatenate([pair * place_b[j] for j in range(4)], axis=1))
            left = jnp.concatenate(left, axis=0)
            right = []
            for j in range(4):
                row = jnp.sum(jnp.where(place[j], low, 0.0), axis=0, keepdims=True)
                row = jnp.broadcast_to(row.astype(BF16), (CAP, 128))
                right.append(jnp.where(low_row == row, jnp.ones((), BF16), jnp.zeros((), BF16)))
            outs.append(mm_nt(left, jnp.concatenate(right, axis=1)))
        for h in range(z.blocks):
            block = jnp.concatenate([out[h * 8 : h * 8 + 8] for out in outs], axis=0)
            top = block.astype(BF16)
            g.counts[h, pl.ds(start, 16), :] = top
            g.counts_lo[h, pl.ds(start, 16), :] = (block - top.astype(F32)).astype(BF16)

    UNROLL = 4
    groups = R // 16 // UNROLL

    def count_groups(first, last):
        def body(i):
            for q in range(UNROLL):
                count_group(i * UNROLL + q)

        loop(last, body, first)

    def hidden(s):
        def body(i):
            rows = at(i, CH)
            value = mm(g.feats[rows, :], g.nwfull[s]) + g.nbfull[s, 0:1, :]
            value = jnp.maximum(value, 0.0)
            top = value.astype(BF16)
            rest = (value - top.astype(F32)).astype(BF16)
            g.msg[rows, at(s, C)] = top
            weight = g.wfull[me_n, pl.ds(pl.multiple_of(D + s * C, C), C), :]
            g.zacc[rows, :] += mm(top, weight) + mm(rest, weight)

        sweep(R // CH, body)

    done = [0]

    def counts_until(last):
        last = groups * last // 16
        count_groups(done[0], last)
        done[0] = last

    def zero(i):
        g.zacc[at(i, CH), :] = jnp.zeros((CH, C), F32)

    loop(R // CH, zero)
    for i in (0, 1, 2):
        load(i).wait()
    hidden(me_n)
    counts_until(2)
    load(6).wait()
    g.send_t[...] = g.send[...].T

    def select(d):
        r = peer_w(d)
        which = lax.broadcasted_iota(I32, (CAP, W), 1)
        col = jnp.sum(jnp.where(which == r, g.send_t[...], 0), axis=1, keepdims=True)
        place_u = lax.broadcasted_iota(I32, (CAP, R), 1)
        g.sel[r] = jnp.where(place_u == col, 1.0, 0.0).astype(BF16)

    loop(W, select, 1)
    share_pass(0)
    loop(N, quarter_send, 1)
    counts_until(8)
    share_forward(0, 1)

    def take(d):
        arrived("sf0", d, g.nwfull.at[0, 0:half])
        hidden(behind_n(d))

    counts_until(10)
    share_forward(0, 2)
    loop(N, lambda d: cot_copy(d).start(), 1)
    arrived("nb", 0, g.nbfull.at[0 : N - 1])
    take(1)
    loop(N, functools.partial(share_forward, 0), 3)
    take(2)
    share_send(2)
    loop(N, take, 3)

    def column_max(i, most):
        return jnp.maximum(most, jnp.max(jnp.abs(g.zacc[at(i, CH), :]), axis=0, keepdims=True))

    most = lax.fori_loop(0, R // CH, column_max, jnp.full((1, C), 1e-30, F32))
    scale = most * (1.0 / 32766.0)
    g.zscale[...] = jnp.broadcast_to(scale, (8, C))
    loop(W, lambda d: zscale_copy(d).start(), 1)
    inv_scale = 1.0 / scale

    def code_z(i):
        rows = at(i, CH)
        whole = jnp.round(g.zacc[rows, :] * inv_scale)
        high = jnp.floor(whole * (1.0 / 256.0))
        g.zqa[rows, :] = high.astype(BF16)
        g.zqb[rows, :] = (whole - high * 256.0).astype(BF16)

    loop(R // CH, code_z)

    def send_z(d):
        peer = peer_w(d)
        picked = mm(g.sel[peer], g.zqa[...]) * 256.0 + mm(g.sel[peer], g.zqb[...])
        g.zsend[peer] = picked.astype(I32).astype(I16)
        z_copy(d).start()

    near = W // 4 + 1
    loop(near, send_z, 1)
    counts_until(12)
    loop(W, send_z, near)

    def split_z(i):
        rows = at(i, CH)
        value = g.zacc[rows, :]
        top = value.astype(BF16)
        g.zhi[rows, :] = top
        g.zlo[rows, :] = (value - top.astype(F32)).astype(BF16)

    loop(R // CH, split_z)
    counts_until(16)
    load(7).wait()
    load(9).wait()

    def own_part(i):
        rows = at(i, CH)
        value = mm(g.feats[rows, :], g.wfull[me_n, 0:D, :]) + g.cb[...].astype(F32).reshape(1, C)
        g.self_t[:, rows] = value.T
        g.cot_t[:, rows] = g.cot[rows, :].astype(F32).T
        total = jnp.zeros((CH, C), F32)
        for h in range(z.local):
            part = slice(h * CAP, (h + 1) * CAP)
            block = g.counts[h, rows, :]
            total += mm(block, g.zhi[part, :]) + mm(block, g.zlo[part, :]) + mm(g.counts_lo[h, rows, :], g.zhi[part, :])
        g.acc[rows, :] = total

    sweep(R // CH, own_part)
    ones = jnp.ones((16, 128), BF16)
    g.invs[...] = 2.0 / mm_nt(ones, g.wts[...].astype(BF16))

    def mine_t(i):
        cols = at(i, C)
        g.msg_t[cols, :] = g.msg[at(me_n, U), cols].astype(F32).T.astype(BF16)

    loop(D // C, mine_t)

    def take_z(d):
        s = peer_w(d)
        piece = min(32, CAP)
        for i in range(CAP // piece):
            rows = at(i, piece)
            value = g.ztab[s, rows, :].astype(I32).astype(F32) * g.zscales[s, 0:1, :]
            top = value.astype(BF16)
            g.thi[s, rows, :] = top
            g.tlo[s, rows, :] = (value - top.astype(F32)).astype(BF16)

    def pool(first, last):
        loop(last, take_z, first)

        def body(i):
            rows = at(i, CH)

            def add(d, total):
                s = peer_w(d)
                block = g.counts[z.local + s, rows, :]
                rest = g.counts_lo[z.local + s, rows, :]
                return total + mm(block, g.thi[s]) + mm(block, g.tlo[s]) + mm(rest, g.thi[s])

            g.acc[rows, :] = lax.fori_loop(first, last, add, g.acc[rows, :], unroll=W <= 8)

        return body

    arrived("zs", 0, g.zscales.at[0 : W - 1])
    for first_d, last_d in ((1, near), (W - 1, W)):
        loop(last_d, lambda d: z_copy(d).wait_recv(), first_d)
        sweep(R // CH, pool(first_d, last_d))
    loop(W - 1, lambda d: z_copy(d).wait_recv(), near)
    loop(N, quarter_pass, 1)
    pool_rest = pool(near, W - 1)

    def activate(i):
        pool_rest(i)
        rows = at(i, CH)
        pre = g.acc[rows, :].T * g.invs[0:1, rows] + g.self_t[:, rows]
        g.self_t[:, rows] = pre
        act = jnp.maximum(pre, 0.0)
        g.act[:, rows] = act.astype(BF16)
        squares = jnp.sum(act * act, axis=0, keepdims=True)
        inner = jnp.sum(act * g.cot_t[:, rows], axis=0, keepdims=True)
        g.stat[2 * i : 2 * i + 2, :] = jnp.concatenate([squares, inner], axis=0)

    sweep(R // CH, activate)
    loop(N, lambda d: stat_copy(d).start(), 1)
    pl.semaphore_signal(g.turn, inc=1, device_id={"wide": sibling}, device_id_type=MESH)
    g.actrows[me_n] = g.act[:, at(me_n, U)]
    pl.semaphore_wait(g.turn, 1)
    loop(N, lambda d: act_copy(d).start(), 1)
    arrived("st", 0, g.stats.at[0 : N - 1])
    g.stats[me_n] = g.stat[...]

    def norms(i):
        total = g.stats[0, 2 * i : 2 * i + 2, :]
        for s in range(1, N):
            total += g.stats[s, 2 * i : 2 * i + 2, :]
        return lax.rsqrt(total[0:1] / D + EPSILON), total[1:2]

    def grad_act(i):
        rows = at(i, CH)
        inv, inner = norms(i)
        pre = g.self_t[:, rows]
        act = jnp.maximum(pre, 0.0)
        grad = g.cot_t[:, rows] * inv - act * (inner * (inv * inv * inv) / D)
        grad = jnp.where(pre > 0, grad, 0.0)
        g.gp[:, rows] = grad.astype(BF16)
        g.gps[:, rows] = (grad * g.invs[0:1, rows]).astype(BF16)

    sweep(R // CH, grad_act)

    def send_ret(d):
        peer = peer_w(d)
        g.gsend[peer] = mm(g.gps[...], g.counts[z.local + peer]).astype(BF16)
        ret_copy(0, d).start()

    loop(W, send_ret, 1)

    def more_ret(p):
        loop(W, lambda d: ret_copy(p, d).start(), 1)

    more_ret(1)
    more_ret(2)
    join = max(1, 128 // CAP)
    for h in range(0, z.local, join):
        parts = [mm(g.gps[...], g.counts[h + q]) for q in range(join)]
        parts = jnp.concatenate(parts, axis=1) if join > 1 else parts[0]
        g.yacc[:, h * CAP : (h + join) * CAP] = parts

    def embed(i):
        rows = at(i, CH)
        inv, _ = norms(i)
        value = jnp.maximum(g.self_t[:, rows], 0.0) * inv
        g.emb[rows, :] = value.T.astype(BF16)

    sweep(R // CH, embed)
    emb_store = pltpu.make_async_copy(g.emb, g.emb_out, g.store.at[4])
    emb_store.start()
    more_ret(3)

    LW = min(512, D)

    def grad_self(i):
        lanes = at(i, LW)
        g.gc[0, :, lanes] = mm(g.gp[...], g.feats[:, lanes]).astype(BF16)

    sweep(D // LW, grad_self)
    ones_r = jnp.ones((8, R), BF16)
    g.gcb[...] = mm_nt(ones_r, g.gp[...])


    def take_ret(p):
        part = at(p, C // PARTS)
        arrived("gr", p, g.gret.at[0 : W - 1, part])

        def body(i):
            lanes = at(i, CH)

            def add(d, total):
                s = peer_w(d)
                return total + mm(g.gret[s, part, :], g.sel[s, :, lanes])

            total = lax.fori_loop(1, W, add, g.yacc[part, lanes], unroll=W <= 8)
            g.y[part, lanes] = total.astype(BF16)

        sweep(R // CH, body)
        loop(N, lambda d: y_copy(p, d).start(), 1)

    take_ret(0)
    loop(N, quarter_forward, 1)
    share_pass(2)
    for p in range(1, PARTS):
        take_ret(p)
    g.yrows[me_n] = g.y[:, at(me_n, U)]

    def grad_pool(i):
        lanes = at(i, LW)
        g.gc[1, :, lanes] = mm(g.y[...], g.msg[:, lanes]).astype(BF16)

    sweep(D // LW, grad_pool)
    loop(W, lambda d: bias_copy("bc", g.gcb, g.gcb_in, d).start(), 1)
    pair_start("c")

    reduce_pair("c")
    arrived("ct", 0, g.cotrows.at[0 : N - 1])
    g.cotrows[me_n] = g.cot[at(me_n, U), :]
    for s in range(N):
        g.cotrows_t[s] = g.cotrows[s].astype(F32).T
    arrived("sf1", 0, g.wfull.at[0 : N - 1, 0:half])
    arrived("y", 0, g.yrows.at[0 : N - 1])

    def hidden_rows(i):
        rows = at(i, CH)
        wrows = slice(D + i * CH, D + (i + 1) * CH)
        total = jnp.zeros((CH, U), F32)
        for s in range(N):
            total += mm(g.wfull[s, wrows, :], g.yrows[s])
        g.gh[rows, :] = jnp.where(g.msg_t[rows, :] > 0, total, 0.0).astype(BF16)

    sweep(D // CH, hidden_rows)
    loop(N, lambda d: gh_copy(0, d).start(), 1)
    g.ghc[me_n] = g.gh[at(me_n, C), :]

    def feature_rows(i):
        rows = at(i, C)
        total = jnp.zeros((C, U), F32)
        for s in range(N):
            total += mm(g.wfull[s, rows, :], g.gprows[s]) + mm(g.nwfull[s, rows, :], g.gh[s * C : (s + 1) * C, :])
        g.gft[i] = total.T.astype(BF16)

    loop(N, functools.partial(share_forward, 2), 1)
    arrived("ac", 0, g.actrows.at[0 : N - 1])
    per = CH // U
    lanes = at(lax.rem(me_n, per), U) if per > 1 else slice(None)
    total = g.stats[0, :, lanes]
    for s in range(1, N):
        total += g.stats[s, :, lanes]
    row = lax.broadcasted_iota(I32, total.shape, 0) - 2 * (me_n // per)
    inv = lax.rsqrt(jnp.sum(jnp.where(row == 0, total, 0.0), axis=0, keepdims=True) / D + EPSILON)
    inner = jnp.sum(jnp.where(row == 1, total, 0.0), axis=0, keepdims=True)
    factor = inner * (inv * inv * inv) / D
    for s in range(N):
        act = g.actrows[s].astype(F32)
        grad_rows = jnp.where(act > 0, g.cotrows_t[s] * inv - act * factor, 0.0)
        g.gprows[s] = grad_rows.astype(BF16)
    arrived("sf2", 0, g.wfull.at[0 : N - 1, 0:half])
    loop(N, lambda d: gh_copy(1, d).start(), 1)
    sweep(N, feature_rows)
    gf_store = pltpu.make_async_copy(g.gft.at[me_n], g.gf_out.at[me_n], g.store.at[3])
    gf_store.start()

    reduce_sum("c")

    def grad_neigh(q):
        rows = at(q, C // 2)
        out = (g.gn0, g.gn1)[q]

        def body(i):
            lanes = at(i, LW)
            total = jnp.zeros((C // 2, LW), F32)
            for s in range(N):
                total += mm(g.ghc[s, rows, :], g.feats[s * U : (s + 1) * U, lanes])
            out[0, :, lanes] = total.astype(BF16)

        sweep(D // LW, body)

    arrived("gh", 0, g.ghc.at[0 : N - 1, 0 : C // 2])
    grad_neigh(0)
    pair_start("n0")
    arrived("gh", 1, g.ghc.at[0 : N - 1, 0 : C // 2])
    loop(N, lambda d: gf_copy(d).start(), 1)
    reduce_pair("n0")
    grad_neigh(1)
    pair_start("n1")
    total = jnp.zeros((8, C), F32)
    ones_u = jnp.ones((8, U), BF16)
    for s in range(N):
        total += mm_nt(ones_u, g.ghc[s])
    g.gnb[...] = total
    loop(W, lambda d: bias_copy("bn", g.gnb, g.gnb_in, d).start(), 1)
    reduce_pair("n1")
    reduce_sum("n0")
    def bias_sum(name, own, others):
        arrived(name, 0, others.at[0 : W - 1])
        left(name, others.at[0 : W - 1])
        own[...] = lax.fori_loop(1, W, lambda d, total: total + others[peer_w(d)], own[...])

    bias_sum("bc", g.gcb, g.gcb_in)
    bias_sum("bn", g.gnb, g.gnb_in)
    gcb_store = pltpu.make_async_copy(g.gcb, g.gcb_out, g.store.at[5])
    gnb_store = pltpu.make_async_copy(g.gnb, g.gnb_out, g.store.at[6])
    gcb_store.start()
    gnb_store.start()
    gather_pass("c")
    reduce_sum("n1")
    gn0_store = gather_pass("n0")
    gn1_store = gather_pass("n1")
    gather_wait("c")
    for p in range(2):
        for i in range(D // CH):
            g.gct[p, at(i, CH), :] = g.gc_sum[p, :, at(i, CH)].astype(F32).T.astype(BF16)
    gc_store = pltpu.make_async_copy(g.gct, g.gc_out, g.store.at[0])
    gc_store.start()
    for k in SUMS[1:]:
        gather_wait(k)
    arrived("gf", 0, g.gf_out.at[0 : N - 1])

    for k in (0, 2):
        left("sh%d" % k, fulls[k].at[0 : N - 1, 0:part_w])
        left("sp%d" % k, fulls[k].at[0 : N - 1, 0 : (W // 2 - 1) * part_w])
        left("sf%d" % k, fulls[k].at[0 : N - 1, 0:half])
    left("sh1", g.wfull.at[0 : N - 1, 0 : 2 * eighth])
    left("sp1", g.wfull.at[0 : N - 1, 0 : 2 * eighth])
    left("sf1", g.wfull.at[0 : N - 1, 0:half])
    left("nb", g.nbfull.at[0 : N - 1])
    left("z", g.zsend.at[0 : W - 1])
    left("zs", g.zscales.at[0 : W - 1])
    left("st", g.stats.at[0 : N - 1])
    left("ct", g.cotrows.at[0 : N - 1])
    left("ac", g.actrows.at[0 : N - 1])
    left("gr", g.gsend.at[0 : W - 1])
    left("y", g.yrows.at[0 : N - 1])
    left("gh", g.ghc.at[0 : N - 1])
    left("gf", g.gf_out.at[0 : N - 1])
    for k in SUMS:
        left("hs" + k, grad(k, "_half"))
        left("rs" + k, grad(k, "_in").at[0 : W // 2 - 1])
        left("ag" + k, grad(k, "_in").at[0 : W // 2 - 1])
        left("fw" + k, grad(k, "_sum").at[core_rows(k, core)])
    for store in (emb_store, gf_store, gc_store, gcb_store, gnb_store, gn0_store, gn1_store):
        store.wait()


def finish(z, *refs):
    names = ["emb", "gf", "gn", "gc", "gnb", "gcb"]
    ins = dict(zip(names, refs[:6]))
    outs = dict(zip(names, refs[6:12]))
    emb, gf, gn, gc, nb, cb, gf_t, gn_t, gc_t, nb_t, cb_t, load, store = refs[12:]
    D, C, N, U = z.width, z.cols, z.narrow, z.part
    step = D // N
    emb_load = pltpu.make_async_copy(ins["emb"], emb, load.at[6])
    emb_load.start()
    jobs = [
        (ins["gn"].at[0], gn, [(gn.at[:, at(i, step)], gn_t.at[at(i, step)], outs["gn"].at[at(i, step)]) for i in range(N)]),
        (ins["gf"], gf, [(gf.at[i], gf_t.at[at(i, U)], outs["gf"].at[at(i, U)]) for i in range(N)]),
    ]
    for p in range(2):
        parts = [(gc.at[p, at(i, step)], gc_t.at[p, at(i, step)], outs["gc"].at[p, at(i, step)]) for i in range(N)]
        jobs.append((ins["gc"].at[p], gc.at[p], parts))
    loads = [pltpu.make_async_copy(src, held, load.at[i]) for i, (src, held, _) in enumerate(jobs)]
    small = (("gnb", nb, nb_t), ("gcb", cb, cb_t))
    loads += [pltpu.make_async_copy(ins[k], held, load.at[4 + i]) for i, (k, held, _) in enumerate(small)]
    for copy in loads:
        copy.start()
    stores = [pltpu.make_async_copy(emb, outs["emb"], store.at[0])]

    def keep(src, dst):
        stores.append(pltpu.make_async_copy(src, dst, store.at[len(stores)]))
        stores[-1].start()

    for i, (_, _, parts) in enumerate(jobs):
        loads[i].wait()
        for k, (part, turned, out) in enumerate(parts):
            turned[...] = part[...].astype(F32).T if i == 0 else part[...].astype(F32)
            keep(turned, out)
        if i == 0:
            emb_load.wait()
            stores[0].start()
    for i, (k, held, turned) in enumerate(small):
        loads[4 + i].wait()
        turned[...] = held[0:1, :]
        keep(turned, outs[k])
    for copy in stores:
        copy.wait()


def shards(wide, narrow, node_feats, neigh_weight, neigh_bias, combine_weight, combine_bias, cotangent,
           neighbour_slot, neighbour_mask, visit_count, send_rows):
    z = Sizes(node_feats, neigh_weight, send_rows, neighbour_slot.T, wide, narrow)
    R, D, C, W, N, U = z.rows, z.width, z.cols, z.wide, z.narrow, z.part
    bufs, sems, kinds = scratch(z)
    names = NAMES_IN + NAMES_OUT + list(bufs) + list(sems)
    outs = (
        jax.ShapeDtypeStruct((R, C), BF16),
        jax.ShapeDtypeStruct((N, U, C), BF16),
        jax.ShapeDtypeStruct((1, C, D), BF16),
        jax.ShapeDtypeStruct((2, D, C), BF16),
        jax.ShapeDtypeStruct((8, C), F32),
        jax.ShapeDtypeStruct((8, C), F32),
    )
    emb, gf, gn, gc, gnb, gcb = pl.pallas_call(
        functools.partial(kernel, z, names, kinds),
        out_shape=outs,
        in_specs=[pl.BlockSpec(memory_space=pl.ANY)] * len(NAMES_IN),
        out_specs=[pl.BlockSpec(memory_space=pl.ANY)] * len(NAMES_OUT),
        scratch_shapes=list(bufs.values()) + list(sems.values()),
        compiler_params=pltpu.CompilerParams(
            collective_id=0, has_side_effects=True, vmem_limit_bytes=60 * 2**20
        ),
        cost_estimate=pl.CostEstimate(flops=2 * 10**10, bytes_accessed=2 * 10**7, transcendentals=0),
        name="layer",
    )(
        node_feats, neigh_weight, neigh_bias, combine_weight, combine_bias, cotangent,
        neighbour_slot.T, neighbour_mask.T, visit_count.T, send_rows,
    )
    hbm = pl.BlockSpec(memory_space=pl.ANY)
    emb, grad_features, grad_neigh, grad_combine, gnb, gcb = pl.pallas_call(
        functools.partial(finish, z),
        out_shape=(
            jax.ShapeDtypeStruct((R, C), BF16),
            jax.ShapeDtypeStruct((R, C), F32),
            jax.ShapeDtypeStruct((D, C), F32),
            jax.ShapeDtypeStruct((2, D, C), F32),
            jax.ShapeDtypeStruct((1, C), F32),
            jax.ShapeDtypeStruct((1, C), F32),
        ),
        in_specs=[hbm] * 6,
        out_specs=[hbm] * 6,
        scratch_shapes=[
            pltpu.VMEM((R, C), BF16),
            pltpu.VMEM((N, U, C), BF16),
            pltpu.VMEM((C, D), BF16),
            pltpu.VMEM((2, D, C), BF16),
            pltpu.VMEM((8, C), F32),
            pltpu.VMEM((8, C), F32),
            pltpu.VMEM((R, C), F32),
            pltpu.VMEM((D, C), F32),
            pltpu.VMEM((2, D, C), F32),
            pltpu.VMEM((1, C), F32),
            pltpu.VMEM((1, C), F32),
            pltpu.SemaphoreType.DMA((7,)),
            pltpu.SemaphoreType.DMA((4 * N + 3,)),
        ],
        compiler_params=pltpu.CompilerParams(vmem_limit_bytes=60 * 2**20),
        name="finish",
    )(emb, gf, gn, gc, gnb, gcb)
    return emb, grad_features, grad_neigh, gnb.reshape(C), grad_combine.reshape(2 * D, C), gcb.reshape(C)


def solution(mesh):
    placed = (
        P("wide", None),
        P(None, "narrow"),
        P("narrow"),
        P(None, "narrow"),
        P("narrow"),
        P("wide", "narrow"),
        P("wide", None),
        P("wide", None),
        P("wide", None),
        P("wide", None),
    )
    return jax.shard_map(
        functools.partial(shards, mesh.shape["wide"], mesh.shape["narrow"]),
        mesh=mesh,
        in_specs=placed,
        out_specs=(
            P("wide", "narrow"),
            P("wide", "narrow"),
            P(None, "narrow"),
            P("narrow"),
            P(None, "narrow"),
            P("narrow"),
        ),
        check_vma=False,
    )
```

```python
import functools

import jax
import jax.numpy as jnp
from jax import lax
from jax.experimental import pallas as pl
from jax.experimental.pallas import tpu as pltpu
from jax.sharding import PartitionSpec as P

EPSILON = 1e-06
PARTS = 4
SUMS = ("c", "n0", "n1")
F32 = jnp.float32
BF16 = jnp.bfloat16
I32 = jnp.int32
I16 = jnp.int16
MESH = pl.DeviceIdType.MESH


def mm(left, right):
    return jnp.dot(left, right, preferred_element_type=F32)


def mm_nt(left, right):
    return lax.dot_general(left, right, (((1,), (1,)), ((), ())), preferred_element_type=F32)


def at(index, size):
    if isinstance(index, int):
        return slice(index * size, (index + 1) * size)
    return pl.ds(pl.multiple_of(index * size, size), size)


class Sizes:
    def __init__(self, feats, neigh, send, slot, wide, narrow):
        self.rows, self.width = feats.shape
        self.cols = neigh.shape[1]
        self.cap = send.shape[1]
        self.slots = slot.shape[0]
        self.wide, self.narrow = wide, narrow
        self.chunk = min(256, self.rows)
        self.part = self.rows // narrow
        self.local = self.rows // self.cap
        self.blocks = self.local + wide
        self.pairs = wide // 2

    def red(self, rows):
        size = max(16, rows // 2 // self.pairs)
        down = rows // 2 // size
        return size, down, self.width * down // self.pairs


NAMES_IN = ["feats_in", "nw_in", "nb_in", "comb_in", "cb_in", "cot_in", "slot_in", "mask_in", "visit_in", "send_in"]
NAMES_OUT = ["emb_out", "gf_out", "gn_out", "gc_out", "gnb_out", "gcb_out"]


def scratch(z):
    R, D, C, W, N, U, CAP = z.rows, z.width, z.cols, z.wide, z.narrow, z.part, z.cap
    v = lambda *shape: pltpu.VMEM(shape[:-1], shape[-1])
    bufs = dict(
        feats=v(R, D, BF16),
        nwfull=v(N, D, C, BF16),
        nbfull=v(N, 8, C, F32),
        nb=v(C, BF16),
        cb=v(C, BF16),
        wfull=v(N, 2 * D, C, BF16),
        cot=v(R, C, BF16),
        slot=v(z.slots, R, I32),
        mask=v(z.slots, R, I32),
        visit=v(z.slots, R, I32),
        send=v(W, CAP, I32),
        send_t=v(CAP, W, I32),
        code=v(R, 128, I32),
        wts=v(R, 128, F32),
        counts=v(z.blocks, R, CAP, BF16),
        counts_lo=v(z.blocks, R, CAP, BF16),
        sel=v(W, CAP, R, BF16),
        msg=v(R, D, BF16),
        zacc=v(R, C, F32),
        zhi=v(R, C, BF16),
        zlo=v(R, C, BF16),
        zqa=v(R, C, BF16),
        zqb=v(R, C, BF16),
        zscale=v(8, C, F32),
        thi=v(W, CAP, C, BF16),
        tlo=v(W, CAP, C, BF16),
        zscales=v(W, 8, C, F32),
        zsend=v(W, CAP, C, I16),
        ztab=v(W, CAP, C, I16),
        acc=v(R, C, F32),
        self_t=v(C, R, F32),
        cot_t=v(C, R, F32),
        invs=v(16, R, F32),
        stat=v(2 * (R // z.chunk), z.chunk, F32),
        stats=v(N, 2 * (R // z.chunk), z.chunk, F32),
        emb=v(R, C, BF16),
        gp=v(C, R, BF16),
        gps=v(C, R, BF16),
        act=v(C, R, BF16),
        actrows=v(N, C, U, BF16),
        cotrows=v(N, U, C, BF16),
        cotrows_t=v(N, C, U, F32),
        gprows=v(N, C, U, BF16),
        gsend=v(W, C, CAP, BF16),
        gret=v(W, C, CAP, BF16),
        yacc=v(C, R, F32),
        y=v(C, R, BF16),
        yrows=v(N, C, U, BF16),
        msg_t=v(D, U, BF16),
        gh=v(D, U, BF16),
        ghc=v(N, C, U, BF16),
        gft=v(N, U, C, BF16),
        gct=v(2, D, C, BF16),
        gc=v(2, C, D, BF16),
        gc_half=v(2, C // 2, D, BF16),
        gc_in=v(W // 2, 2, z.red(C)[0], z.red(C)[2], BF16),
        gc_sum=v(2, C, D, BF16),
        gn0=v(1, C // 2, D, BF16),
        gn0_half=v(1, C // 4, D, BF16),
        gn0_in=v(W // 2, 1, z.red(C // 2)[0], z.red(C // 2)[2], BF16),
        gn0_sum=v(1, C // 2, D, BF16),
        gn1=v(1, C // 2, D, BF16),
        gn1_half=v(1, C // 4, D, BF16),
        gn1_in=v(W // 2, 1, z.red(C // 2)[0], z.red(C // 2)[2], BF16),
        gn1_sum=v(1, C // 2, D, BF16),
        gcb=v(8, C, F32),
        gcb_in=v(W, 8, C, F32),
        gnb=v(8, C, F32),
        gnb_in=v(W, 8, C, F32),
    )
    kinds = dict(
        sh0=N, sh1=N, sh2=N, sp0=N, sp1=N, sp2=N, sf0=N, sf1=1, sf2=1, nb=1, st=1, ct=1, ac=1, y=1, gh=2, gf=1,
        z=W, zs=1, gr=PARTS, bc=1, bn=1,
    )
    for k in SUMS:
        kinds.update({"hs" + k: 1, "rs" + k: 1, "ag" + k: 1, "fw" + k: 1})
    sems = {name + "_r": pltpu.SemaphoreType.DMA((count,)) for name, count in kinds.items()}
    sems["turn"] = pltpu.SemaphoreType.REGULAR
    sems["sent"] = pltpu.SemaphoreType.DMA((len(kinds),))
    sems["load"] = pltpu.SemaphoreType.DMA((10,))
    sems["store"] = pltpu.SemaphoreType.DMA((7,))
    return bufs, sems, list(kinds)


class Refs:
    pass


def kernel(z, names, kinds, *refs):
    g = Refs()
    for name, ref in zip(names, refs):
        setattr(g, name, ref)
    R, D, C, W, N, U, CAP = z.rows, z.width, z.cols, z.wide, z.narrow, z.part, z.cap
    CH = z.chunk
    half = D // 2
    me_w, me_n = lax.axis_index("wide"), lax.axis_index("narrow")
    core = lax.rem(me_w, 2)
    sibling = me_w + 1 - 2 * core

    def loop(count, body, start=0):
        def step(i, carry):
            body(i)
            return carry

        lax.fori_loop(start, count, step, 0)

    def sweep(count, body):
        for i in range(count):
            body(i)

    def flip(me, e, size):
        peer, bit = 0, 1
        while bit < size:
            peer = peer + bit * lax.rem(me // bit + e // bit, 2)
            bit *= 2
        return peer

    def peer_n(d):
        return flip(me_n, N - d, N)

    def peer_w(d):
        return flip(me_w, W - d, W)

    def ahead_n(d):
        return lax.rem(me_n + d, N)

    def behind_n(d):
        return lax.rem(me_n - d + N, N)

    def across(e):
        return flip(me_w, e, W)

    def remote(name, index, src, dst, axis="narrow", peer=0):
        return pltpu.make_async_remote_copy(
            src_ref=src,
            dst_ref=dst,
            send_sem=g.sent.at[kinds.index(name)],
            recv_sem=getattr(g, name + "_r").at[index],
            device_id={axis: peer},
            device_id_type=MESH,
        )

    def arrived(name, index, ref):
        remote(name, index, ref, ref, "narrow", peer_n(1)).wait_recv()

    def left(name, ref):
        remote(name, 0, ref, ref, "narrow", peer_n(1)).wait_send()

    def rows_at(start, size):
        return pl.ds(pl.multiple_of(start, size), size)

    sources = (g.nw_in, None, g.comb_in)
    fulls = (g.nwfull, None, g.wfull)
    part_w = D // W

    def share():
        return rows_at((core * (W // 2) + me_w // 2) * part_w, part_w)

    def share_send(k):
        def body(d):
            remote("sh%d" % k, d, sources[k].at[share()], fulls[k].at[me_n, share()], "narrow", ahead_n(d)).start()

        loop(N, body, 1)

    def share_pass(k):
        def body(d):
            part = fulls[k].at[behind_n(d), share()]
            arrived("sh%d" % k, d, part)
            loop(W // 2, lambda e: remote("sp%d" % k, d, part, part, "wide", across(2 * e)).start(), 1)

        loop(N, body, 1)

    def share_forward(k, d):
        s = behind_n(d)
        arrived("sp%d" % k, d, fulls[k].at[s, 0 : (W // 2 - 1) * part_w])
        part = fulls[k].at[s, rows_at(core * half, half)]
        remote("sf%d" % k, d if k == 0 else 0, part, part, "wide", sibling).start()

    hops = (2, 4)
    eighth = D // 8

    def hop_bit(h):
        return lax.rem(me_w // hops[h], 2)

    def quarter(h):
        return rows_at(D + h * half + (2 * core + hop_bit(h)) * eighth, eighth)

    def quarter_send(d):
        for h in range(2):
            mine = quarter(h)
            remote("sh1", d, g.comb_in.at[mine], g.wfull.at[me_n, mine], "narrow", ahead_n(d)).start()

    def quarter_pass(d):
        s = behind_n(d)
        arrived("sh1", d, g.wfull.at[s, 0 : 2 * eighth])
        for h in range(2):
            part = g.wfull.at[s, quarter(h)]
            remote("sp1", d, part, part, "wide", me_w + hops[h] - 2 * hops[h] * hop_bit(h)).start()

    def quarter_forward(d):
        s = behind_n(d)
        arrived("sp1", d, g.wfull.at[s, 0 : 2 * eighth])
        for h in range(2):
            part = g.wfull.at[s, rows_at(D + h * half + 2 * core * eighth, 2 * eighth)]
            remote("sf1", 0, part, part, "wide", sibling).start()

    def nb_copy(d):
        return remote("nb", 0, g.nbfull.at[me_n], g.nbfull.at[me_n], "narrow", peer_n(d))

    def z_copy(d):
        peer = peer_w(d)
        return remote("z", d, g.zsend.at[peer], g.ztab.at[me_w], "wide", peer)

    def zscale_copy(d):
        return remote("zs", 0, g.zscale, g.zscales.at[me_w], "wide", peer_w(d))

    def stat_copy(d):
        return remote("st", 0, g.stat, g.stats.at[me_n], "narrow", peer_n(d))

    def cot_copy(d):
        s = peer_n(d)
        return remote("ct", 0, g.cot_in.at[at(s, U)], g.cotrows.at[me_n], "narrow", s)

    def act_copy(d):
        s = peer_n(d)
        return remote("ac", 0, g.act.at[:, at(s, U)], g.actrows.at[me_n], "narrow", s)

    def ret_copy(p, d):
        peer, rows = peer_w(d), at(p, C // PARTS)
        return remote("gr", p, g.gsend.at[peer, rows], g.gret.at[me_w, rows], "wide", peer)

    def y_copy(p, d):
        s, rows = peer_n(d), at(p, C // PARTS)
        return remote("y", 0, g.y.at[rows, at(s, U)], g.yrows.at[me_n, rows], "narrow", s)

    def gh_copy(q, d):
        s = peer_n(d)
        return remote("gh", q, g.gh.at[rows_at(s * C + q * (C // 2), C // 2)], g.ghc.at[me_n, at(q, C // 2)], "narrow", s)

    def gf_copy(d):
        s = peer_n(d)
        return remote("gf", 0, g.gft.at[s], g.gf_out.at[me_n], "narrow", s)

    def bias_copy(name, src, dst, d):
        return remote(name, 0, src, dst.at[me_w], "wide", peer_w(d))

    def grad(k, suffix=""):
        return getattr(g, "g" + k + suffix)

    def core_rows(k, which):
        return (slice(None), at(which, grad(k).shape[1] // 2))

    def red_block(k, w):
        rows = grad(k).shape[1]
        size, down, lanes = z.red(rows)
        q = w // 2
        row = lax.rem(w, 2) * (rows // 2) + lax.rem(q, down) * size
        return (slice(None), rows_at(row, size), at(q // down, lanes))

    def out_rows(k, which):
        rows = grad(k).shape[1]
        if k == "c":
            return g.gc_sum.at[:, at(which, rows // 2)]
        return g.gn_out.at[:, rows_at(int(k[1]) * rows + which * (rows // 2), rows // 2)]

    def pair_start(k):
        remote("hs" + k, 0, grad(k).at[core_rows(k, 1 - core)], grad(k, "_half"), "wide", sibling).start()

    def reduce_pair(k):
        arrived("hs" + k, 0, grad(k, "_half"))
        own, mine = grad(k), core_rows(k, core)
        own[mine] = (own[mine].astype(F32) + grad(k, "_half")[...].astype(F32)).astype(BF16)

        def body(e):
            peer = across(2 * e)
            remote("rs" + k, 0, own.at[red_block(k, peer)], grad(k, "_in").at[me_w // 2], "wide", peer).start()

        loop(W // 2, body, 1)

    def reduce_sum(k):
        others = grad(k, "_in")
        arrived("rs" + k, 0, others.at[0 : W // 2 - 1])
        mine = red_block(k, me_w)
        total = lax.fori_loop(
            1, W // 2, lambda e, t: t + others[across(2 * e) // 2].astype(F32), grad(k)[mine].astype(F32), unroll=W <= 8
        )
        grad(k, "_sum")[mine] = total.astype(BF16)
        part = grad(k, "_sum").at[mine]
        loop(W // 2, lambda e: remote("ag" + k, 0, part, part, "wide", across(2 * e)).start(), 1)

    def gather_pass(k):
        arrived("ag" + k, 0, grad(k, "_in").at[0 : W // 2 - 1])
        part = grad(k, "_sum").at[core_rows(k, core)]
        remote("fw" + k, 0, part, out_rows(k, core), "wide", sibling).start()
        if k == "c":
            return None
        store = pltpu.make_async_copy(part, out_rows(k, core), g.store.at[SUMS.index(k)])
        store.start()
        return store

    def gather_wait(k):
        arrived("fw" + k, 0, out_rows(k, 1 - core))

    loads = [
        (g.feats_in, g.feats),
        (g.nw_in, g.nwfull.at[me_n]),
        (g.comb_in, g.wfull.at[me_n]),
        (g.slot_in, g.slot),
        (g.mask_in, g.mask),
        (g.visit_in, g.visit),
        (g.send_in, g.send),
        (g.cot_in, g.cot),
        (g.nb_in, g.nb),
        (g.cb_in, g.cb),
    ]

    def load(i):
        return pltpu.make_async_copy(loads[i][0], loads[i][1], g.load.at[i])

    barrier = pltpu.get_barrier_semaphore()
    loop(W, lambda d: pl.semaphore_signal(barrier, inc=1, device_id={"wide": peer_w(d)}, device_id_type=MESH), 1)
    loop(N, lambda d: pl.semaphore_signal(barrier, inc=1, device_id={"narrow": peer_n(d)}, device_id_type=MESH), 1)
    order = (6, 8, 3, 4, 5, 0, 1, 2, 7, 9)
    for i in order:
        load(i).start()
    pl.semaphore_wait(barrier, W - 1 + N - 1)
    share_send(0)
    load(8).wait()
    g.nbfull[me_n] = jnp.broadcast_to(g.nb[...].astype(F32).reshape(1, C), (8, C))
    loop(N, lambda d: nb_copy(d).start(), 1)

    for i in (3, 4, 5):
        load(i).wait()
    K = z.slots
    shift = CAP.bit_length() - 1

    def fill(i):
        rows = at(i, CH)
        g.code[rows, :] = jnp.zeros((CH, 128), I32)
        g.wts[rows, :] = jnp.zeros((CH, 128), F32)
        code = g.slot[:, rows].T
        g.code[rows, 0:K] = code
        g.code[rows, 64 : 64 + K] = code
        weight = (g.mask[:, rows] * g.visit[:, rows]).astype(F32).T
        g.wts[rows, 0:K] = weight
        g.wts[rows, 64 : 64 + K] = weight

    loop(R // CH, fill)

    lane = lax.broadcasted_iota(I32, (8, 128), 1)
    sub = lax.broadcasted_iota(I32, (8, 128), 0)
    half_lane = jnp.where(lane >= 64, 1, 0)
    place = [sub == 2 * j + half_lane for j in range(4)]
    place_b = [jnp.where(m, 1.0, 0.0) for m in place]
    place_b = [jnp.concatenate([m, m], axis=0).astype(BF16) for m in place_b]
    low_row = lax.broadcasted_iota(I32, (CAP, 128), 0).astype(F32).astype(BF16)

    def count_group(i):
        start = pl.multiple_of(i * 16, 16)
        outs = []
        for p in range(2):
            rows = pl.ds(pl.multiple_of(start + 8 * p, 8), 8)
            code, weight = g.code[rows, :], g.wts[rows, :]
            high, low = code >> shift, (code & (CAP - 1)).astype(F32)
            left = []
            for h in range(0, z.blocks, 2):
                pair = [jnp.where(high == h + q, weight, 0.0) for q in range(2)]
                pair = jnp.concatenate(pair, axis=0).astype(BF16)
                left.append(jnp.concatenate([pair * place_b[j] for j in range(4)], axis=1))
            left = jnp.concatenate(left, axis=0)
            right = []
            for j in range(4):
                row = jnp.sum(jnp.where(place[j], low, 0.0), axis=0, keepdims=True)
                row = jnp.broadcast_to(row.astype(BF16), (CAP, 128))
                right.append(jnp.where(low_row == row, jnp.ones((), BF16), jnp.zeros((), BF16)))
            outs.append(mm_nt(left, jnp.concatenate(right, axis=1)))
        for h in range(z.blocks):
            block = jnp.concatenate([out[h * 8 : h * 8 + 8] for out in outs], axis=0)
            top = block.astype(BF16)
            g.counts[h, pl.ds(start, 16), :] = top
            g.counts_lo[h, pl.ds(start, 16), :] = (block - top.astype(F32)).astype(BF16)

    UNROLL = 4
    groups = R // 16 // UNROLL

    def count_groups(first, last):
        def body(i):
            for q in range(UNROLL):
                count_group(i * UNROLL + q)

        loop(last, body, first)

    def hidden(s):
        def body(i):
            rows = at(i, CH)
            value = mm(g.feats[rows, :], g.nwfull[s]) + g.nbfull[s, 0:1, :]
            value = jnp.maximum(value, 0.0)
            top = value.astype(BF16)
            rest = (value - top.astype(F32)).astype(BF16)
            g.msg[rows, at(s, C)] = top
            weight = g.wfull[me_n, pl.ds(pl.multiple_of(D + s * C, C), C), :]
            g.zacc[rows, :] += mm(top, weight) + mm(rest, weight)

        sweep(R // CH, body)

    done = [0]

    def counts_until(last):
        last = groups * last // 16
        count_groups(done[0], last)
        done[0] = last

    def zero(i):
        g.zacc[at(i, CH), :] = jnp.zeros((CH, C), F32)

    loop(R // CH, zero)
    for i in (0, 1, 2):
        load(i).wait()
    hidden(me_n)
    counts_until(2)
    load(6).wait()
    g.send_t[...] = g.send[...].T

    def select(d):
        r = peer_w(d)
        which = lax.broadcasted_iota(I32, (CAP, W), 1)
        col = jnp.sum(jnp.where(which == r, g.send_t[...], 0), axis=1, keepdims=True)
        place_u = lax.broadcasted_iota(I32, (CAP, R), 1)
        g.sel[r] = jnp.where(place_u == col, 1.0, 0.0).astype(BF16)

    loop(W, select, 1)
    share_pass(0)
    loop(N, quarter_send, 1)
    counts_until(8)
    share_forward(0, 1)

    def take(d):
        arrived("sf0", d, g.nwfull.at[0, 0:half])
        hidden(behind_n(d))

    counts_until(10)
    share_forward(0, 2)
    loop(N, lambda d: cot_copy(d).start(), 1)
    arrived("nb", 0, g.nbfull.at[0 : N - 1])
    take(1)
    loop(N, functools.partial(share_forward, 0), 3)
    take(2)
    share_send(2)
    loop(N, take, 3)

    def column_max(i, most):
        return jnp.maximum(most, jnp.max(jnp.abs(g.zacc[at(i, CH), :]), axis=0, keepdims=True))

    most = lax.fori_loop(0, R // CH, column_max, jnp.full((1, C), 1e-30, F32))
    scale = most * (1.0 / 32766.0)
    g.zscale[...] = jnp.broadcast_to(scale, (8, C))
    loop(W, lambda d: zscale_copy(d).start(), 1)
    inv_scale = 1.0 / scale

    def code_z(i):
        rows = at(i, CH)
        whole = jnp.round(g.zacc[rows, :] * inv_scale)
        high = jnp.floor(whole * (1.0 / 256.0))
        g.zqa[rows, :] = high.astype(BF16)
        g.zqb[rows, :] = (whole - high * 256.0).astype(BF16)

    loop(R // CH, code_z)

    def send_z(d):
        peer = peer_w(d)
        picked = mm(g.sel[peer], g.zqa[...]) * 256.0 + mm(g.sel[peer], g.zqb[...])
        g.zsend[peer] = picked.astype(I32).astype(I16)
        z_copy(d).start()

    near = W // 4 + 1
    loop(near, send_z, 1)
    counts_until(12)
    loop(W, send_z, near)

    def split_z(i):
        rows = at(i, CH)
        value = g.zacc[rows, :]
        top = value.astype(BF16)
        g.zhi[rows, :] = top
        g.zlo[rows, :] = (value - top.astype(F32)).astype(BF16)

    loop(R // CH, split_z)
    counts_until(16)
    load(7).wait()
    load(9).wait()

    def own_part(i):
        rows = at(i, CH)
        value = mm(g.feats[rows, :], g.wfull[me_n, 0:D, :]) + g.cb[...].astype(F32).reshape(1, C)
        g.self_t[:, rows] = value.T
        g.cot_t[:, rows] = g.cot[rows, :].astype(F32).T
        total = jnp.zeros((CH, C), F32)
        for h in range(z.local):
            part = slice(h * CAP, (h + 1) * CAP)
            block = g.counts[h, rows, :]
            total += mm(block, g.zhi[part, :]) + mm(block, g.zlo[part, :]) + mm(g.counts_lo[h, rows, :], g.zhi[part, :])
        g.acc[rows, :] = total

    sweep(R // CH, own_part)
    ones = jnp.ones((16, 128), BF16)
    g.invs[...] = 2.0 / mm_nt(ones, g.wts[...].astype(BF16))

    def mine_t(i):
        cols = at(i, C)
        g.msg_t[cols, :] = g.msg[at(me_n, U), cols].astype(F32).T.astype(BF16)

    loop(D // C, mine_t)

    def take_z(d):
        s = peer_w(d)
        piece = min(32, CAP)
        for i in range(CAP // piece):
            rows = at(i, piece)
            value = g.ztab[s, rows, :].astype(I32).astype(F32) * g.zscales[s, 0:1, :]
            top = value.astype(BF16)
            g.thi[s, rows, :] = top
            g.tlo[s, rows, :] = (value - top.astype(F32)).astype(BF16)

    def pool(first, last):
        loop(last, take_z, first)

        def body(i):
            rows = at(i, CH)

            def add(d, total):
                s = peer_w(d)
                block = g.counts[z.local + s, rows, :]
                rest = g.counts_lo[z.local + s, rows, :]
                return total + mm(block, g.thi[s]) + mm(block, g.tlo[s]) + mm(rest, g.thi[s])

            g.acc[rows, :] = lax.fori_loop(first, last, add, g.acc[rows, :], unroll=W <= 8)

        return body

    arrived("zs", 0, g.zscales.at[0 : W - 1])
    for first_d, last_d in ((1, near), (W - 1, W)):
        loop(last_d, lambda d: z_copy(d).wait_recv(), first_d)
        sweep(R // CH, pool(first_d, last_d))
    loop(W - 1, lambda d: z_copy(d).wait_recv(), near)
    loop(N, quarter_pass, 1)
    pool_rest = pool(near, W - 1)

    def activate(i):
        pool_rest(i)
        rows = at(i, CH)
        pre = g.acc[rows, :].T * g.invs[0:1, rows] + g.self_t[:, rows]
        g.self_t[:, rows] = pre
        act = jnp.maximum(pre, 0.0)
        g.act[:, rows] = act.astype(BF16)
        squares = jnp.sum(act * act, axis=0, keepdims=True)
        inner = jnp.sum(act * g.cot_t[:, rows], axis=0, keepdims=True)
        g.stat[2 * i : 2 * i + 2, :] = jnp.concatenate([squares, inner], axis=0)

    sweep(R // CH, activate)
    loop(N, lambda d: stat_copy(d).start(), 1)
    pl.semaphore_signal(g.turn, inc=1, device_id={"wide": sibling}, device_id_type=MESH)
    g.actrows[me_n] = g.act[:, at(me_n, U)]
    pl.semaphore_wait(g.turn, 1)
    loop(N, lambda d: act_copy(d).start(), 1)
    arrived("st", 0, g.stats.at[0 : N - 1])
    g.stats[me_n] = g.stat[...]

    def norms(i):
        total = g.stats[0, 2 * i : 2 * i + 2, :]
        for s in range(1, N):
            total += g.stats[s, 2 * i : 2 * i + 2, :]
        return lax.rsqrt(total[0:1] / D + EPSILON), total[1:2]

    def grad_act(i):
        rows = at(i, CH)
        inv, inner = norms(i)
        pre = g.self_t[:, rows]
        act = jnp.maximum(pre, 0.0)
        grad = g.cot_t[:, rows] * inv - act * (inner * (inv * inv * inv) / D)
        grad = jnp.where(pre > 0, grad, 0.0)
        g.gp[:, rows] = grad.astype(BF16)
        g.gps[:, rows] = (grad * g.invs[0:1, rows]).astype(BF16)

    sweep(R // CH, grad_act)

    def send_ret(d):
        peer = peer_w(d)
        g.gsend[peer] = mm(g.gps[...], g.counts[z.local + peer]).astype(BF16)
        ret_copy(0, d).start()

    loop(W, send_ret, 1)

    def more_ret(p):
        loop(W, lambda d: ret_copy(p, d).start(), 1)

    more_ret(1)
    more_ret(2)
    join = max(1, 128 // CAP)
    for h in range(0, z.local, join):
        parts = [mm(g.gps[...], g.counts[h + q]) for q in range(join)]
        parts = jnp.concatenate(parts, axis=1) if join > 1 else parts[0]
        g.yacc[:, h * CAP : (h + join) * CAP] = parts

    def embed(i):
        rows = at(i, CH)
        inv, _ = norms(i)
        value = jnp.maximum(g.self_t[:, rows], 0.0) * inv
        g.emb[rows, :] = value.T.astype(BF16)

    sweep(R // CH, embed)
    emb_store = pltpu.make_async_copy(g.emb, g.emb_out, g.store.at[4])
    emb_store.start()
    more_ret(3)

    LW = min(512, D)

    def grad_self(i):
        lanes = at(i, LW)
        g.gc[0, :, lanes] = mm(g.gp[...], g.feats[:, lanes]).astype(BF16)

    sweep(D // LW, grad_self)
    ones_r = jnp.ones((8, R), BF16)
    g.gcb[...] = mm_nt(ones_r, g.gp[...])


    def take_ret(p):
        part = at(p, C // PARTS)
        arrived("gr", p, g.gret.at[0 : W - 1, part])

        def body(i):
            lanes = at(i, CH)

            def add(d, total):
                s = peer_w(d)
                return total + mm(g.gret[s, part, :], g.sel[s, :, lanes])

            total = lax.fori_loop(1, W, add, g.yacc[part, lanes], unroll=W <= 8)
            g.y[part, lanes] = total.astype(BF16)

        sweep(R // CH, body)
        loop(N, lambda d: y_copy(p, d).start(), 1)

    take_ret(0)
    loop(N, quarter_forward, 1)
    share_pass(2)
    for p in range(1, PARTS):
        take_ret(p)
    g.yrows[me_n] = g.y[:, at(me_n, U)]

    def grad_pool(i):
        lanes = at(i, LW)
        g.gc[1, :, lanes] = mm(g.y[...], g.msg[:, lanes]).astype(BF16)

    sweep(D // LW, grad_pool)
    loop(W, lambda d: bias_copy("bc", g.gcb, g.gcb_in, d).start(), 1)
    pair_start("c")

    reduce_pair("c")
    arrived("ct", 0, g.cotrows.at[0 : N - 1])
    g.cotrows[me_n] = g.cot[at(me_n, U), :]
    for s in range(N):
        g.cotrows_t[s] = g.cotrows[s].astype(F32).T
    arrived("sf1", 0, g.wfull.at[0 : N - 1, 0:half])
    arrived("y", 0, g.yrows.at[0 : N - 1])

    def hidden_rows(i):
        rows = at(i, CH)
        wrows = slice(D + i * CH, D + (i + 1) * CH)
        total = jnp.zeros((CH, U), F32)
        for s in range(N):
            total += mm(g.wfull[s, wrows, :], g.yrows[s])
        g.gh[rows, :] = jnp.where(g.msg_t[rows, :] > 0, total, 0.0).astype(BF16)

    sweep(D // CH, hidden_rows)
    loop(N, lambda d: gh_copy(0, d).start(), 1)
    g.ghc[me_n] = g.gh[at(me_n, C), :]

    def feature_rows(i):
        rows = at(i, C)
        total = jnp.zeros((C, U), F32)
        for s in range(N):
            total += mm(g.wfull[s, rows, :], g.gprows[s]) + mm(g.nwfull[s, rows, :], g.gh[s * C : (s + 1) * C, :])
        g.gft[i] = total.T.astype(BF16)

    loop(N, functools.partial(share_forward, 2), 1)
    arrived("ac", 0, g.actrows.at[0 : N - 1])
    per = CH // U
    lanes = at(lax.rem(me_n, per), U) if per > 1 else slice(None)
    total = g.stats[0, :, lanes]
    for s in range(1, N):
        total += g.stats[s, :, lanes]
    row = lax.broadcasted_iota(I32, total.shape, 0) - 2 * (me_n // per)
    inv = lax.rsqrt(jnp.sum(jnp.where(row == 0, total, 0.0), axis=0, keepdims=True) / D + EPSILON)
    inner = jnp.sum(jnp.where(row == 1, total, 0.0), axis=0, keepdims=True)
    factor = inner * (inv * inv * inv) / D
    for s in range(N):
        act = g.actrows[s].astype(F32)
        grad_rows = jnp.where(act > 0, g.cotrows_t[s] * inv - act * factor, 0.0)
        g.gprows[s] = grad_rows.astype(BF16)
    arrived("sf2", 0, g.wfull.at[0 : N - 1, 0:half])
    loop(N, lambda d: gh_copy(1, d).start(), 1)
    sweep(N, feature_rows)
    gf_store = pltpu.make_async_copy(g.gft.at[me_n], g.gf_out.at[me_n], g.store.at[3])
    gf_store.start()

    reduce_sum("c")

    def grad_neigh(q):
        rows = at(q, C // 2)
        out = (g.gn0, g.gn1)[q]

        def body(i):
            lanes = at(i, LW)
            total = jnp.zeros((C // 2, LW), F32)
            for s in range(N):
                total += mm(g.ghc[s, rows, :], g.feats[s * U : (s + 1) * U, lanes])
            out[0, :, lanes] = total.astype(BF16)

        sweep(D // LW, body)

    arrived("gh", 0, g.ghc.at[0 : N - 1, 0 : C // 2])
    grad_neigh(0)
    pair_start("n0")
    arrived("gh", 1, g.ghc.at[0 : N - 1, 0 : C // 2])
    loop(N, lambda d: gf_copy(d).start(), 1)
    reduce_pair("n0")
    grad_neigh(1)
    pair_start("n1")
    total = jnp.zeros((8, C), F32)
    ones_u = jnp.ones((8, U), BF16)
    for s in range(N):
        total += mm_nt(ones_u, g.ghc[s])
    g.gnb[...] = total
    loop(W, lambda d: bias_copy("bn", g.gnb, g.gnb_in, d).start(), 1)
    reduce_pair("n1")
    reduce_sum("n0")
    def bias_sum(name, own, others):
        arrived(name, 0, others.at[0 : W - 1])
        left(name, others.at[0 : W - 1])
        own[...] = lax.fori_loop(1, W, lambda d, total: total + others[peer_w(d)], own[...])

    bias_sum("bc", g.gcb, g.gcb_in)
    bias_sum("bn", g.gnb, g.gnb_in)
    gcb_store = pltpu.make_async_copy(g.gcb, g.gcb_out, g.store.at[5])
    gnb_store = pltpu.make_async_copy(g.gnb, g.gnb_out, g.store.at[6])
    gcb_store.start()
    gnb_store.start()
    gather_pass("c")
    reduce_sum("n1")
    gn0_store = gather_pass("n0")
    gn1_store = gather_pass("n1")
    gather_wait("c")
    for p in range(2):
        for i in range(D // CH):
            g.gct[p, at(i, CH), :] = g.gc_sum[p, :, at(i, CH)].astype(F32).T.astype(BF16)
    gc_store = pltpu.make_async_copy(g.gct, g.gc_out, g.store.at[0])
    gc_store.start()
    for k in SUMS[1:]:
        gather_wait(k)
    arrived("gf", 0, g.gf_out.at[0 : N - 1])

    for k in (0, 2):
        left("sh%d" % k, fulls[k].at[0 : N - 1, 0:part_w])
        left("sp%d" % k, fulls[k].at[0 : N - 1, 0 : (W // 2 - 1) * part_w])
        left("sf%d" % k, fulls[k].at[0 : N - 1, 0:half])
    left("sh1", g.wfull.at[0 : N - 1, 0 : 2 * eighth])
    left("sp1", g.wfull.at[0 : N - 1, 0 : 2 * eighth])
    left("sf1", g.wfull.at[0 : N - 1, 0:half])
    left("nb", g.nbfull.at[0 : N - 1])
    left("z", g.zsend.at[0 : W - 1])
    left("zs", g.zscales.at[0 : W - 1])
    left("st", g.stats.at[0 : N - 1])
    left("ct", g.cotrows.at[0 : N - 1])
    left("ac", g.actrows.at[0 : N - 1])
    left("gr", g.gsend.at[0 : W - 1])
    left("y", g.yrows.at[0 : N - 1])
    left("gh", g.ghc.at[0 : N - 1])
    left("gf", g.gf_out.at[0 : N - 1])
    for k in SUMS:
        left("hs" + k, grad(k, "_half"))
        left("rs" + k, grad(k, "_in").at[0 : W // 2 - 1])
        left("ag" + k, grad(k, "_in").at[0 : W // 2 - 1])
        left("fw" + k, grad(k, "_sum").at[core_rows(k, core)])
    for store in (emb_store, gf_store, gc_store, gcb_store, gnb_store, gn0_store, gn1_store):
        store.wait()


def finish(z, emb, gf, gn, gc, gnb, gcb, *refs):
    emb_out, gf_out, gn_out, gc_out, gnb_out, gcb_out, gf_t, gn_t, gc_t, gnb_t, gcb_t, store = refs
    D, N, U = z.width, z.narrow, z.part
    step = D // N
    stores = []

    def keep(src, dst):
        stores.append(pltpu.make_async_copy(src, dst, store.at[len(stores)]))
        stores[-1].start()

    keep(emb, emb_out)
    for i in range(N):
        rows = at(i, step)
        for p in range(2):
            gc_t[p, rows, :] = gc[p, rows, :].astype(F32)
            keep(gc_t.at[p, rows], gc_out.at[p, rows])
        gn_t[rows, :] = gn[0, :, rows].astype(F32).T
        keep(gn_t.at[rows], gn_out.at[rows])
        gf_t[at(i, U), :] = gf[i].astype(F32)
        keep(gf_t.at[at(i, U)], gf_out.at[at(i, U)])
    gnb_t[...] = gnb[0:1, :]
    gcb_t[...] = gcb[0:1, :]
    keep(gnb_t, gnb_out)
    keep(gcb_t, gcb_out)
    for copy in stores:
        copy.wait()


def shards(wide, narrow, node_feats, neigh_weight, neigh_bias, combine_weight, combine_bias, cotangent,
           neighbour_slot, neighbour_mask, visit_count, send_rows):
    z = Sizes(node_feats, neigh_weight, send_rows, neighbour_slot.T, wide, narrow)
    R, D, C, W, N, U = z.rows, z.width, z.cols, z.wide, z.narrow, z.part
    bufs, sems, kinds = scratch(z)
    names = NAMES_IN + NAMES_OUT + list(bufs) + list(sems)
    outs = (
        pltpu.VMEM((R, C), BF16),
        pltpu.VMEM((N, U, C), BF16),
        pltpu.VMEM((1, C, D), BF16),
        pltpu.VMEM((2, D, C), BF16),
        pltpu.VMEM((8, C), F32),
        pltpu.VMEM((8, C), F32),
    )
    emb, gf, gn, gc, gnb, gcb = pl.pallas_call(
        functools.partial(kernel, z, names, kinds),
        out_shape=outs,
        in_specs=[pl.BlockSpec(memory_space=pl.ANY)] * len(NAMES_IN),
        out_specs=[pl.BlockSpec(memory_space=pl.ANY)] * len(NAMES_OUT),
        scratch_shapes=list(bufs.values()) + list(sems.values()),
        compiler_params=pltpu.CompilerParams(
            collective_id=0, has_side_effects=True, vmem_limit_bytes=56 * 2**20
        ),
        cost_estimate=pl.CostEstimate(flops=2 * 10**10, bytes_accessed=2 * 10**7, transcendentals=0),
        name="layer",
    )(
        node_feats, neigh_weight, neigh_bias, combine_weight, combine_bias, cotangent,
        neighbour_slot.T, neighbour_mask.T, visit_count.T, send_rows,
    )
    hbm = pl.BlockSpec(memory_space=pl.ANY)
    emb, grad_features, grad_neigh, grad_combine, gnb, gcb = pl.pallas_call(
        functools.partial(finish, z),
        out_shape=(
            jax.ShapeDtypeStruct((R, C), BF16),
            jax.ShapeDtypeStruct((R, C), F32),
            jax.ShapeDtypeStruct((D, C), F32),
            jax.ShapeDtypeStruct((2, D, C), F32),
            jax.ShapeDtypeStruct((1, C), F32),
            jax.ShapeDtypeStruct((1, C), F32),
        ),
        in_specs=[pl.BlockSpec(memory_space=pltpu.VMEM)] * 6,
        out_specs=[hbm] * 6,
        scratch_shapes=[
            pltpu.VMEM((R, C), F32),
            pltpu.VMEM((D, C), F32),
            pltpu.VMEM((2, D, C), F32),
            pltpu.VMEM((1, C), F32),
            pltpu.VMEM((1, C), F32),
            pltpu.SemaphoreType.DMA((4 * N + 3,)),
        ],
        compiler_params=pltpu.CompilerParams(vmem_limit_bytes=32 * 2**20),
        name="finish",
    )(emb, gf, gn, gc, gnb, gcb)
    return emb, grad_features, grad_neigh, gnb.reshape(C), grad_combine.reshape(2 * D, C), gcb.reshape(C)


def solution(mesh):
    placed = (
        P("wide", None),
        P(None, "narrow"),
        P("narrow"),
        P(None, "narrow"),
        P("narrow"),
        P("wide", "narrow"),
        P("wide", None),
        P("wide", None),
        P("wide", None),
        P("wide", None),
    )
    return jax.shard_map(
        functools.partial(shards, mesh.shape["wide"], mesh.shape["narrow"]),
        mesh=mesh,
        in_specs=placed,
        out_specs=(
            P("wide", "narrow"),
            P("wide", "narrow"),
            P(None, "narrow"),
            P("narrow"),
            P(None, "narrow"),
            P("narrow"),
        ),
        check_vma=False,
    )
```

```python
import functools

import jax
import jax.numpy as jnp
from jax import lax
from jax.experimental import pallas as pl
from jax.experimental.pallas import tpu as pltpu
from jax.sharding import PartitionSpec as P

EPSILON = 1e-06
PARTS = 4
SUMS = ("c", "n0", "n1")
F32 = jnp.float32
BF16 = jnp.bfloat16
I32 = jnp.int32
I16 = jnp.int16
MESH = pl.DeviceIdType.MESH


def mm(left, right):
    return jnp.dot(left, right, preferred_element_type=F32)


def mm_nt(left, right):
    return lax.dot_general(left, right, (((1,), (1,)), ((), ())), preferred_element_type=F32)


def at(index, size):
    if isinstance(index, int):
        return slice(index * size, (index + 1) * size)
    return pl.ds(pl.multiple_of(index * size, size), size)


class Sizes:
    def __init__(self, feats, neigh, send, slot, wide, narrow):
        self.rows, self.width = feats.shape
        self.cols = neigh.shape[1]
        self.cap = send.shape[1]
        self.slots = slot.shape[0]
        self.wide, self.narrow = wide, narrow
        self.chunk = min(256, self.rows)
        self.part = self.rows // narrow
        self.local = self.rows // self.cap
        self.blocks = self.local + wide
        self.pairs = wide // 2

    def red(self, rows):
        size = max(16, rows // 2 // self.pairs)
        down = rows // 2 // size
        return size, down, self.width * down // self.pairs


NAMES_IN = ["feats_in", "nw_in", "nb_in", "comb_in", "cb_in", "cot_in", "slot_in", "mask_in", "visit_in", "send_in"]
NAMES_OUT = ["emb_out", "gf_out", "gn_out", "gc_out", "gnb_out", "gcb_out"]


def scratch(z):
    R, D, C, W, N, U, CAP = z.rows, z.width, z.cols, z.wide, z.narrow, z.part, z.cap
    v = lambda *shape: pltpu.VMEM(shape[:-1], shape[-1])
    bufs = dict(
        feats=v(R, D, BF16),
        nwfull=v(N, D, C, BF16),
        nbfull=v(N, 8, C, F32),
        nb=v(C, BF16),
        cb=v(C, BF16),
        wfull=v(N, 2 * D, C, BF16),
        cot=v(R, C, BF16),
        slot=v(z.slots, R, I32),
        mask=v(z.slots, R, I32),
        visit=v(z.slots, R, I32),
        send=v(W, CAP, I32),
        send_t=v(CAP, W, I32),
        code=v(R, 128, I32),
        wts=v(R, 128, F32),
        counts=v(z.blocks, R, CAP, BF16),
        counts_lo=v(z.blocks, R, CAP, BF16),
        sel=v(W, CAP, R, BF16),
        msg=v(R, D, BF16),
        zacc=v(R, C, F32),
        zhi=v(R, C, BF16),
        zlo=v(R, C, BF16),
        zqa=v(R, C, BF16),
        zqb=v(R, C, BF16),
        zscale=v(8, C, F32),
        thi=v(W, CAP, C, BF16),
        tlo=v(W, CAP, C, BF16),
        zscales=v(W, 8, C, F32),
        zsend=v(W, CAP, C, I16),
        ztab=v(W, CAP, C, I16),
        acc=v(R, C, F32),
        self_t=v(C, R, F32),
        cot_t=v(C, R, F32),
        invs=v(16, R, F32),
        stat=v(2 * (R // z.chunk), z.chunk, F32),
        stats=v(N, 2 * (R // z.chunk), z.chunk, F32),
        emb=v(R, C, BF16),
        gp=v(C, R, BF16),
        gps=v(C, R, BF16),
        act=v(C, R, BF16),
        actrows=v(N, C, U, BF16),
        cotrows=v(N, U, C, BF16),
        cotrows_t=v(N, C, U, F32),
        gprows=v(N, C, U, BF16),
        gsend=v(W, C, CAP, BF16),
        gret=v(W, C, CAP, BF16),
        yacc=v(C, R, F32),
        y=v(C, R, BF16),
        yrows=v(N, C, U, BF16),
        msg_t=v(D, U, BF16),
        gh=v(D, U, BF16),
        ghc=v(N, C, U, BF16),
        gft=v(N, U, C, BF16),
        gct=v(2, D, C, BF16),
        gc=v(2, C, D, BF16),
        gc_half=v(2, C // 2, D, BF16),
        gc_in=v(W // 2, 2, z.red(C)[0], z.red(C)[2], BF16),
        gc_sum=v(2, C, D, BF16),
        gn0=v(1, C // 2, D, BF16),
        gn0_half=v(1, C // 4, D, BF16),
        gn0_in=v(W // 2, 1, z.red(C // 2)[0], z.red(C // 2)[2], BF16),
        gn0_sum=v(1, C // 2, D, BF16),
        gn1=v(1, C // 2, D, BF16),
        gn1_half=v(1, C // 4, D, BF16),
        gn1_in=v(W // 2, 1, z.red(C // 2)[0], z.red(C // 2)[2], BF16),
        gn1_sum=v(1, C // 2, D, BF16),
        gcb=v(8, C, F32),
        gcb_in=v(W, 8, C, F32),
        gnb=v(8, C, F32),
        gnb_in=v(W, 8, C, F32),
    )
    kinds = dict(
        sh0=N, sh1=N, sh2=N, sp0=N, sp1=N, sp2=N, sf0=N, sf1=1, sf2=1, nb=1, st=1, ct=1, ac=1, y=1, gh=2, gf=1,
        z=W, zs=1, gr=PARTS, bc=1, bn=1,
    )
    for k in SUMS:
        kinds.update({"hs" + k: 1, "rs" + k: 1, "ag" + k: 1, "fw" + k: 1})
    sems = {name + "_r": pltpu.SemaphoreType.DMA((count,)) for name, count in kinds.items()}
    sems["turn"] = pltpu.SemaphoreType.REGULAR
    sems["sent"] = pltpu.SemaphoreType.DMA((len(kinds),))
    sems["load"] = pltpu.SemaphoreType.DMA((10,))
    sems["store"] = pltpu.SemaphoreType.DMA((7,))
    return bufs, sems, list(kinds)


class Refs:
    pass


def kernel(z, names, kinds, *refs):
    g = Refs()
    for name, ref in zip(names, refs):
        setattr(g, name, ref)
    R, D, C, W, N, U, CAP = z.rows, z.width, z.cols, z.wide, z.narrow, z.part, z.cap
    CH = z.chunk
    half = D // 2
    me_w, me_n = lax.axis_index("wide"), lax.axis_index("narrow")
    core = lax.rem(me_w, 2)
    sibling = me_w + 1 - 2 * core

    def loop(count, body, start=0):
        def step(i, carry):
            body(i)
            return carry

        lax.fori_loop(start, count, step, 0)

    def sweep(count, body):
        for i in range(count):
            body(i)

    def flip(me, e, size):
        peer, bit = 0, 1
        while bit < size:
            peer = peer + bit * lax.rem(me // bit + e // bit, 2)
            bit *= 2
        return peer

    def peer_n(d):
        return flip(me_n, N - d, N)

    def peer_w(d):
        return flip(me_w, W - d, W)

    def ahead_n(d):
        return lax.rem(me_n + d, N)

    def behind_n(d):
        return lax.rem(me_n - d + N, N)

    def across(e):
        return flip(me_w, e, W)

    def remote(name, index, src, dst, axis="narrow", peer=0):
        return pltpu.make_async_remote_copy(
            src_ref=src,
            dst_ref=dst,
            send_sem=g.sent.at[kinds.index(name)],
            recv_sem=getattr(g, name + "_r").at[index],
            device_id={axis: peer},
            device_id_type=MESH,
        )

    def arrived(name, index, ref):
        remote(name, index, ref, ref, "narrow", peer_n(1)).wait_recv()

    def left(name, ref):
        remote(name, 0, ref, ref, "narrow", peer_n(1)).wait_send()

    def rows_at(start, size):
        return pl.ds(pl.multiple_of(start, size), size)

    sources = (g.nw_in, None, g.comb_in)
    fulls = (g.nwfull, None, g.wfull)
    part_w = D // W

    def share():
        return rows_at((core * (W // 2) + me_w // 2) * part_w, part_w)

    def share_send(k):
        def body(d):
            remote("sh%d" % k, d, sources[k].at[share()], fulls[k].at[me_n, share()], "narrow", ahead_n(d)).start()

        loop(N, body, 1)

    def share_pass(k):
        def body(d):
            part = fulls[k].at[behind_n(d), share()]
            arrived("sh%d" % k, d, part)
            loop(W // 2, lambda e: remote("sp%d" % k, d, part, part, "wide", across(2 * e)).start(), 1)

        loop(N, body, 1)

    def share_forward(k, d):
        s = behind_n(d)
        arrived("sp%d" % k, d, fulls[k].at[s, 0 : (W // 2 - 1) * part_w])
        part = fulls[k].at[s, rows_at(core * half, half)]
        remote("sf%d" % k, d if k == 0 else 0, part, part, "wide", sibling).start()

    hops = (2, 4)
    eighth = D // 8

    def hop_bit(h):
        return lax.rem(me_w // hops[h], 2)

    def quarter(h):
        return rows_at(D + h * half + (2 * core + hop_bit(h)) * eighth, eighth)

    def quarter_send(d):
        for h in range(2):
            mine = quarter(h)
            remote("sh1", d, g.comb_in.at[mine], g.wfull.at[me_n, mine], "narrow", ahead_n(d)).start()

    def quarter_pass(d):
        s = behind_n(d)
        arrived("sh1", d, g.wfull.at[s, 0 : 2 * eighth])
        for h in range(2):
            part = g.wfull.at[s, quarter(h)]
            remote("sp1", d, part, part, "wide", me_w + hops[h] - 2 * hops[h] * hop_bit(h)).start()

    def quarter_forward(d):
        s = behind_n(d)
        arrived("sp1", d, g.wfull.at[s, 0 : 2 * eighth])
        for h in range(2):
            part = g.wfull.at[s, rows_at(D + h * half + 2 * core * eighth, 2 * eighth)]
            remote("sf1", 0, part, part, "wide", sibling).start()

    def nb_copy(d):
        return remote("nb", 0, g.nbfull.at[me_n], g.nbfull.at[me_n], "narrow", peer_n(d))

    def z_copy(d):
        peer = peer_w(d)
        return remote("z", d, g.zsend.at[peer], g.ztab.at[me_w], "wide", peer)

    def zscale_copy(d):
        return remote("zs", 0, g.zscale, g.zscales.at[me_w], "wide", peer_w(d))

    def stat_copy(d):
        return remote("st", 0, g.stat, g.stats.at[me_n], "narrow", peer_n(d))

    def cot_copy(d):
        s = peer_n(d)
        return remote("ct", 0, g.cot_in.at[at(s, U)], g.cotrows.at[me_n], "narrow", s)

    def act_copy(d):
        s = peer_n(d)
        return remote("ac", 0, g.act.at[:, at(s, U)], g.actrows.at[me_n], "narrow", s)

    def ret_copy(p, d):
        peer, rows = peer_w(d), at(p, C // PARTS)
        return remote("gr", p, g.gsend.at[peer, rows], g.gret.at[me_w, rows], "wide", peer)

    def y_copy(p, d):
        s, rows = peer_n(d), at(p, C // PARTS)
        return remote("y", 0, g.y.at[rows, at(s, U)], g.yrows.at[me_n, rows], "narrow", s)

    def gh_copy(q, d):
        s = peer_n(d)
        return remote("gh", q, g.gh.at[rows_at(s * C + q * (C // 2), C // 2)], g.ghc.at[me_n, at(q, C // 2)], "narrow", s)

    def gf_copy(d):
        s = peer_n(d)
        return remote("gf", 0, g.gft.at[s], g.gf_out.at[me_n], "narrow", s)

    def bias_copy(name, src, dst, d):
        return remote(name, 0, src, dst.at[me_w], "wide", peer_w(d))

    def grad(k, suffix=""):
        return getattr(g, "g" + k + suffix)

    def core_rows(k, which):
        return (slice(None), at(which, grad(k).shape[1] // 2))

    def red_block(k, w):
        rows = grad(k).shape[1]
        size, down, lanes = z.red(rows)
        q = w // 2
        row = lax.rem(w, 2) * (rows // 2) + lax.rem(q, down) * size
        return (slice(None), rows_at(row, size), at(q // down, lanes))

    def out_rows(k, which):
        rows = grad(k).shape[1]
        if k == "c":
            return g.gc_sum.at[:, at(which, rows // 2)]
        return g.gn_out.at[:, rows_at(int(k[1]) * rows + which * (rows // 2), rows // 2)]

    def pair_start(k):
        remote("hs" + k, 0, grad(k).at[core_rows(k, 1 - core)], grad(k, "_half"), "wide", sibling).start()

    def reduce_pair(k):
        arrived("hs" + k, 0, grad(k, "_half"))
        own, mine = grad(k), core_rows(k, core)
        own[mine] = (own[mine].astype(F32) + grad(k, "_half")[...].astype(F32)).astype(BF16)

        def body(e):
            peer = across(2 * e)
            remote("rs" + k, 0, own.at[red_block(k, peer)], grad(k, "_in").at[me_w // 2], "wide", peer).start()

        loop(W // 2, body, 1)

    def reduce_sum(k):
        others = grad(k, "_in")
        arrived("rs" + k, 0, others.at[0 : W // 2 - 1])
        mine = red_block(k, me_w)
        total = lax.fori_loop(
            1, W // 2, lambda e, t: t + others[across(2 * e) // 2].astype(F32), grad(k)[mine].astype(F32), unroll=W <= 8
        )
        grad(k, "_sum")[mine] = total.astype(BF16)
        part = grad(k, "_sum").at[mine]
        loop(W // 2, lambda e: remote("ag" + k, 0, part, part, "wide", across(2 * e)).start(), 1)

    def gather_pass(k):
        arrived("ag" + k, 0, grad(k, "_in").at[0 : W // 2 - 1])
        part = grad(k, "_sum").at[core_rows(k, core)]
        remote("fw" + k, 0, part, out_rows(k, core), "wide", sibling).start()
        if k == "c":
            return None
        store = pltpu.make_async_copy(part, out_rows(k, core), g.store.at[SUMS.index(k)])
        store.start()
        return store

    def gather_wait(k):
        arrived("fw" + k, 0, out_rows(k, 1 - core))

    loads = [
        (g.feats_in, g.feats),
        (g.nw_in, g.nwfull.at[me_n]),
        (g.comb_in, g.wfull.at[me_n]),
        (g.slot_in, g.slot),
        (g.mask_in, g.mask),
        (g.visit_in, g.visit),
        (g.send_in, g.send),
        (g.cot_in, g.cot),
        (g.nb_in, g.nb),
        (g.cb_in, g.cb),
    ]

    def load(i):
        return pltpu.make_async_copy(loads[i][0], loads[i][1], g.load.at[i])

    barrier = pltpu.get_barrier_semaphore()
    loop(W, lambda d: pl.semaphore_signal(barrier, inc=1, device_id={"wide": peer_w(d)}, device_id_type=MESH), 1)
    loop(N, lambda d: pl.semaphore_signal(barrier, inc=1, device_id={"narrow": peer_n(d)}, device_id_type=MESH), 1)
    order = (6, 8, 3, 4, 5, 0, 1, 2, 7, 9)
    for i in order:
        load(i).start()
    pl.semaphore_wait(barrier, W - 1 + N - 1)
    share_send(0)
    load(8).wait()
    g.nbfull[me_n] = jnp.broadcast_to(g.nb[...].astype(F32).reshape(1, C), (8, C))
    loop(N, lambda d: nb_copy(d).start(), 1)

    for i in (3, 4, 5):
        load(i).wait()
    K = z.slots
    shift = CAP.bit_length() - 1

    def fill(i):
        rows = at(i, CH)
        g.code[rows, :] = jnp.zeros((CH, 128), I32)
        g.wts[rows, :] = jnp.zeros((CH, 128), F32)
        code = g.slot[:, rows].T
        g.code[rows, 0:K] = code
        g.code[rows, 64 : 64 + K] = code
        weight = (g.mask[:, rows] * g.visit[:, rows]).astype(F32).T
        g.wts[rows, 0:K] = weight
        g.wts[rows, 64 : 64 + K] = weight

    loop(R // CH, fill)

    lane = lax.broadcasted_iota(I32, (8, 128), 1)
    sub = lax.broadcasted_iota(I32, (8, 128), 0)
    half_lane = jnp.where(lane >= 64, 1, 0)
    place = [sub == 2 * j + half_lane for j in range(4)]
    place_b = [jnp.where(m, 1.0, 0.0) for m in place]
    place_b = [jnp.concatenate([m, m], axis=0).astype(BF16) for m in place_b]
    low_row = lax.broadcasted_iota(I32, (CAP, 128), 0).astype(F32).astype(BF16)

    def count_group(i):
        start = pl.multiple_of(i * 16, 16)
        outs = []
        for p in range(2):
            rows = pl.ds(pl.multiple_of(start + 8 * p, 8), 8)
            code, weight = g.code[rows, :], g.wts[rows, :]
            high, low = code >> shift, (code & (CAP - 1)).astype(F32)
            left = []
            for h in range(0, z.blocks, 2):
                pair = [jnp.where(high == h + q, weight, 0.0) for q in range(2)]
                pair = jnp.concatenate(pair, axis=0).astype(BF16)
                left.append(jnp.concatenate([pair * place_b[j] for j in range(4)], axis=1))
            left = jnp.concatenate(left, axis=0)
            right = []
            for j in range(4):
                row = jnp.sum(jnp.where(place[j], low, 0.0), axis=0, keepdims=True)
                row = jnp.broadcast_to(row.astype(BF16), (CAP, 128))
                right.append(jnp.where(low_row == row, jnp.ones((), BF16), jnp.zeros((), BF16)))
            outs.append(mm_nt(left, jnp.concatenate(right, axis=1)))
        for h in range(z.blocks):
            block = jnp.concatenate([out[h * 8 : h * 8 + 8] for out in outs], axis=0)
            top = block.astype(BF16)
            g.counts[h, pl.ds(start, 16), :] = top
            g.counts_lo[h, pl.ds(start, 16), :] = (block - top.astype(F32)).astype(BF16)

    UNROLL = 4
    groups = R // 16 // UNROLL

    def count_groups(first, last):
        def body(i):
            for q in range(UNROLL):
                count_group(i * UNROLL + q)

        loop(last, body, first)

    def hidden(s):
        def body(i):
            rows = at(i, CH)
            value = mm(g.feats[rows, :], g.nwfull[s]) + g.nbfull[s, 0:1, :]
            value = jnp.maximum(value, 0.0)
            top = value.astype(BF16)
            rest = (value - top.astype(F32)).astype(BF16)
            g.msg[rows, at(s, C)] = top
            weight = g.wfull[me_n, pl.ds(pl.multiple_of(D + s * C, C), C), :]
            g.zacc[rows, :] += mm(top, weight) + mm(rest, weight)

        sweep(R // CH, body)

    done = [0]

    def counts_until(last):
        last = groups * last // 16
        count_groups(done[0], last)
        done[0] = last

    def zero(i):
        g.zacc[at(i, CH), :] = jnp.zeros((CH, C), F32)

    loop(R // CH, zero)
    for i in (0, 1, 2):
        load(i).wait()
    hidden(me_n)
    counts_until(2)
    load(6).wait()
    g.send_t[...] = g.send[...].T

    def select(d):
        r = peer_w(d)
        which = lax.broadcasted_iota(I32, (CAP, W), 1)
        col = jnp.sum(jnp.where(which == r, g.send_t[...], 0), axis=1, keepdims=True)
        place_u = lax.broadcasted_iota(I32, (CAP, R), 1)
        g.sel[r] = jnp.where(place_u == col, 1.0, 0.0).astype(BF16)

    loop(W, select, 1)
    share_pass(0)
    loop(N, quarter_send, 1)
    counts_until(8)
    share_forward(0, 1)

    def take(d):
        arrived("sf0", d, g.nwfull.at[0, 0:half])
        hidden(behind_n(d))

    counts_until(10)
    share_forward(0, 2)
    loop(N, lambda d: cot_copy(d).start(), 1)
    arrived("nb", 0, g.nbfull.at[0 : N - 1])
    take(1)
    loop(N, functools.partial(share_forward, 0), 3)
    take(2)
    share_send(2)
    loop(N, take, 3)

    def column_max(i, most):
        return jnp.maximum(most, jnp.max(jnp.abs(g.zacc[at(i, CH), :]), axis=0, keepdims=True))

    most = lax.fori_loop(0, R // CH, column_max, jnp.full((1, C), 1e-30, F32))
    scale = most * (1.0 / 32766.0)
    g.zscale[...] = jnp.broadcast_to(scale, (8, C))
    loop(W, lambda d: zscale_copy(d).start(), 1)
    inv_scale = 1.0 / scale

    def code_z(i):
        rows = at(i, CH)
        whole = jnp.round(g.zacc[rows, :] * inv_scale)
        high = jnp.floor(whole * (1.0 / 256.0))
        g.zqa[rows, :] = high.astype(BF16)
        g.zqb[rows, :] = (whole - high * 256.0).astype(BF16)

    loop(R // CH, code_z)

    def send_z(d):
        peer = peer_w(d)
        picked = mm(g.sel[peer], g.zqa[...]) * 256.0 + mm(g.sel[peer], g.zqb[...])
        g.zsend[peer] = picked.astype(I32).astype(I16)
        z_copy(d).start()

    near = W // 4 + 1
    loop(near, send_z, 1)
    counts_until(12)
    loop(W, send_z, near)

    def split_z(i):
        rows = at(i, CH)
        value = g.zacc[rows, :]
        top = value.astype(BF16)
        g.zhi[rows, :] = top
        g.zlo[rows, :] = (value - top.astype(F32)).astype(BF16)

    loop(R // CH, split_z)
    counts_until(16)
    load(7).wait()
    load(9).wait()

    def own_part(i):
        rows = at(i, CH)
        value = mm(g.feats[rows, :], g.wfull[me_n, 0:D, :]) + g.cb[...].astype(F32).reshape(1, C)
        g.self_t[:, rows] = value.T
        g.cot_t[:, rows] = g.cot[rows, :].astype(F32).T
        total = jnp.zeros((CH, C), F32)
        for h in range(z.local):
            part = slice(h * CAP, (h + 1) * CAP)
            block = g.counts[h, rows, :]
            total += mm(block, g.zhi[part, :]) + mm(block, g.zlo[part, :]) + mm(g.counts_lo[h, rows, :], g.zhi[part, :])
        g.acc[rows, :] = total

    sweep(R // CH, own_part)
    ones = jnp.ones((16, 128), BF16)
    g.invs[...] = 2.0 / mm_nt(ones, g.wts[...].astype(BF16))

    def mine_t(i):
        cols = at(i, C)
        g.msg_t[cols, :] = g.msg[at(me_n, U), cols].astype(F32).T.astype(BF16)

    loop(D // C, mine_t)

    def take_z(d):
        s = peer_w(d)
        piece = min(32, CAP)
        for i in range(CAP // piece):
            rows = at(i, piece)
            value = g.ztab[s, rows, :].astype(I32).astype(F32) * g.zscales[s, 0:1, :]
            top = value.astype(BF16)
            g.thi[s, rows, :] = top
            g.tlo[s, rows, :] = (value - top.astype(F32)).astype(BF16)

    def pool(first, last):
        loop(last, take_z, first)

        def body(i):
            rows = at(i, CH)

            def add(d, total):
                s = peer_w(d)
                block = g.counts[z.local + s, rows, :]
                rest = g.counts_lo[z.local + s, rows, :]
                return total + mm(block, g.thi[s]) + mm(block, g.tlo[s]) + mm(rest, g.thi[s])

            g.acc[rows, :] = lax.fori_loop(first, last, add, g.acc[rows, :], unroll=W <= 8)

        return body

    arrived("zs", 0, g.zscales.at[0 : W - 1])
    for first_d, last_d in ((1, near), (W - 1, W)):
        loop(last_d, lambda d: z_copy(d).wait_recv(), first_d)
        sweep(R // CH, pool(first_d, last_d))
    loop(W - 1, lambda d: z_copy(d).wait_recv(), near)
    loop(N, quarter_pass, 1)
    pool_rest = pool(near, W - 1)

    def activate(i):
        pool_rest(i)
        rows = at(i, CH)
        pre = g.acc[rows, :].T * g.invs[0:1, rows] + g.self_t[:, rows]
        g.self_t[:, rows] = pre
        act = jnp.maximum(pre, 0.0)
        g.act[:, rows] = act.astype(BF16)
        squares = jnp.sum(act * act, axis=0, keepdims=True)
        inner = jnp.sum(act * g.cot_t[:, rows], axis=0, keepdims=True)
        g.stat[2 * i : 2 * i + 2, :] = jnp.concatenate([squares, inner], axis=0)

    sweep(R // CH, activate)
    loop(N, lambda d: stat_copy(d).start(), 1)
    pl.semaphore_signal(g.turn, inc=1, device_id={"wide": sibling}, device_id_type=MESH)
    g.actrows[me_n] = g.act[:, at(me_n, U)]
    pl.semaphore_wait(g.turn, 1)
    loop(N, lambda d: act_copy(d).start(), 1)
    arrived("st", 0, g.stats.at[0 : N - 1])
    g.stats[me_n] = g.stat[...]

    def norms(i):
        total = g.stats[0, 2 * i : 2 * i + 2, :]
        for s in range(1, N):
            total += g.stats[s, 2 * i : 2 * i + 2, :]
        return lax.rsqrt(total[0:1] / D + EPSILON), total[1:2]

    def grad_act(i):
        rows = at(i, CH)
        inv, inner = norms(i)
        pre = g.self_t[:, rows]
        act = jnp.maximum(pre, 0.0)
        grad = g.cot_t[:, rows] * inv - act * (inner * (inv * inv * inv) / D)
        grad = jnp.where(pre > 0, grad, 0.0)
        g.gp[:, rows] = grad.astype(BF16)
        g.gps[:, rows] = (grad * g.invs[0:1, rows]).astype(BF16)

    sweep(R // CH, grad_act)

    def send_ret(d):
        peer = peer_w(d)
        g.gsend[peer] = mm(g.gps[...], g.counts[z.local + peer]).astype(BF16)
        ret_copy(0, d).start()

    loop(W, send_ret, 1)

    def more_ret(p):
        loop(W, lambda d: ret_copy(p, d).start(), 1)

    more_ret(1)
    more_ret(2)
    join = max(1, 128 // CAP)
    for h in range(0, z.local, join):
        parts = [mm(g.gps[...], g.counts[h + q]) for q in range(join)]
        parts = jnp.concatenate(parts, axis=1) if join > 1 else parts[0]
        g.yacc[:, h * CAP : (h + join) * CAP] = parts

    def embed(i):
        rows = at(i, CH)
        inv, _ = norms(i)
        value = jnp.maximum(g.self_t[:, rows], 0.0) * inv
        g.emb[rows, :] = value.T.astype(BF16)

    sweep(R // CH, embed)
    emb_store = pltpu.make_async_copy(g.emb, g.emb_out, g.store.at[4])
    emb_store.start()
    more_ret(3)

    LW = min(512, D)

    def grad_self(i):
        lanes = at(i, LW)
        g.gc[0, :, lanes] = mm(g.gp[...], g.feats[:, lanes]).astype(BF16)

    sweep(D // LW, grad_self)
    ones_r = jnp.ones((8, R), BF16)
    g.gcb[...] = mm_nt(ones_r, g.gp[...])


    def take_ret(p):
        part = at(p, C // PARTS)
        arrived("gr", p, g.gret.at[0 : W - 1, part])

        def body(i):
            lanes = at(i, CH)

            def add(d, total):
                s = peer_w(d)
                return total + mm(g.gret[s, part, :], g.sel[s, :, lanes])

            total = lax.fori_loop(1, W, add, g.yacc[part, lanes], unroll=W <= 8)
            g.y[part, lanes] = total.astype(BF16)

        sweep(R // CH, body)
        loop(N, lambda d: y_copy(p, d).start(), 1)

    take_ret(0)
    loop(N, quarter_forward, 1)
    share_pass(2)
    for p in range(1, PARTS):
        take_ret(p)
    g.yrows[me_n] = g.y[:, at(me_n, U)]

    def grad_pool(i):
        lanes = at(i, LW)
        g.gc[1, :, lanes] = mm(g.y[...], g.msg[:, lanes]).astype(BF16)

    sweep(D // LW, grad_pool)
    loop(W, lambda d: bias_copy("bc", g.gcb, g.gcb_in, d).start(), 1)
    pair_start("c")

    reduce_pair("c")
    arrived("ct", 0, g.cotrows.at[0 : N - 1])
    g.cotrows[me_n] = g.cot[at(me_n, U), :]
    for s in range(N):
        g.cotrows_t[s] = g.cotrows[s].astype(F32).T
    arrived("sf1", 0, g.wfull.at[0 : N - 1, 0:half])
    arrived("y", 0, g.yrows.at[0 : N - 1])

    def hidden_rows(i):
        rows = at(i, CH)
        wrows = slice(D + i * CH, D + (i + 1) * CH)
        total = jnp.zeros((CH, U), F32)
        for s in range(N):
            total += mm(g.wfull[s, wrows, :], g.yrows[s])
        g.gh[rows, :] = jnp.where(g.msg_t[rows, :] > 0, total, 0.0).astype(BF16)

    sweep(D // CH, hidden_rows)
    loop(N, lambda d: gh_copy(0, d).start(), 1)
    g.ghc[me_n] = g.gh[at(me_n, C), :]

    def feature_rows(i):
        rows = at(i, C)
        total = jnp.zeros((C, U), F32)
        for s in range(N):
            total += mm(g.wfull[s, rows, :], g.gprows[s]) + mm(g.nwfull[s, rows, :], g.gh[s * C : (s + 1) * C, :])
        g.gft[i] = total.T.astype(BF16)

    loop(N, functools.partial(share_forward, 2), 1)
    arrived("ac", 0, g.actrows.at[0 : N - 1])
    per = CH // U
    lanes = at(lax.rem(me_n, per), U) if per > 1 else slice(None)
    total = g.stats[0, :, lanes]
    for s in range(1, N):
        total += g.stats[s, :, lanes]
    row = lax.broadcasted_iota(I32, total.shape, 0) - 2 * (me_n // per)
    inv = lax.rsqrt(jnp.sum(jnp.where(row == 0, total, 0.0), axis=0, keepdims=True) / D + EPSILON)
    inner = jnp.sum(jnp.where(row == 1, total, 0.0), axis=0, keepdims=True)
    factor = inner * (inv * inv * inv) / D
    for s in range(N):
        act = g.actrows[s].astype(F32)
        grad_rows = jnp.where(act > 0, g.cotrows_t[s] * inv - act * factor, 0.0)
        g.gprows[s] = grad_rows.astype(BF16)
    arrived("sf2", 0, g.wfull.at[0 : N - 1, 0:half])
    loop(N, lambda d: gh_copy(1, d).start(), 1)
    sweep(N, feature_rows)
    gf_store = pltpu.make_async_copy(g.gft.at[me_n], g.gf_out.at[me_n], g.store.at[3])
    gf_store.start()

    reduce_sum("c")

    def grad_neigh(q):
        rows = at(q, C // 2)
        out = (g.gn0, g.gn1)[q]

        def body(i):
            lanes = at(i, LW)
            total = jnp.zeros((C // 2, LW), F32)
            for s in range(N):
                total += mm(g.ghc[s, rows, :], g.feats[s * U : (s + 1) * U, lanes])
            out[0, :, lanes] = total.astype(BF16)

        sweep(D // LW, body)

    arrived("gh", 0, g.ghc.at[0 : N - 1, 0 : C // 2])
    grad_neigh(0)
    pair_start("n0")
    arrived("gh", 1, g.ghc.at[0 : N - 1, 0 : C // 2])
    loop(N, lambda d: gf_copy(d).start(), 1)
    reduce_pair("n0")
    grad_neigh(1)
    pair_start("n1")
    total = jnp.zeros((8, C), F32)
    ones_u = jnp.ones((8, U), BF16)
    for s in range(N):
        total += mm_nt(ones_u, g.ghc[s])
    g.gnb[...] = total
    loop(W, lambda d: bias_copy("bn", g.gnb, g.gnb_in, d).start(), 1)
    reduce_pair("n1")
    reduce_sum("n0")
    def bias_sum(name, own, others):
        arrived(name, 0, others.at[0 : W - 1])
        left(name, others.at[0 : W - 1])
        own[...] = lax.fori_loop(1, W, lambda d, total: total + others[peer_w(d)], own[...])

    bias_sum("bc", g.gcb, g.gcb_in)
    bias_sum("bn", g.gnb, g.gnb_in)
    gcb_store = pltpu.make_async_copy(g.gcb, g.gcb_out, g.store.at[5])
    gnb_store = pltpu.make_async_copy(g.gnb, g.gnb_out, g.store.at[6])
    gcb_store.start()
    gnb_store.start()
    gather_pass("c")
    reduce_sum("n1")
    gn0_store = gather_pass("n0")
    gn1_store = gather_pass("n1")
    gather_wait("c")
    for p in range(2):
        for i in range(D // CH):
            g.gct[p, at(i, CH), :] = g.gc_sum[p, :, at(i, CH)].astype(F32).T.astype(BF16)
    gc_store = pltpu.make_async_copy(g.gct, g.gc_out, g.store.at[0])
    gc_store.start()
    for k in SUMS[1:]:
        gather_wait(k)
    arrived("gf", 0, g.gf_out.at[0 : N - 1])

    for k in (0, 2):
        left("sh%d" % k, fulls[k].at[0 : N - 1, 0:part_w])
        left("sp%d" % k, fulls[k].at[0 : N - 1, 0 : (W // 2 - 1) * part_w])
        left("sf%d" % k, fulls[k].at[0 : N - 1, 0:half])
    left("sh1", g.wfull.at[0 : N - 1, 0 : 2 * eighth])
    left("sp1", g.wfull.at[0 : N - 1, 0 : 2 * eighth])
    left("sf1", g.wfull.at[0 : N - 1, 0:half])
    left("nb", g.nbfull.at[0 : N - 1])
    left("z", g.zsend.at[0 : W - 1])
    left("zs", g.zscales.at[0 : W - 1])
    left("st", g.stats.at[0 : N - 1])
    left("ct", g.cotrows.at[0 : N - 1])
    left("ac", g.actrows.at[0 : N - 1])
    left("gr", g.gsend.at[0 : W - 1])
    left("y", g.yrows.at[0 : N - 1])
    left("gh", g.ghc.at[0 : N - 1])
    left("gf", g.gf_out.at[0 : N - 1])
    for k in SUMS:
        left("hs" + k, grad(k, "_half"))
        left("rs" + k, grad(k, "_in").at[0 : W // 2 - 1])
        left("ag" + k, grad(k, "_in").at[0 : W // 2 - 1])
        left("fw" + k, grad(k, "_sum").at[core_rows(k, core)])
    for store in (emb_store, gf_store, gc_store, gcb_store, gnb_store, gn0_store, gn1_store):
        store.wait()


def finish(z, emb, gf, gn, gc, gnb, gcb, *refs):
    emb_out, gf_out, gn_out, gc_out, gnb_out, gcb_out, gf_t, gn_t, gc_t, gnb_t, gcb_t, store = refs
    D, N, U = z.width, z.narrow, z.part
    step = D // N
    stores = []

    def keep(src, dst):
        stores.append(pltpu.make_async_copy(src, dst, store.at[len(stores)]))
        stores[-1].start()

    keep(emb, emb_out)
    for i in range(N):
        rows = at(i, step)
        for p in range(2):
            gc_t[p, rows, :] = gc[p, rows, :].astype(F32)
            keep(gc_t.at[p, rows], gc_out.at[p, rows])
        gn_t[rows, :] = gn[0, :, rows].astype(F32).T
        keep(gn_t.at[rows], gn_out.at[rows])
        gf_t[at(i, U), :] = gf[i].astype(F32)
        keep(gf_t.at[at(i, U)], gf_out.at[at(i, U)])
    gnb_t[...] = gnb[0:1, :]
    gcb_t[...] = gcb[0:1, :]
    keep(gnb_t, gnb_out)
    keep(gcb_t, gcb_out)
    for copy in stores:
        copy.wait()


def shards(wide, narrow, node_feats, neigh_weight, neigh_bias, combine_weight, combine_bias, cotangent,
           neighbour_slot, neighbour_mask, visit_count, send_rows):
    z = Sizes(node_feats, neigh_weight, send_rows, neighbour_slot.T, wide, narrow)
    R, D, C, W, N, U = z.rows, z.width, z.cols, z.wide, z.narrow, z.part
    bufs, sems, kinds = scratch(z)
    names = NAMES_IN + NAMES_OUT + list(bufs) + list(sems)
    outs = (
        pltpu.VMEM((R, C), BF16),
        pltpu.VMEM((N, U, C), BF16),
        pltpu.VMEM((1, C, D), BF16),
        pltpu.VMEM((2, D, C), BF16),
        pltpu.VMEM((8, C), F32),
        pltpu.VMEM((8, C), F32),
    )
    emb, gf, gn, gc, gnb, gcb = pl.pallas_call(
        functools.partial(kernel, z, names, kinds),
        out_shape=outs,
        in_specs=[pl.BlockSpec(memory_space=pl.ANY)] * len(NAMES_IN),
        out_specs=[pl.BlockSpec(memory_space=pl.ANY)] * len(NAMES_OUT),
        scratch_shapes=list(bufs.values()) + list(sems.values()),
        compiler_params=pltpu.CompilerParams(
            collective_id=0, has_side_effects=True, vmem_limit_bytes=58 * 2**20
        ),
        cost_estimate=pl.CostEstimate(flops=2 * 10**10, bytes_accessed=2 * 10**7, transcendentals=0),
        name="layer",
    )(
        node_feats, neigh_weight, neigh_bias, combine_weight, combine_bias, cotangent,
        neighbour_slot.T, neighbour_mask.T, visit_count.T, send_rows,
    )
    hbm = pl.BlockSpec(memory_space=pl.ANY)
    emb, grad_features, grad_neigh, grad_combine, gnb, gcb = pl.pallas_call(
        functools.partial(finish, z),
        out_shape=(
            jax.ShapeDtypeStruct((R, C), BF16),
            jax.ShapeDtypeStruct((R, C), F32),
            jax.ShapeDtypeStruct((D, C), F32),
            jax.ShapeDtypeStruct((2, D, C), F32),
            jax.ShapeDtypeStruct((1, C), F32),
            jax.ShapeDtypeStruct((1, C), F32),
        ),
        in_specs=[pl.BlockSpec(memory_space=pltpu.VMEM)] * 6,
        out_specs=[hbm] * 6,
        scratch_shapes=[
            pltpu.VMEM((R, C), F32),
            pltpu.VMEM((D, C), F32),
            pltpu.VMEM((2, D, C), F32),
            pltpu.VMEM((1, C), F32),
            pltpu.VMEM((1, C), F32),
            pltpu.SemaphoreType.DMA((4 * N + 3,)),
        ],
        compiler_params=pltpu.CompilerParams(vmem_limit_bytes=32 * 2**20),
        name="finish",
    )(emb, gf, gn, gc, gnb, gcb)
    return emb, grad_features, grad_neigh, gnb.reshape(C), grad_combine.reshape(2 * D, C), gcb.reshape(C)


def solution(mesh):
    placed = (
        P("wide", None),
        P(None, "narrow"),
        P("narrow"),
        P(None, "narrow"),
        P("narrow"),
        P("wide", "narrow"),
        P("wide", None),
        P("wide", None),
        P("wide", None),
        P("wide", None),
    )
    return jax.shard_map(
        functools.partial(shards, mesh.shape["wide"], mesh.shape["narrow"]),
        mesh=mesh,
        in_specs=placed,
        out_specs=(
            P("wide", "narrow"),
            P("wide", "narrow"),
            P(None, "narrow"),
            P("narrow"),
            P(None, "narrow"),
            P("narrow"),
        ),
        check_vma=False,
    )
```

```python
import functools

import jax
import jax.numpy as jnp
from jax import lax
from jax.experimental import pallas as pl
from jax.experimental.pallas import tpu as pltpu
from jax.sharding import PartitionSpec as P

EPSILON = 1e-06
PARTS = 4
SUMS = ("c", "n0", "n1")
F32 = jnp.float32
BF16 = jnp.bfloat16
I32 = jnp.int32
I16 = jnp.int16
MESH = pl.DeviceIdType.MESH


def mm(left, right):
    return jnp.dot(left, right, preferred_element_type=F32)


def mm_nt(left, right):
    return lax.dot_general(left, right, (((1,), (1,)), ((), ())), preferred_element_type=F32)


def at(index, size):
    if isinstance(index, int):
        return slice(index * size, (index + 1) * size)
    return pl.ds(pl.multiple_of(index * size, size), size)


class Sizes:
    def __init__(self, feats, neigh, send, slot, wide, narrow):
        self.rows, self.width = feats.shape
        self.cols = neigh.shape[1]
        self.cap = send.shape[1]
        self.slots = slot.shape[0]
        self.wide, self.narrow = wide, narrow
        self.chunk = min(256, self.rows)
        self.part = self.rows // narrow
        self.local = self.rows // self.cap
        self.blocks = self.local + wide
        self.pairs = wide // 2

    def red(self, rows):
        size = max(16, rows // 2 // self.pairs)
        down = rows // 2 // size
        return size, down, self.width * down // self.pairs


NAMES_IN = ["feats_in", "nw_in", "nb_in", "comb_in", "cb_in", "cot_in", "slot_in", "mask_in", "visit_in", "send_in"]
NAMES_OUT = ["emb_out", "gf_out", "gn_out", "gc_out", "gnb_out", "gcb_out"]


def scratch(z):
    R, D, C, W, N, U, CAP = z.rows, z.width, z.cols, z.wide, z.narrow, z.part, z.cap
    v = lambda *shape: pltpu.VMEM(shape[:-1], shape[-1])
    bufs = dict(
        feats=v(R, D, BF16),
        nwfull=v(N, D, C, BF16),
        nbfull=v(N, 8, C, F32),
        nb=v(C, BF16),
        cb=v(C, BF16),
        wfull=v(N, 2 * D, C, BF16),
        cot=v(R, C, BF16),
        slot=v(z.slots, R, I32),
        mask=v(z.slots, R, I32),
        visit=v(z.slots, R, I32),
        send=v(W, CAP, I32),
        send_t=v(CAP, W, I32),
        code=v(R, 128, I32),
        wts=v(R, 128, F32),
        counts=v(z.blocks, R, CAP, BF16),
        counts_lo=v(z.blocks, R, CAP, BF16),
        sel=v(W, CAP, R, BF16),
        msg=v(R, D, BF16),
        zacc=v(R, C, F32),
        zhi=v(R, C, BF16),
        zlo=v(R, C, BF16),
        zqa=v(R, C, BF16),
        zqb=v(R, C, BF16),
        zscale=v(8, C, F32),
        thi=v(W, CAP, C, BF16),
        tlo=v(W, CAP, C, BF16),
        zscales=v(W, 8, C, F32),
        zsend=v(W, CAP, C, I16),
        ztab=v(W, CAP, C, I16),
        acc=v(R, C, F32),
        self_t=v(C, R, F32),
        cot_t=v(C, R, F32),
        invs=v(16, R, F32),
        stat=v(2 * (R // z.chunk), z.chunk, F32),
        stats=v(N, 2 * (R // z.chunk), z.chunk, F32),
        emb=v(R, C, BF16),
        gp=v(C, R, BF16),
        gps=v(C, R, BF16),
        act=v(C, R, BF16),
        actrows=v(N, C, U, BF16),
        cotrows=v(N, U, C, BF16),
        cotrows_t=v(N, C, U, F32),
        gprows=v(N, C, U, BF16),
        gsend=v(W, C, CAP, BF16),
        gret=v(W, C, CAP, BF16),
        yacc=v(C, R, F32),
        y=v(C, R, BF16),
        yrows=v(N, C, U, BF16),
        msg_t=v(D, U, BF16),
        gh=v(D, U, BF16),
        ghc=v(N, C, U, BF16),
        gft=v(N, U, C, BF16),
        gct=v(2, D, C, BF16),
        gc=v(2, C, D, BF16),
        gc_half=v(2, C // 2, D, BF16),
        gc_in=v(W // 2, 2, z.red(C)[0], z.red(C)[2], BF16),
        gc_sum=v(2, C, D, BF16),
        gn0=v(1, C // 2, D, BF16),
        gn0_half=v(1, C // 4, D, BF16),
        gn0_in=v(W // 2, 1, z.red(C // 2)[0], z.red(C // 2)[2], BF16),
        gn0_sum=v(1, C // 2, D, BF16),
        gn1=v(1, C // 2, D, BF16),
        gn1_half=v(1, C // 4, D, BF16),
        gn1_in=v(W // 2, 1, z.red(C // 2)[0], z.red(C // 2)[2], BF16),
        gn1_sum=v(1, C // 2, D, BF16),
        gcb=v(8, C, F32),
        gcb_in=v(W, 8, C, F32),
        gnb=v(8, C, F32),
        gnb_in=v(W, 8, C, F32),
    )
    kinds = dict(
        sh0=N, sh1=1, sh2=N, sp0=N, sp1=1, sp2=N, sf0=N, sf1=1, sf2=1, nb=1, st=1, ct=1, ac=1, y=1, gh=2, gf=1,
        z=W, zs=1, gr=PARTS, bc=1, bn=1,
    )
    for k in SUMS:
        kinds.update({"hs" + k: 1, "rs" + k: 1, "ag" + k: 1, "fw" + k: 1})
    sems = {name + "_r": pltpu.SemaphoreType.DMA((count,)) for name, count in kinds.items()}
    sems["turn"] = pltpu.SemaphoreType.REGULAR
    sems["sent"] = pltpu.SemaphoreType.DMA((len(kinds),))
    sems["load"] = pltpu.SemaphoreType.DMA((10,))
    sems["store"] = pltpu.SemaphoreType.DMA((7,))
    return bufs, sems, list(kinds)


class Refs:
    pass


def kernel(z, names, kinds, *refs):
    g = Refs()
    for name, ref in zip(names, refs):
        setattr(g, name, ref)
    R, D, C, W, N, U, CAP = z.rows, z.width, z.cols, z.wide, z.narrow, z.part, z.cap
    CH = z.chunk
    half = D // 2
    me_w, me_n = lax.axis_index("wide"), lax.axis_index("narrow")
    core = lax.rem(me_w, 2)
    sibling = me_w + 1 - 2 * core

    def loop(count, body, start=0):
        def step(i, carry):
            body(i)
            return carry

        lax.fori_loop(start, count, step, 0)

    def sweep(count, body):
        for i in range(count):
            body(i)

    def flip(me, e, size):
        peer, bit = 0, 1
        while bit < size:
            peer = peer + bit * lax.rem(me // bit + e // bit, 2)
            bit *= 2
        return peer

    def peer_n(d):
        return flip(me_n, N - d, N)

    def peer_w(d):
        return flip(me_w, W - d, W)

    def ahead_n(d):
        return lax.rem(me_n + d, N)

    def behind_n(d):
        return lax.rem(me_n - d + N, N)

    def across(e):
        return flip(me_w, e, W)

    def remote(name, index, src, dst, axis="narrow", peer=0):
        return pltpu.make_async_remote_copy(
            src_ref=src,
            dst_ref=dst,
            send_sem=g.sent.at[kinds.index(name)],
            recv_sem=getattr(g, name + "_r").at[index],
            device_id={axis: peer},
            device_id_type=MESH,
        )

    def arrived(name, index, ref):
        remote(name, index, ref, ref, "narrow", peer_n(1)).wait_recv()

    def left(name, ref):
        remote(name, 0, ref, ref, "narrow", peer_n(1)).wait_send()

    def rows_at(start, size):
        return pl.ds(pl.multiple_of(start, size), size)

    sources = (g.nw_in, None, g.comb_in)
    fulls = (g.nwfull, None, g.wfull)
    part_w = D // W

    def share():
        return rows_at((core * (W // 2) + me_w // 2) * part_w, part_w)

    def share_send(k):
        def body(d):
            remote("sh%d" % k, d, sources[k].at[share()], fulls[k].at[me_n, share()], "narrow", ahead_n(d)).start()

        loop(N, body, 1)

    def share_pass(k):
        def body(d):
            part = fulls[k].at[behind_n(d), share()]
            arrived("sh%d" % k, d, part)
            loop(W // 2, lambda e: remote("sp%d" % k, d, part, part, "wide", across(2 * e)).start(), 1)

        loop(N, body, 1)

    def share_forward(k, d):
        s = behind_n(d)
        arrived("sp%d" % k, d, fulls[k].at[s, 0 : (W // 2 - 1) * part_w])
        part = fulls[k].at[s, rows_at(core * half, half)]
        remote("sf%d" % k, d if k == 0 else 0, part, part, "wide", sibling).start()

    hops = (2, 4)
    eighth = D // 8

    def hop_bit(h):
        return lax.rem(me_w // hops[h], 2)

    def quarter(h):
        return rows_at(D + h * half + (2 * core + hop_bit(h)) * eighth, eighth)

    def quarter_send(d):
        for h in range(2):
            mine = quarter(h)
            remote("sh1", 0, g.comb_in.at[mine], g.wfull.at[me_n, mine], "narrow", ahead_n(d)).start()

    def quarter_pass(d):
        s = behind_n(d)
        for h in range(2):
            part = g.wfull.at[s, quarter(h)]
            remote("sp1", 0, part, part, "wide", me_w + hops[h] - 2 * hops[h] * hop_bit(h)).start()

    def quarter_forward(d):
        s = behind_n(d)
        for h in range(2):
            part = g.wfull.at[s, rows_at(D + h * half + 2 * core * eighth, 2 * eighth)]
            remote("sf1", 0, part, part, "wide", sibling).start()

    def nb_copy(d):
        return remote("nb", 0, g.nbfull.at[me_n], g.nbfull.at[me_n], "narrow", peer_n(d))

    def z_copy(d):
        peer = peer_w(d)
        return remote("z", d, g.zsend.at[peer], g.ztab.at[me_w], "wide", peer)

    def zscale_copy(d):
        return remote("zs", 0, g.zscale, g.zscales.at[me_w], "wide", peer_w(d))

    def stat_copy(d):
        return remote("st", 0, g.stat, g.stats.at[me_n], "narrow", peer_n(d))

    def cot_copy(d):
        s = peer_n(d)
        return remote("ct", 0, g.cot_in.at[at(s, U)], g.cotrows.at[me_n], "narrow", s)

    def act_copy(d):
        s = peer_n(d)
        return remote("ac", 0, g.act.at[:, at(s, U)], g.actrows.at[me_n], "narrow", s)

    def ret_copy(p, d):
        peer, rows = peer_w(d), at(p, C // PARTS)
        return remote("gr", p, g.gsend.at[peer, rows], g.gret.at[me_w, rows], "wide", peer)

    def y_copy(p, d):
        s, rows = peer_n(d), at(p, C // PARTS)
        return remote("y", 0, g.y.at[rows, at(s, U)], g.yrows.at[me_n, rows], "narrow", s)

    def gh_copy(q, d):
        s = peer_n(d)
        return remote("gh", q, g.gh.at[rows_at(s * C + q * (C // 2), C // 2)], g.ghc.at[me_n, at(q, C // 2)], "narrow", s)

    def gf_copy(d):
        s = peer_n(d)
        return remote("gf", 0, g.gft.at[s], g.gf_out.at[me_n], "narrow", s)

    def bias_copy(name, src, dst, d):
        return remote(name, 0, src, dst.at[me_w], "wide", peer_w(d))

    def grad(k, suffix=""):
        return getattr(g, "g" + k + suffix)

    def core_rows(k, which):
        return (slice(None), at(which, grad(k).shape[1] // 2))

    def red_block(k, w):
        rows = grad(k).shape[1]
        size, down, lanes = z.red(rows)
        q = w // 2
        row = lax.rem(w, 2) * (rows // 2) + lax.rem(q, down) * size
        return (slice(None), rows_at(row, size), at(q // down, lanes))

    def out_rows(k, which):
        rows = grad(k).shape[1]
        if k == "c":
            return g.gc_sum.at[:, at(which, rows // 2)]
        return g.gn_out.at[:, rows_at(int(k[1]) * rows + which * (rows // 2), rows // 2)]

    def pair_start(k):
        remote("hs" + k, 0, grad(k).at[core_rows(k, 1 - core)], grad(k, "_half"), "wide", sibling).start()

    def reduce_pair(k):
        arrived("hs" + k, 0, grad(k, "_half"))
        own, mine = grad(k), core_rows(k, core)
        own[mine] = (own[mine].astype(F32) + grad(k, "_half")[...].astype(F32)).astype(BF16)

        def body(e):
            peer = across(2 * e)
            remote("rs" + k, 0, own.at[red_block(k, peer)], grad(k, "_in").at[me_w // 2], "wide", peer).start()

        loop(W // 2, body, 1)

    def reduce_sum(k):
        others = grad(k, "_in")
        arrived("rs" + k, 0, others.at[0 : W // 2 - 1])
        mine = red_block(k, me_w)
        total = lax.fori_loop(
            1, W // 2, lambda e, t: t + others[across(2 * e) // 2].astype(F32), grad(k)[mine].astype(F32), unroll=W <= 8
        )
        grad(k, "_sum")[mine] = total.astype(BF16)
        part = grad(k, "_sum").at[mine]
        loop(W // 2, lambda e: remote("ag" + k, 0, part, part, "wide", across(2 * e)).start(), 1)

    def gather_pass(k):
        arrived("ag" + k, 0, grad(k, "_in").at[0 : W // 2 - 1])
        part = grad(k, "_sum").at[core_rows(k, core)]
        remote("fw" + k, 0, part, out_rows(k, core), "wide", sibling).start()
        if k == "c":
            return None
        store = pltpu.make_async_copy(part, out_rows(k, core), g.store.at[SUMS.index(k)])
        store.start()
        return store

    def gather_wait(k):
        arrived("fw" + k, 0, out_rows(k, 1 - core))

    loads = [
        (g.feats_in, g.feats),
        (g.nw_in, g.nwfull.at[me_n]),
        (g.comb_in, g.wfull.at[me_n]),
        (g.slot_in, g.slot),
        (g.mask_in, g.mask),
        (g.visit_in, g.visit),
        (g.send_in, g.send),
        (g.cot_in, g.cot),
        (g.nb_in, g.nb),
        (g.cb_in, g.cb),
    ]

    def load(i):
        return pltpu.make_async_copy(loads[i][0], loads[i][1], g.load.at[i])

    barrier = pltpu.get_barrier_semaphore()
    loop(W, lambda d: pl.semaphore_signal(barrier, inc=1, device_id={"wide": peer_w(d)}, device_id_type=MESH), 1)
    loop(N, lambda d: pl.semaphore_signal(barrier, inc=1, device_id={"narrow": peer_n(d)}, device_id_type=MESH), 1)
    order = (6, 8, 3, 4, 5, 0, 1, 2, 7, 9)
    for i in order:
        load(i).start()
    pl.semaphore_wait(barrier, W - 1 + N - 1)
    share_send(0)
    load(8).wait()
    g.nbfull[me_n] = jnp.broadcast_to(g.nb[...].astype(F32).reshape(1, C), (8, C))
    loop(N, lambda d: nb_copy(d).start(), 1)

    for i in (3, 4, 5):
        load(i).wait()
    K = z.slots
    shift = CAP.bit_length() - 1

    def fill(i):
        rows = at(i, CH)
        g.code[rows, :] = jnp.zeros((CH, 128), I32)
        g.wts[rows, :] = jnp.zeros((CH, 128), F32)
        code = g.slot[:, rows].T
        g.code[rows, 0:K] = code
        g.code[rows, 64 : 64 + K] = code
        weight = (g.mask[:, rows] * g.visit[:, rows]).astype(F32).T
        g.wts[rows, 0:K] = weight
        g.wts[rows, 64 : 64 + K] = weight

    loop(R // CH, fill)

    lane = lax.broadcasted_iota(I32, (8, 128), 1)
    sub = lax.broadcasted_iota(I32, (8, 128), 0)
    half_lane = jnp.where(lane >= 64, 1, 0)
    place = [sub == 2 * j + half_lane for j in range(4)]
    place_b = [jnp.where(m, 1.0, 0.0) for m in place]
    place_b = [jnp.concatenate([m, m], axis=0).astype(BF16) for m in place_b]
    low_row = lax.broadcasted_iota(I32, (CAP, 128), 0).astype(F32).astype(BF16)

    def count_group(i):
        start = pl.multiple_of(i * 16, 16)
        outs = []
        for p in range(2):
            rows = pl.ds(pl.multiple_of(start + 8 * p, 8), 8)
            code, weight = g.code[rows, :], g.wts[rows, :]
            high, low = code >> shift, (code & (CAP - 1)).astype(F32)
            left = []
            for h in range(0, z.blocks, 2):
                pair = [jnp.where(high == h + q, weight, 0.0) for q in range(2)]
                pair = jnp.concatenate(pair, axis=0).astype(BF16)
                left.append(jnp.concatenate([pair * place_b[j] for j in range(4)], axis=1))
            left = jnp.concatenate(left, axis=0)
            right = []
            for j in range(4):
                row = jnp.sum(jnp.where(place[j], low, 0.0), axis=0, keepdims=True)
                row = jnp.broadcast_to(row.astype(BF16), (CAP, 128))
                right.append(jnp.where(low_row == row, jnp.ones((), BF16), jnp.zeros((), BF16)))
            outs.append(mm_nt(left, jnp.concatenate(right, axis=1)))
        for h in range(z.blocks):
            block = jnp.concatenate([out[h * 8 : h * 8 + 8] for out in outs], axis=0)
            top = block.astype(BF16)
            g.counts[h, pl.ds(start, 16), :] = top
            g.counts_lo[h, pl.ds(start, 16), :] = (block - top.astype(F32)).astype(BF16)

    UNROLL = 4
    groups = R // 16 // UNROLL

    def count_groups(first, last):
        def body(i):
            for q in range(UNROLL):
                count_group(i * UNROLL + q)

        loop(last, body, first)

    def hidden(s):
        def body(i):
            rows = at(i, CH)
            value = mm(g.feats[rows, :], g.nwfull[s]) + g.nbfull[s, 0:1, :]
            value = jnp.maximum(value, 0.0)
            top = value.astype(BF16)
            rest = (value - top.astype(F32)).astype(BF16)
            g.msg[rows, at(s, C)] = top
            weight = g.wfull[me_n, pl.ds(pl.multiple_of(D + s * C, C), C), :]
            g.zacc[rows, :] += mm(top, weight) + mm(rest, weight)

        sweep(R // CH, body)

    done = [0]

    def counts_until(last):
        last = groups * last // 16
        count_groups(done[0], last)
        done[0] = last

    def zero(i):
        g.zacc[at(i, CH), :] = jnp.zeros((CH, C), F32)

    loop(R // CH, zero)
    for i in (0, 1, 2):
        load(i).wait()
    hidden(me_n)
    counts_until(2)
    load(6).wait()
    g.send_t[...] = g.send[...].T

    def select(d):
        r = peer_w(d)
        which = lax.broadcasted_iota(I32, (CAP, W), 1)
        col = jnp.sum(jnp.where(which == r, g.send_t[...], 0), axis=1, keepdims=True)
        place_u = lax.broadcasted_iota(I32, (CAP, R), 1)
        g.sel[r] = jnp.where(place_u == col, 1.0, 0.0).astype(BF16)

    loop(W, select, 1)
    share_pass(0)
    loop(N, quarter_send, 1)
    counts_until(8)
    share_forward(0, 1)

    def take(d):
        arrived("sf0", d, g.nwfull.at[0, 0:half])
        hidden(behind_n(d))

    counts_until(10)
    share_forward(0, 2)
    loop(N, lambda d: cot_copy(d).start(), 1)
    arrived("nb", 0, g.nbfull.at[0 : N - 1])
    take(1)
    loop(N, functools.partial(share_forward, 0), 3)
    take(2)
    share_send(2)
    loop(N, take, 3)

    def column_max(i, most):
        return jnp.maximum(most, jnp.max(jnp.abs(g.zacc[at(i, CH), :]), axis=0, keepdims=True))

    most = lax.fori_loop(0, R // CH, column_max, jnp.full((1, C), 1e-30, F32))
    scale = most * (1.0 / 32766.0)
    g.zscale[...] = jnp.broadcast_to(scale, (8, C))
    loop(W, lambda d: zscale_copy(d).start(), 1)
    inv_scale = 1.0 / scale

    def code_z(i):
        rows = at(i, CH)
        whole = jnp.round(g.zacc[rows, :] * inv_scale)
        high = jnp.floor(whole * (1.0 / 256.0))
        g.zqa[rows, :] = high.astype(BF16)
        g.zqb[rows, :] = (whole - high * 256.0).astype(BF16)

    loop(R // CH, code_z)

    def send_z(d):
        peer = peer_w(d)
        picked = mm(g.sel[peer], g.zqa[...]) * 256.0 + mm(g.sel[peer], g.zqb[...])
        g.zsend[peer] = picked.astype(I32).astype(I16)
        z_copy(d).start()

    near = W // 4 + 1
    loop(near, send_z, 1)
    counts_until(12)
    loop(W, send_z, near)

    def split_z(i):
        rows = at(i, CH)
        value = g.zacc[rows, :]
        top = value.astype(BF16)
        g.zhi[rows, :] = top
        g.zlo[rows, :] = (value - top.astype(F32)).astype(BF16)

    loop(R // CH, split_z)
    counts_until(16)
    load(7).wait()
    load(9).wait()

    def own_part(i):
        rows = at(i, CH)
        value = mm(g.feats[rows, :], g.wfull[me_n, 0:D, :]) + g.cb[...].astype(F32).reshape(1, C)
        g.self_t[:, rows] = value.T
        g.cot_t[:, rows] = g.cot[rows, :].astype(F32).T
        total = jnp.zeros((CH, C), F32)
        for h in range(z.local):
            part = slice(h * CAP, (h + 1) * CAP)
            block = g.counts[h, rows, :]
            total += mm(block, g.zhi[part, :]) + mm(block, g.zlo[part, :]) + mm(g.counts_lo[h, rows, :], g.zhi[part, :])
        g.acc[rows, :] = total

    sweep(R // CH, own_part)
    ones = jnp.ones((16, 128), BF16)
    g.invs[...] = 2.0 / mm_nt(ones, g.wts[...].astype(BF16))

    def mine_t(i):
        cols = at(i, C)
        g.msg_t[cols, :] = g.msg[at(me_n, U), cols].astype(F32).T.astype(BF16)

    loop(D // C, mine_t)

    def take_z(d):
        s = peer_w(d)
        piece = min(32, CAP)
        for i in range(CAP // piece):
            rows = at(i, piece)
            value = g.ztab[s, rows, :].astype(I32).astype(F32) * g.zscales[s, 0:1, :]
            top = value.astype(BF16)
            g.thi[s, rows, :] = top
            g.tlo[s, rows, :] = (value - top.astype(F32)).astype(BF16)

    def pool(first, last):
        loop(last, take_z, first)

        def body(i):
            rows = at(i, CH)

            def add(d, total):
                s = peer_w(d)
                block = g.counts[z.local + s, rows, :]
                rest = g.counts_lo[z.local + s, rows, :]
                return total + mm(block, g.thi[s]) + mm(block, g.tlo[s]) + mm(rest, g.thi[s])

            g.acc[rows, :] = lax.fori_loop(first, last, add, g.acc[rows, :], unroll=W <= 8)

        return body

    arrived("zs", 0, g.zscales.at[0 : W - 1])
    for first_d, last_d in ((1, near), (W - 1, W)):
        loop(last_d, lambda d: z_copy(d).wait_recv(), first_d)
        sweep(R // CH, pool(first_d, last_d))
    loop(W - 1, lambda d: z_copy(d).wait_recv(), near)
    arrived("sh1", 0, g.wfull.at[0 : N - 1, 0 : 2 * eighth])
    loop(N, quarter_pass, 1)
    pool_rest = pool(near, W - 1)

    def activate(i):
        pool_rest(i)
        rows = at(i, CH)
        pre = g.acc[rows, :].T * g.invs[0:1, rows] + g.self_t[:, rows]
        g.self_t[:, rows] = pre
        act = jnp.maximum(pre, 0.0)
        g.act[:, rows] = act.astype(BF16)
        squares = jnp.sum(act * act, axis=0, keepdims=True)
        inner = jnp.sum(act * g.cot_t[:, rows], axis=0, keepdims=True)
        g.stat[2 * i : 2 * i + 2, :] = jnp.concatenate([squares, inner], axis=0)

    sweep(R // CH, activate)
    loop(N, lambda d: stat_copy(d).start(), 1)
    pl.semaphore_signal(g.turn, inc=1, device_id={"wide": sibling}, device_id_type=MESH)
    g.actrows[me_n] = g.act[:, at(me_n, U)]
    pl.semaphore_wait(g.turn, 1)
    loop(N, lambda d: act_copy(d).start(), 1)
    arrived("st", 0, g.stats.at[0 : N - 1])
    g.stats[me_n] = g.stat[...]

    def norms(i):
        total = g.stats[0, 2 * i : 2 * i + 2, :]
        for s in range(1, N):
            total += g.stats[s, 2 * i : 2 * i + 2, :]
        return lax.rsqrt(total[0:1] / D + EPSILON), total[1:2]

    def grad_act(i):
        rows = at(i, CH)
        inv, inner = norms(i)
        pre = g.self_t[:, rows]
        act = jnp.maximum(pre, 0.0)
        grad = g.cot_t[:, rows] * inv - act * (inner * (inv * inv * inv) / D)
        grad = jnp.where(pre > 0, grad, 0.0)
        g.gp[:, rows] = grad.astype(BF16)
        g.gps[:, rows] = (grad * g.invs[0:1, rows]).astype(BF16)

    sweep(R // CH, grad_act)

    def send_ret(d):
        peer = peer_w(d)
        g.gsend[peer] = mm(g.gps[...], g.counts[z.local + peer]).astype(BF16)
        ret_copy(0, d).start()

    loop(W, send_ret, 1)

    def more_ret(p):
        loop(W, lambda d: ret_copy(p, d).start(), 1)

    more_ret(1)
    more_ret(2)
    join = max(1, 128 // CAP)
    for h in range(0, z.local, join):
        parts = [mm(g.gps[...], g.counts[h + q]) for q in range(join)]
        parts = jnp.concatenate(parts, axis=1) if join > 1 else parts[0]
        g.yacc[:, h * CAP : (h + join) * CAP] = parts

    def embed(i):
        rows = at(i, CH)
        inv, _ = norms(i)
        value = jnp.maximum(g.self_t[:, rows], 0.0) * inv
        g.emb[rows, :] = value.T.astype(BF16)

    sweep(R // CH, embed)
    emb_store = pltpu.make_async_copy(g.emb, g.emb_out, g.store.at[4])
    emb_store.start()
    more_ret(3)

    LW = min(512, D)

    def grad_self(i):
        lanes = at(i, LW)
        g.gc[0, :, lanes] = mm(g.gp[...], g.feats[:, lanes]).astype(BF16)

    sweep(D // LW, grad_self)
    ones_r = jnp.ones((8, R), BF16)
    g.gcb[...] = mm_nt(ones_r, g.gp[...])


    def take_ret(p):
        part = at(p, C // PARTS)
        arrived("gr", p, g.gret.at[0 : W - 1, part])

        def body(i):
            lanes = at(i, CH)

            def add(d, total):
                s = peer_w(d)
                return total + mm(g.gret[s, part, :], g.sel[s, :, lanes])

            total = lax.fori_loop(1, W, add, g.yacc[part, lanes], unroll=W <= 8)
            g.y[part, lanes] = total.astype(BF16)

        sweep(R // CH, body)
        loop(N, lambda d: y_copy(p, d).start(), 1)

    take_ret(0)
    arrived("sp1", 0, g.wfull.at[0 : N - 1, 0 : 2 * eighth])
    loop(N, quarter_forward, 1)
    share_pass(2)
    for p in range(1, PARTS):
        take_ret(p)
    g.yrows[me_n] = g.y[:, at(me_n, U)]

    def grad_pool(i):
        lanes = at(i, LW)
        g.gc[1, :, lanes] = mm(g.y[...], g.msg[:, lanes]).astype(BF16)

    sweep(D // LW, grad_pool)
    loop(W, lambda d: bias_copy("bc", g.gcb, g.gcb_in, d).start(), 1)
    pair_start("c")

    reduce_pair("c")
    arrived("ct", 0, g.cotrows.at[0 : N - 1])
    g.cotrows[me_n] = g.cot[at(me_n, U), :]
    for s in range(N):
        g.cotrows_t[s] = g.cotrows[s].astype(F32).T
    arrived("sf1", 0, g.wfull.at[0 : N - 1, 0:half])
    arrived("y", 0, g.yrows.at[0 : N - 1])

    def hidden_rows(i):
        rows = at(i, CH)
        wrows = slice(D + i * CH, D + (i + 1) * CH)
        total = jnp.zeros((CH, U), F32)
        for s in range(N):
            total += mm(g.wfull[s, wrows, :], g.yrows[s])
        g.gh[rows, :] = jnp.where(g.msg_t[rows, :] > 0, total, 0.0).astype(BF16)

    sweep(D // CH, hidden_rows)
    loop(N, lambda d: gh_copy(0, d).start(), 1)
    g.ghc[me_n] = g.gh[at(me_n, C), :]

    def feature_rows(i):
        rows = at(i, C)
        total = jnp.zeros((C, U), F32)
        for s in range(N):
            total += mm(g.wfull[s, rows, :], g.gprows[s]) + mm(g.nwfull[s, rows, :], g.gh[s * C : (s + 1) * C, :])
        g.gft[i] = total.T.astype(BF16)

    loop(N, functools.partial(share_forward, 2), 1)
    arrived("ac", 0, g.actrows.at[0 : N - 1])
    per = CH // U
    lanes = at(lax.rem(me_n, per), U) if per > 1 else slice(None)
    total = g.stats[0, :, lanes]
    for s in range(1, N):
        total += g.stats[s, :, lanes]
    row = lax.broadcasted_iota(I32, total.shape, 0) - 2 * (me_n // per)
    inv = lax.rsqrt(jnp.sum(jnp.where(row == 0, total, 0.0), axis=0, keepdims=True) / D + EPSILON)
    inner = jnp.sum(jnp.where(row == 1, total, 0.0), axis=0, keepdims=True)
    factor = inner * (inv * inv * inv) / D
    for s in range(N):
        act = g.actrows[s].astype(F32)
        grad_rows = jnp.where(act > 0, g.cotrows_t[s] * inv - act * factor, 0.0)
        g.gprows[s] = grad_rows.astype(BF16)
    arrived("sf2", 0, g.wfull.at[0 : N - 1, 0:half])
    loop(N, lambda d: gh_copy(1, d).start(), 1)
    sweep(N, feature_rows)
    gf_store = pltpu.make_async_copy(g.gft.at[me_n], g.gf_out.at[me_n], g.store.at[3])
    gf_store.start()

    reduce_sum("c")

    def grad_neigh(q):
        rows = at(q, C // 2)
        out = (g.gn0, g.gn1)[q]

        def body(i):
            lanes = at(i, LW)
            total = jnp.zeros((C // 2, LW), F32)
            for s in range(N):
                total += mm(g.ghc[s, rows, :], g.feats[s * U : (s + 1) * U, lanes])
            out[0, :, lanes] = total.astype(BF16)

        sweep(D // LW, body)

    arrived("gh", 0, g.ghc.at[0 : N - 1, 0 : C // 2])
    grad_neigh(0)
    pair_start("n0")
    arrived("gh", 1, g.ghc.at[0 : N - 1, 0 : C // 2])
    loop(N, lambda d: gf_copy(d).start(), 1)
    reduce_pair("n0")
    grad_neigh(1)
    pair_start("n1")
    total = jnp.zeros((8, C), F32)
    ones_u = jnp.ones((8, U), BF16)
    for s in range(N):
        total += mm_nt(ones_u, g.ghc[s])
    g.gnb[...] = total
    loop(W, lambda d: bias_copy("bn", g.gnb, g.gnb_in, d).start(), 1)
    reduce_pair("n1")
    reduce_sum("n0")
    def bias_sum(name, own, others):
        arrived(name, 0, others.at[0 : W - 1])
        left(name, others.at[0 : W - 1])
        own[...] = lax.fori_loop(1, W, lambda d, total: total + others[peer_w(d)], own[...])

    bias_sum("bc", g.gcb, g.gcb_in)
    bias_sum("bn", g.gnb, g.gnb_in)
    gcb_store = pltpu.make_async_copy(g.gcb, g.gcb_out, g.store.at[5])
    gnb_store = pltpu.make_async_copy(g.gnb, g.gnb_out, g.store.at[6])
    gcb_store.start()
    gnb_store.start()
    gather_pass("c")
    reduce_sum("n1")
    gn0_store = gather_pass("n0")
    gn1_store = gather_pass("n1")
    gather_wait("c")
    for p in range(2):
        for i in range(D // CH):
            g.gct[p, at(i, CH), :] = g.gc_sum[p, :, at(i, CH)].astype(F32).T.astype(BF16)
    gc_store = pltpu.make_async_copy(g.gct, g.gc_out, g.store.at[0])
    gc_store.start()
    for k in SUMS[1:]:
        gather_wait(k)
    arrived("gf", 0, g.gf_out.at[0 : N - 1])

    for k in (0, 2):
        left("sh%d" % k, fulls[k].at[0 : N - 1, 0:part_w])
        left("sp%d" % k, fulls[k].at[0 : N - 1, 0 : (W // 2 - 1) * part_w])
        left("sf%d" % k, fulls[k].at[0 : N - 1, 0:half])
    left("sh1", g.wfull.at[0 : N - 1, 0 : 2 * eighth])
    left("sp1", g.wfull.at[0 : N - 1, 0 : 2 * eighth])
    left("sf1", g.wfull.at[0 : N - 1, 0:half])
    left("nb", g.nbfull.at[0 : N - 1])
    left("z", g.zsend.at[0 : W - 1])
    left("zs", g.zscales.at[0 : W - 1])
    left("st", g.stats.at[0 : N - 1])
    left("ct", g.cotrows.at[0 : N - 1])
    left("ac", g.actrows.at[0 : N - 1])
    left("gr", g.gsend.at[0 : W - 1])
    left("y", g.yrows.at[0 : N - 1])
    left("gh", g.ghc.at[0 : N - 1])
    left("gf", g.gf_out.at[0 : N - 1])
    for k in SUMS:
        left("hs" + k, grad(k, "_half"))
        left("rs" + k, grad(k, "_in").at[0 : W // 2 - 1])
        left("ag" + k, grad(k, "_in").at[0 : W // 2 - 1])
        left("fw" + k, grad(k, "_sum").at[core_rows(k, core)])
    for store in (emb_store, gf_store, gc_store, gcb_store, gnb_store, gn0_store, gn1_store):
        store.wait()


def finish(z, emb, gf, gn, gc, gnb, gcb, *refs):
    emb_out, gf_out, gn_out, gc_out, gnb_out, gcb_out, gf_t, gn_t, gc_t, gnb_t, gcb_t, store = refs
    D, N, U = z.width, z.narrow, z.part
    step = D // N
    stores = []

    def keep(src, dst):
        stores.append(pltpu.make_async_copy(src, dst, store.at[len(stores)]))
        stores[-1].start()

    keep(emb, emb_out)
    for i in range(N):
        rows = at(i, step)
        for p in range(2):
            gc_t[p, rows, :] = gc[p, rows, :].astype(F32)
            keep(gc_t.at[p, rows], gc_out.at[p, rows])
        gn_t[rows, :] = gn[0, :, rows].astype(F32).T
        keep(gn_t.at[rows], gn_out.at[rows])
        gf_t[at(i, U), :] = gf[i].astype(F32)
        keep(gf_t.at[at(i, U)], gf_out.at[at(i, U)])
    gnb_t[...] = gnb[0:1, :]
    gcb_t[...] = gcb[0:1, :]
    keep(gnb_t, gnb_out)
    keep(gcb_t, gcb_out)
    for copy in stores:
        copy.wait()


def shards(wide, narrow, node_feats, neigh_weight, neigh_bias, combine_weight, combine_bias, cotangent,
           neighbour_slot, neighbour_mask, visit_count, send_rows):
    z = Sizes(node_feats, neigh_weight, send_rows, neighbour_slot.T, wide, narrow)
    R, D, C, W, N, U = z.rows, z.width, z.cols, z.wide, z.narrow, z.part
    bufs, sems, kinds = scratch(z)
    names = NAMES_IN + NAMES_OUT + list(bufs) + list(sems)
    outs = (
        pltpu.VMEM((R, C), BF16),
        pltpu.VMEM((N, U, C), BF16),
        pltpu.VMEM((1, C, D), BF16),
        pltpu.VMEM((2, D, C), BF16),
        pltpu.VMEM((8, C), F32),
        pltpu.VMEM((8, C), F32),
    )
    emb, gf, gn, gc, gnb, gcb = pl.pallas_call(
        functools.partial(kernel, z, names, kinds),
        out_shape=outs,
        in_specs=[pl.BlockSpec(memory_space=pl.ANY)] * len(NAMES_IN),
        out_specs=[pl.BlockSpec(memory_space=pl.ANY)] * len(NAMES_OUT),
        scratch_shapes=list(bufs.values()) + list(sems.values()),
        compiler_params=pltpu.CompilerParams(
            collective_id=0, has_side_effects=True, vmem_limit_bytes=58 * 2**20
        ),
        cost_estimate=pl.CostEstimate(flops=2 * 10**10, bytes_accessed=2 * 10**7, transcendentals=0),
        name="layer",
    )(
        node_feats, neigh_weight, neigh_bias, combine_weight, combine_bias, cotangent,
        neighbour_slot.T, neighbour_mask.T, visit_count.T, send_rows,
    )
    hbm = pl.BlockSpec(memory_space=pl.ANY)
    emb, grad_features, grad_neigh, grad_combine, gnb, gcb = pl.pallas_call(
        functools.partial(finish, z),
        out_shape=(
            jax.ShapeDtypeStruct((R, C), BF16),
            jax.ShapeDtypeStruct((R, C), F32),
            jax.ShapeDtypeStruct((D, C), F32),
            jax.ShapeDtypeStruct((2, D, C), F32),
            jax.ShapeDtypeStruct((1, C), F32),
            jax.ShapeDtypeStruct((1, C), F32),
        ),
        in_specs=[pl.BlockSpec(memory_space=pltpu.VMEM)] * 6,
        out_specs=[hbm] * 6,
        scratch_shapes=[
            pltpu.VMEM((R, C), F32),
            pltpu.VMEM((D, C), F32),
            pltpu.VMEM((2, D, C), F32),
            pltpu.VMEM((1, C), F32),
            pltpu.VMEM((1, C), F32),
            pltpu.SemaphoreType.DMA((4 * N + 3,)),
        ],
        compiler_params=pltpu.CompilerParams(vmem_limit_bytes=32 * 2**20),
        name="finish",
    )(emb, gf, gn, gc, gnb, gcb)
    return emb, grad_features, grad_neigh, gnb.reshape(C), grad_combine.reshape(2 * D, C), gcb.reshape(C)


def solution(mesh):
    placed = (
        P("wide", None),
        P(None, "narrow"),
        P("narrow"),
        P(None, "narrow"),
        P("narrow"),
        P("wide", "narrow"),
        P("wide", None),
        P("wide", None),
        P("wide", None),
        P("wide", None),
    )
    return jax.shard_map(
        functools.partial(shards, mesh.shape["wide"], mesh.shape["narrow"]),
        mesh=mesh,
        in_specs=placed,
        out_specs=(
            P("wide", "narrow"),
            P("wide", "narrow"),
            P(None, "narrow"),
            P("narrow"),
            P(None, "narrow"),
            P("narrow"),
        ),
        check_vma=False,
    )
```
